32 devices in a mesh: seq: 8 (over z, y), batch: 4 (over x, core).
Axes of the slice: x: 2, y: 2, z: 4, core: 2. Of those that a mesh axis runs over, the one named last changes fastest.
Arguments:
- token_ids: int32 [32768], P(('batch', 'seq')), parts along dimension 0, may hold values from 0 to 4
- embed_table: bfloat16 [5, 256], replicated, may hold values from -6 to 6
- input_weight_matrix: bfloat16 [256, 1064], replicated, may hold values from -0.375 to 0.375
- output_weight_matrix: bfloat16 [512, 256], replicated, may hold values from -0.25 to 0.25
- conv_weight: float32 [2, 4, 512], replicated, may hold values from -3 to 3
- dt_bias: float32 [2, 8], replicated, may hold values from -1 to 1
- decay_rate: float32 [2, 8], replicated, may hold values from 0 to 0.05
- skip_gain: float32 [2, 8], replicated, may hold values from -4 to 4
- norm_gain: float32 [2, 512], replicated, may hold values from 0.1 to 1.9
Outputs:
- hidden: bfloat16 [32768, 256], P(('batch', 'seq')), parts along dimension 0
The draws below stay inside these ranges and needn't reach their ends.
There are 4 independent parts, one for each index of `batch`. The reference program is written for one: setup_inputs(seed, part) draws one part's arguments, and reference() takes and returns one part's arrays. A program takes and returns all parts, laid end to end along the dimension named above; an argument that names none is the same for every part. Nothing has to cross between parts.
All inputs are finite; a program needn't handle non-finite values.
Results may differ from the reference program's by a relative error of at most 0.0029.
The reference program's roundings to bfloat16 on the way count: a program that leaves them out, or rounds other values in their place, can miss the bound.
Values may be sent and summed in bfloat16 or wider, within the bound.
No kernel may reach another device: no remote copies, remote signals or barrier semaphores. Data moves between devices by JAX's collectives and lax.ppermute only.
A program may use at most 128 MiB of HBM per device.

```python
import math
import jax
import jax.numpy as jnp
from jax import lax

D = 256
E = 512
NS = 16
P_SIZE = 64
KW = 4
BLK = 128
L_DEV = 1024
H = 8
LENGTH = 8192


def draw_token_ids(key, part):
    span = max(L_DEV, LENGTH // 8)
    count = LENGTH // span + 2
    key_offset, key_major, key_other, key_pick = jax.random.split(key, 4)
    offset = jax.random.randint(key_offset, (), 0, span)
    stretch = (jnp.arange(LENGTH, dtype=jnp.int32) + offset) // span
    dominant = jax.random.randint(key_major, (count,), 0, 5)
    others = jax.random.randint(key_other, (LENGTH,), 0, 5)
    picked = jax.random.randint(key_pick, (LENGTH,), 0, 4) < 3
    return jnp.where(picked, dominant[stretch], others).astype(jnp.int32)


def draw_decay_rate(key, part):
    key_slow, key_fast, key_keep, key_share = jax.random.split(key, 4)
    slow_rates = jnp.exp(jax.random.uniform(key_slow, (2, H), jnp.float32, math.log(0.3), math.log(2.5))) * (1.0 / LENGTH)
    fast_rates = jnp.exp(jax.random.uniform(key_fast, (2, H), jnp.float32, math.log(0.02), math.log(0.05)))
    keeper = jax.random.randint(key_keep, (2,), 0, H)
    forced = jnp.arange(H)[None, :] == keeper[:, None]
    slow_heads = forced | (jax.random.uniform(key_share, (2, H), jnp.float32) < 0.6)
    return jnp.where(slow_heads, slow_rates, fast_rates).astype(jnp.float32)


def noise(stream_key, dims, deviation, reach, held_as=jnp.bfloat16):
    entries = deviation * jax.random.normal(stream_key, dims, jnp.float32)
    return jnp.clip(entries, min=-reach, max=reach).astype(held_as)


def setup_inputs(seed: int = 0, part: int = 0) -> dict:
    key_of = jax.random.split(jax.random.key(seed), 10)
    part_splits = jax.random.split(jax.random.fold_in(key_of[9], part), 10)
    return {
        "token_ids": draw_token_ids(jax.random.fold_in(jax.random.fold_in(key_of[9], part), 71), part),
        "embed_table": noise(key_of[1], (5, D), 1.0, 6.0),
        "input_weight_matrix": noise(key_of[2], (D, 2 * E + 2 * NS + H), D ** -0.5, 0.375),
        "output_weight_matrix": noise(key_of[3], (E, D), E ** -0.5, 0.25),
        "conv_weight": noise(key_of[4], (2, KW, E), KW ** -0.5, 3.0, jnp.float32),
        "dt_bias": jnp.clip(jax.random.uniform(key_of[5], (2, H), jnp.float32, -1.0, 1.0), -1.0, 1.0),
        "decay_rate": draw_decay_rate(jax.random.fold_in(key_of[9], 71), part),
        "skip_gain": noise(key_of[7], (2, H), 1.0, 4.0, jnp.float32),
        "norm_gain": jnp.clip(1.0 + 0.18 * jax.random.normal(key_of[8], (2, E), jnp.float32), 0.1, 1.9),
    }


EPSILON = 1e-05

def complement(ids):
    return jnp.where(ids < 4, 3 - ids, ids).astype(jnp.int32)

def embed_rows(ids, embed_table):
    onehot = (ids[:, None] == jnp.arange(5, dtype=jnp.int32)[None, :]).astype(jnp.bfloat16)
    return jnp.dot(onehot, embed_table, preferred_element_type=jnp.float32).astype(jnp.bfloat16)

def block_step(state, pieces):
    highest = lax.Precision.HIGHEST
    inner_x, log_decay, step, b_part, c_part = pieces
    count = log_decay.shape[0]
    cumul = jnp.cumsum(log_decay, axis=0)
    index = jnp.arange(count)
    lower = index[:, None] >= index[None, :]
    spread = cumul[:, None, :] - cumul[None, :, :]
    decay = jnp.exp(jnp.where(lower[:, :, None], spread, -1e+30))
    scores = jnp.dot(c_part, b_part.T, precision=highest)
    weighted = inner_x * step[:, :, None]
    inner = jnp.einsum('trh,rhp->thp', scores[:, :, None] * decay, weighted, precision=highest)
    carried = jnp.exp(cumul)[:, :, None] * jnp.einsum('tn,hpn->thp', c_part, state, precision=highest)
    tail = jnp.exp(cumul[-1][None, :] - cumul)
    new_state = jnp.exp(cumul[-1])[:, None, None] * state + jnp.einsum('rh,rhp,rn->hpn', tail, weighted, b_part, precision=highest)
    return (new_state, inner + carried)

def run_chain(inner_x, log_decay, step, b_part, c_part):
    length = log_decay.shape[0]
    blocks = length // BLK
    init = jnp.zeros((H, P_SIZE, NS), jnp.float32)
    pieces = (inner_x.reshape(blocks, BLK, H, P_SIZE), log_decay.reshape(blocks, BLK, H), step.reshape(blocks, BLK, H), b_part.reshape(blocks, BLK, NS), c_part.reshape(blocks, BLK, NS))
    _, outputs = lax.scan(block_step, init, pieces)
    return outputs.reshape(length, H, P_SIZE)

def direction(projected, k, backward, conv_weight, dt_bias, decay_rate, skip_gain, norm_gain):
    gate = projected[:, :E].astype(jnp.float32)
    values = projected[:, E:2 * E].astype(jnp.float32)
    b_part = projected[:, 2 * E:2 * E + NS].astype(jnp.float32)
    c_part = projected[:, 2 * E + NS:2 * E + 2 * NS].astype(jnp.float32)
    raw = projected[:, 2 * E + 2 * NS:].astype(jnp.float32)
    if backward:
        values, b_part, c_part, raw = (values[::-1], b_part[::-1], c_part[::-1], raw[::-1])
    length = values.shape[0]
    padded_input = jnp.concatenate([jnp.zeros((KW - 1, E), jnp.float32), values], axis=0)
    acc = conv_weight[k, 0][None, :] * padded_input[0:length]
    for j in range(1, KW):
        acc = acc + conv_weight[k, j][None, :] * padded_input[j:j + length]
    inner_x = jax.nn.silu(acc).reshape(length, H, P_SIZE)
    step = jax.nn.softplus(raw + dt_bias[k][None, :])
    log_decay = -decay_rate[k][None, :] * step
    outputs = run_chain(inner_x, log_decay, step, b_part, c_part) + skip_gain[k][None, :, None] * inner_x
    if backward:
        outputs = outputs[::-1]
    gated = outputs * jax.nn.silu(gate).reshape(length, H, P_SIZE)
    meansq = lax.optimization_barrier(jnp.mean(gated * gated, axis=-1, keepdims=True))
    normed = gated * lax.rsqrt(meansq + EPSILON) * norm_gain[k].reshape(1, H, P_SIZE)
    return normed.reshape(length, E)

def strand(feature_vectors, input_weight_matrix, output_weight_matrix, conv_weight, dt_bias, decay_rate, skip_gain, norm_gain):
    projected = jnp.dot(feature_vectors, input_weight_matrix, preferred_element_type=jnp.float32).astype(jnp.bfloat16)
    first = direction(projected, 0, False, conv_weight, dt_bias, decay_rate, skip_gain, norm_gain)
    second = direction(projected, 1, True, conv_weight, dt_bias, decay_rate, skip_gain, norm_gain)
    mixer_output = (first + second).astype(jnp.bfloat16)
    return jnp.dot(mixer_output, output_weight_matrix, preferred_element_type=jnp.float32).astype(jnp.bfloat16)

def reference(token_ids, embed_table, input_weight_matrix, output_weight_matrix, conv_weight, dt_bias, decay_rate, skip_gain, norm_gain):
    feature_vectors = embed_rows(token_ids, embed_table)
    rc_features = embed_rows(complement(token_ids[::-1]), embed_table)
    own_out = strand(feature_vectors, input_weight_matrix, output_weight_matrix, conv_weight, dt_bias, decay_rate, skip_gain, norm_gain)
    rc_out = strand(rc_features, input_weight_matrix, output_weight_matrix, conv_weight, dt_bias, decay_rate, skip_gain, norm_gain)
    hidden = feature_vectors.astype(jnp.float32) + own_out.astype(jnp.float32) + rc_out[::-1, ::-1].astype(jnp.float32)
    return hidden.astype(jnp.bfloat16)
```

```python
import jax
import jax.numpy as jnp
from jax import lax
from jax.experimental import pallas as pl
from jax.experimental.pallas import tpu as pltpu
from jax.sharding import PartitionSpec as P

D = 256
E = 512
NS = 16
H = 8
KW = 4
SYM = 5
LOG2E = 1.4426950408889634
EPSILON = 1e-05
CH = 128

F32 = jnp.float32
BF16 = jnp.bfloat16

CHAINS = ((0, 0, 0), (0, 1, 1), (1, 0, 1), (1, 1, 0))


def iota(shape, dim):
    return lax.broadcasted_iota(jnp.int32, shape, dim)


def nn(a, b, **kw):
    return lax.dot_general(a, b, (((1,), (0,)), ((), ())), preferred_element_type=F32, **kw)


def nt(a, b, **kw):
    return lax.dot_general(a, b, (((1,), (1,)), ((), ())), preferred_element_type=F32, **kw)


def split(value):
    high = value.astype(BF16)
    low = (value - high.astype(F32)).astype(BF16)
    return high, low


def softplus(x):
    return jnp.maximum(x, 0.0) + jnp.log1p(jnp.exp(-jnp.abs(x)))


def silu_half(half):
    return half + half * jnp.tanh(half)


def tap_row(direction, j):
    return j if direction == 0 else 2 * (KW - 1) - j


def window_onehot(rows):
    sub = iota((8, CH), 0).astype(F32)
    blocks = [jnp.where(row == sub, 1.0, 0.0) for row in rows]
    blocks.append(jnp.zeros((8, CH), F32))
    stacked = jnp.concatenate(blocks + blocks, axis=0)
    return stacked.T.astype(BF16)


def shifted(tok, offset, rows):
    if offset == 0:
        return tok
    lane = iota((rows, CH), 1)
    row = iota((rows, CH), 0)
    moved = pltpu.roll(tok, (-offset) % CH, 1)
    if offset < 0:
        other = pltpu.roll(moved, 1, 0)
        crossing = lane < -offset
        outside = crossing & (row == 0)
    else:
        other = pltpu.roll(moved, rows - 1, 0)
        crossing = lane >= CH - offset
        outside = crossing & (row == rows - 1)
    return jnp.where(outside, 5.0, jnp.where(crossing, other, moved))


def pick(values, u):
    out = values[0]
    for k in range(1, SYM):
        out = jnp.where(u == k, values[k], out)
    return out


def tile_at(ref, row):
    return ref[pl.ds(pl.multiple_of(row, 8), 8), :]


def local_kernel(
    tok_s, tok_v, emb, w_in, w_out, cw, bias, rate, skip, gain,
    yad, ybc, feat, atab, gtab, zg, cst, lac, tw, xch, xcl, pst, wflip,
    emb16,
):
    nchunk = tok_v.shape[0]
    highest = lax.Precision.HIGHEST
    emb16[...] = jnp.zeros_like(emb16)
    e32 = emb[...].astype(F32)
    emb16[0:SYM, :] = e32
    for v in range(4):
        emb16[8 + v : 9 + v, :] = e32[3 - v : 4 - v, :]
    emb16[12:13, :] = e32[4:5, :]
    embs = emb16[...].astype(BF16)
    z16 = nn(embs, w_in[:, 0:E]).astype(BF16).astype(F32)
    x16 = nn(embs, w_in[:, E : 2 * E]).astype(BF16).astype(F32)
    rest = nn(embs, w_in[:, 2 * E :]).astype(BF16)
    nrest = 2 * NS + H
    expand = jnp.where(
        iota((nrest, E), 0) == (iota((nrest, E), 1) >> 6) + 2 * NS, 1.0, 0.0
    ).astype(BF16)
    heads = jnp.where(iota((H, E), 0) == (iota((H, E), 1) >> 6), 1.0, 0.0)
    r_exp = nn(rest, expand)
    bias_e = nn(bias[...], heads, precision=highest)
    rate_e = nn(rate[...], heads, precision=highest)
    skip_e = nn(skip[...], heads, precision=highest)
    shift = jnp.where(
        iota((nrest, nrest), 0) + NS == iota((nrest, nrest), 1),
        jnp.where(iota((nrest, nrest), 0) < NS, 1.0, 0.0),
        0.0,
    ).astype(BF16)
    rest_b = nn(rest, shift).astype(BF16)
    cb = nt(rest_b, rest)
    sz = z16 * (0.5 + 0.5 * jnp.tanh(0.5 * z16))
    for s in range(2):
        for i in range(4):
            zg[pl.ds(s * 4 + i, 8, stride=8), :] = sz[8 * s : 8 * s + 8, 128 * i : 128 * i + 128]
    pick_r = jnp.where(
        iota((H, nrest), 0) + 2 * NS == iota((H, nrest), 1), 1.0, 0.0
    ).astype(BF16)
    r_t = nt(pick_r, rest)
    eye = jnp.where(iota((H, H), 0) == iota((H, H), 1), 1.0, 0.0)
    bias_t = nt(eye, bias[...], precision=highest)
    rate_t = nt(eye, rate[...], precision=highest)
    for q, (d, s, k) in enumerate(CHAINS):
        dt = softplus(r_exp[8 * s : 8 * s + 8, :] + bias_e[k : k + 1, :])
        a = jnp.exp(-rate_e[k : k + 1, :] * dt)
        for i in range(4):
            lanes = slice(128 * i, 128 * i + 128)
            atab[pl.ds(d * 64 + s * 4 + i, 8, stride=8), :] = a[:, lanes]
            cst[d * 8 + s * 4 + i : d * 8 + s * 4 + i + 1, :] = skip_e[k : k + 1, lanes]
            cst[16 + d * 8 + s * 4 + i : 17 + d * 8 + s * 4 + i, :] = gain[k : k + 1, lanes]
        for u in range(SYM):
            g = cb[8 * s : 8 * s + 8, 8 * s + u : 8 * s + u + 1] * dt
            for i in range(4):
                gtab[pl.ds((d * SYM + u) * 64 + s * 4 + i, 8, stride=8), :] = g[
                    :, 128 * i : 128 * i + 128
                ]
        la = (
            -rate_t[:, k : k + 1] * softplus(r_t[:, 8 * s : 8 * s + 8] + bias_t[:, k : k + 1])
        ) * LOG2E
        for v in range(SYM):
            lac[(d * SYM + v) * 16 + s * 8 : (d * SYM + v) * 16 + s * 8 + 8, :] = jnp.broadcast_to(
                la[:, v : v + 1], (8, CH)
            )
        xs = x16[8 * s : 8 * s + 8, :]
        blocks = [jnp.zeros((8, E), F32)] * 8
        for j in range(KW):
            blocks[tap_row(d, j)] = (0.5 * cw[k, j : j + 1, :]) * xs
        high, low = split(jnp.concatenate(blocks, axis=0))
        tw[q, 0:64, :] = high
        tw[q, 64:128, :] = low
        code = iota((CH, CH), 0).astype(F32)
        lane = iota((CH, CH), 1) & 63
        slot = lane >> 3
        sym = (lane & 7).astype(F32)
        d0 = jnp.floor((code + 0.5) * (1.0 / 25.0))
        d01 = jnp.floor((code + 0.5) * (1.0 / 5.0))
        digits = (d0, d01 - 5.0 * d0, code - 5.0 * d01)
        hot = jnp.zeros((CH, CH), F32)
        for j in range(KW - 1):
            hot = jnp.where(
                slot == tap_row(d, j), jnp.where(sym == digits[j], 1.0, 0.0), hot
            )
        partial = nn(hot.astype(BF16), tw[q])
        last = blocks[tap_row(d, KW - 1)]
        for v in range(SYM):
            high, low = split(silu_half(partial + last[v : v + 1, :]))
            xch[(q * SYM + v) * CH : (q * SYM + v + 1) * CH, :] = high
            xcl[(q * SYM + v) * CH : (q * SYM + v + 1) * CH, :] = low
    flip = jnp.where(iota((D, D), 0) + iota((D, D), 1) == D - 1, 1.0, 0.0).astype(BF16)
    wflip[...] = nn(w_out[...], flip).astype(BF16)

    tok = tok_v[...].astype(F32)
    shifts = [shifted(tok, o, nchunk) for o in range(-3, 4)]
    emb_rows = jnp.concatenate(
        [jnp.zeros((24, D), F32), emb16[0:8, :], jnp.zeros((96, D), F32)], axis=0
    ).astype(BF16)
    for c in range(nchunk):
        hot = window_onehot([sh[c : c + 1, :] for sh in shifts])
        feat[c * CH : (c + 1) * CH, :] = nn(hot, emb_rows).astype(BF16)
        for q, (d, s, k) in enumerate(CHAINS):
            x = silu_half(nn(hot, tw[q]))
            ref = (yad, ybc)[d]
            for i in range(4):
                ref[pl.ds(c * 8 * CH + s * 4 + i, CH, stride=8), :] = x[:, 128 * i : 128 * i + 128]
    total = nchunk * CH
    yad[0:24, :] = jnp.zeros((24, CH), F32)
    ybc[total * 8 - 24 : total * 8, :] = jnp.zeros((24, CH), F32)

    skip0 = cst[0:8, :]
    skip1 = cst[8:16, :]

    def advance(direction, ref, skip_t, t, state):
        u = tok_s[t]
        x = tile_at(ref, t * 8)
        a = tile_at(atab, direction * 64 + u * 8)
        new = [
            a * state[w] + tile_at(gtab, (direction * SYM + w) * 64 + u * 8) * x
            for w in range(SYM)
        ]
        ref[pl.ds(pl.multiple_of(t * 8, 8), 8), :] = pick(new, u) + skip_t * x
        return new, a

    unroll = 8

    def group(g, carry):
        ya, yb, pa, pb = carry
        ya, yb = list(ya), list(yb)
        for i in range(unroll):
            n = g * unroll + i
            ya, a0 = advance(0, yad, skip0, n, ya)
            yb, a1 = advance(1, ybc, skip1, total - 1 - n, yb)
            if i < 3:
                a0 = jnp.where(g == 0, 1.0, a0)
                a1 = jnp.where(g == 0, 1.0, a1)
            pa = pa * a0
            pb = pb * a1
        return tuple(ya), tuple(yb), pa, pb

    def chunk(c, carry):
        pst[pl.ds(pl.multiple_of(c * 8, 8), 8), :] = carry[2]
        pst[pl.ds(pl.multiple_of((2 * nchunk - 1 - c) * 8, 8), 8), :] = carry[3]
        per = CH // unroll
        return lax.fori_loop(c * per, (c + 1) * per, group, carry)

    zero = jnp.zeros((8, CH), F32)
    one = jnp.ones((8, CH), F32)
    lax.fori_loop(0, nchunk, chunk, ((zero,) * SYM, (zero,) * SYM, one, one))


def finish_kernel(
    mine, tok_s, tok_all, yad, ybc, feat, atab, gtab, zg, cst, lac, tw, xch, xcl, pst, w_out, wflip,
    out,
    tok_f, code, tri, hist, svec, xrim, ycar, yrim, gad, gbc, mix,
):
    step = pl.program_id(0)
    nchunk = pl.num_programs(0)
    rows = tok_all.shape[0]
    own = rows // 8
    j = mine[0]

    @pl.when(step == 0)
    def _():
        tok = tok_all[...].astype(F32)
        tok_f[3] = tok
        for o in (-3, -2, -1, 1, 2, 3):
            tok_f[3 + o] = shifted(tok, o, rows)
        lane = iota((rows, CH), 1)
        row = iota((rows, CH), 0)
        lane_f = lane.astype(F32)
        before = 25.0 * tok_f[0] + 5.0 * tok_f[1] + tok_f[2]
        after = 25.0 * tok_f[6] + 5.0 * tok_f[5] + tok_f[4]
        code[0] = jnp.where((row == 0) & (lane < 3), 125.0 + lane_f, before)
        code[1] = jnp.where((row == rows - 1) & (lane >= CH - 3), lane_f, after)
        si = iota((CH, CH), 0)
        ri = iota((CH, CH), 1)
        ones = jnp.ones((CH, CH), F32)
        tri[0] = jnp.concatenate([jnp.where(si > ri, 1.0, 0.0), ones], axis=1).astype(BF16)
        tri[1] = jnp.concatenate([jnp.where(si < ri, 1.0, 0.0), ones], axis=1).astype(BF16)
        hist[...] = jnp.zeros_like(hist)
        sub8 = iota((8, CH), 0).astype(F32)
        subc = iota((CH, CH), 0).astype(F32)

        def block(b, off):
            side = jnp.where(b >= j, 1, 0)
            index = jnp.where(b >= j, b + 1, j - 1 - b)
            off = off * jnp.where(b == j, 0.0, 1.0)
            use_prefix = side.astype(F32)
            at = pl.ds(pl.multiple_of(index * 8, 8), 8)
            tk = tok_f[3, at, :]
            cd = code[side, at, :]
            hots = [jnp.where(tk[m : m + 1, :] == sub8, 1.0, 0.0) for m in range(8)]
            counts = nn(jnp.concatenate(hots, axis=0).astype(BF16), tri[side])
            totals = [counts[8 * m : 8 * m + 8, CH:] for m in range(8)]
            prefix = [jnp.zeros((8, CH), F32)]
            for m in range(8):
                prefix.append(prefix[-1] + totals[m])
            las = [lac[pl.ds(pl.multiple_of((side * SYM + v) * 16, 16), 16), :] for v in range(SYM)]
            acc = jnp.zeros((160, CH), F32)
            for pair in range(4):
                lefts, rights = [], []
                for m in (2 * pair, 2 * pair + 1):
                    suffix = prefix[8] - prefix[m + 1]
                    inside = suffix + use_prefix * (prefix[m] - suffix)
                    count = counts[8 * m : 8 * m + 8, :CH] + off + inside
                    exponent = las[0] * count[0:1, :]
                    for v in range(1, SYM):
                        exponent = exponent + las[v] * count[v : v + 1, :]
                    weight = jnp.exp2(exponent)
                    masked = jnp.concatenate(
                        [jnp.where(tk[m : m + 1, :] == float(v), weight, 0.0) for v in range(SYM)],
                        axis=0,
                    )
                    high, low = split(masked)
                    lefts.append(jnp.concatenate([high, low], axis=0))
                    rights.append(jnp.where(cd[m : m + 1, :] == subc, 1.0, 0.0).astype(BF16))
                acc = acc + nt(
                    jnp.concatenate(lefts, axis=1), jnp.concatenate(rights, axis=1)
                )
            hist[side] = hist[side] + acc
            return off + prefix[8]

        lax.fori_loop(0, own - 1, block, jnp.zeros((8, CH), F32))

        last8 = rows - 8
        mine8 = pl.ds(pl.multiple_of(j * 8, 8), 8)
        xs = {}
        for d in range(2):
            edge = 0 if d == 0 else 7
            seq_at = pl.ds(0 if d == 0 else last8, 8)
            hot_seq = window_onehot([tok_f[o, seq_at, :][edge : edge + 1, :] for o in range(7)])
            hot_own = window_onehot([tok_f[o, mine8, :][edge : edge + 1, :] for o in range(7)])
            for s in range(2):
                q = 2 * d + s
                xseq = silu_half(nn(hot_seq, tw[q]))
                xown = silu_half(nn(hot_own, tw[q]))
                if d == 0:
                    xs[q] = pltpu.roll(xseq[0:8, :], 5, 0)
                else:
                    xs[q] = xseq[CH - 8 :, :]
                for n in range(KW - 1):
                    t = n if d == 0 else CH - 1 - n
                    for i in range(4):
                        at = (d * 3 + n) * 8 + s * 4 + i
                        xrim[at : at + 1, :] = xown[t : t + 1, 128 * i : 128 * i + 128]
        diag = iota((H, E), 0) == (iota((H, E), 1) >> 6)
        sub16 = iota((16, E), 0)
        for q in range(4):
            d, s = q // 2, q % 2
            rim = jnp.concatenate([jnp.zeros((8, E), F32), xs[q]], axis=0)
            rim_h, rim_l = split(rim)
            for v in range(SYM):
                tail = slice((q * SYM + v + 1) * CH - 16, (q * SYM + v + 1) * CH)
                xch[tail, :] = jnp.where(
                    sub16 >= 13, rim_h.astype(F32), xch[tail, :].astype(F32)
                ).astype(BF16)
                xcl[tail, :] = jnp.where(
                    sub16 >= 13, rim_l.astype(F32), xcl[tail, :].astype(F32)
                ).astype(BF16)
                at = v * 16 + s * 8
                w = hist[d, at : at + 8, :] + hist[d, 80 + at : 88 + at, :]
                high, low = split(w)
                both = jnp.concatenate([high.astype(F32), low.astype(F32)], axis=0).astype(BF16)
                table = slice((q * SYM + v) * CH, (q * SYM + v + 1) * CH)
                one = nn(both, xch[table, :])
                two = nn(both, xcl[table, :])
                full = one[0:8, :] + one[8:16, :] + two[0:8, :]
                vec = jnp.sum(jnp.where(diag, full, 0.0), axis=0, keepdims=True)
                for i in range(4):
                    at = (d * SYM + v) * 8 + s * 4 + i
                    svec[at : at + 1, :] = vec[:, 128 * i : 128 * i + 128]
        total = nchunk * CH
        for d in range(2):
            state = []
            for w in range(SYM):
                value = jnp.zeros((8, CH), F32)
                for v in range(SYM):
                    at = (d * SYM + w) * 64 + v * 8
                    sat = (d * SYM + v) * 8
                    value = value + gtab[at : at + 8, :] * svec[sat : sat + 8, :]
                state.append(value)
            skip_t = cst[d * 8 : d * 8 + 8, :]
            for n in range(KW - 1):
                u = tok_s[n if d == 0 else total - 1 - n]
                x = xrim[(d * 3 + n) * 8 : (d * 3 + n) * 8 + 8, :]
                a = tile_at(atab, d * 64 + u * 8)
                state = [
                    a * state[w] + tile_at(gtab, (d * SYM + w) * 64 + u * 8) * x
                    for w in range(SYM)
                ]
                yrim[(d * 3 + n) * 8 : (d * 3 + n) * 8 + 8, :] = pick(state, u) + skip_t * x
            for w in range(SYM):
                ycar[(d * SYM + w) * 8 : (d * SYM + w) * 8 + 8, :] = state[w]

    first = step * CH
    unroll = 8

    def advance(d, ref, dest, n, decay, lead):
        local = n if d == 0 else CH - 1 - n
        u = tok_s[first + local]
        a = tile_at(atab, d * 64 + u * 8)
        if lead is not None:
            a = jnp.where(lead, 1.0, a)
        decay = decay * a
        y = tile_at(ref, local * 8) + decay * tile_at(ycar, d * SYM * 8 + u * 8)
        dest[pl.ds(pl.multiple_of(local * 8, 8), 8), :] = y * tile_at(zg, u * 8)
        return decay

    def group(g, carry):
        pa, pb = carry
        for i in range(unroll):
            n = g * unroll + i
            lead0 = (g == 0) & (step == 0) if i < 3 else None
            lead1 = (g == 0) & (step == nchunk - 1) if i < 3 else None
            pa = advance(0, yad, gad, n, pa, lead0)
            pb = advance(1, ybc, gbc, n, pb, lead1)
        return pa, pb

    lax.fori_loop(
        0, CH // unroll, group, (tile_at(pst, step * 8), tile_at(pst, (nchunk + step) * 8))
    )

    @pl.when(step == 0)
    def _():
        for n in range(3):
            gad[n * 8 : n * 8 + 8, :] = yrim[n * 8 : n * 8 + 8, :] * tile_at(zg, tok_s[n] * 8)

    @pl.when(step == nchunk - 1)
    def _():
        for n in range(3):
            at = (CH - 1 - n) * 8
            gbc[at : at + 8, :] = yrim[24 + n * 8 : 32 + n * 8, :] * tile_at(
                zg, tok_s[first + CH - 1 - n] * 8
            )

    mean = jnp.where(
        ((iota((2 * CH, CH), 0) & 127) >> 6) == (iota((2 * CH, CH), 1) >> 6), 1.0 / 64.0, 0.0
    ).astype(BF16)
    normed = None
    for d, ref in ((0, gad), (1, gbc)):
        g = ref[...]
        high, low = split(g * g)
        meansq = nn(jnp.concatenate([high, low], axis=1), mean)
        scaled = (g * lax.rsqrt(meansq + EPSILON)).reshape(CH, 8, CH) * cst[
            16 + d * 8 : 24 + d * 8, :
        ][None]
        normed = scaled if normed is None else normed + scaled
    mix[...] = normed.reshape(CH * 8, CH)
    parts = [mix[pl.ds(i, CH, stride=8), :].astype(BF16) for i in range(8)]
    mine_out = nn(jnp.concatenate(parts[0:4], axis=1), w_out[...]).astype(BF16).astype(F32)
    other = nn(jnp.concatenate(parts[4:8], axis=1), wflip[...]).astype(BF16).astype(F32)
    out[...] = (feat[...].astype(F32) + mine_out + other).astype(BF16)


def per_device(
    token_ids,
    embed_table,
    input_weight_matrix,
    output_weight_matrix,
    conv_weight,
    dt_bias,
    decay_rate,
    skip_gain,
    norm_gain,
):
    length = token_ids.shape[0]
    nchunk = length // CH
    own = lax.axis_size("seq")
    tok2 = token_ids.reshape(nchunk, CH)
    tok_all = lax.all_gather(tok2, "seq", tiled=True)
    rows = own * nchunk
    vm = pl.BlockSpec(memory_space=pltpu.VMEM)
    sm = pl.BlockSpec(memory_space=pltpu.SMEM)
    sds = jax.ShapeDtypeStruct
    shapes = (
        sds((length * 8, CH), F32),
        sds((length * 8, CH), F32),
        sds((length, D), BF16),
        sds((2 * 64, CH), F32),
        sds((2 * SYM * 64, CH), F32),
        sds((64, CH), F32),
        sds((32, CH), F32),
        sds((2 * SYM * 16, CH), F32),
        sds((4, CH, E), BF16),
        sds((4 * SYM * CH, E), BF16),
        sds((4 * SYM * CH, E), BF16),
        sds((2 * nchunk * 8, CH), F32),
        sds((E, D), BF16),
    )
    yad, ybc, feat, atab, gtab, zg, cst, lac, tw, xch, xcl, pst, wflip = pl.pallas_call(
        local_kernel,
        out_shape=shapes,
        in_specs=[sm] + [vm] * 9,
        out_specs=[vm] * len(shapes),
        scratch_shapes=[pltpu.VMEM((16, D), F32)],
        compiler_params=pltpu.CompilerParams(vmem_limit_bytes=40 * 1024 * 1024),
        cost_estimate=pl.CostEstimate(
            flops=4_000_000_000, bytes_accessed=16_000_000, transcendentals=4_000_000
        ),
        name="local_chains",
    )(
        token_ids, tok2, embed_table, input_weight_matrix, output_weight_matrix, conv_weight,
        dt_bias, decay_rate, skip_gain, norm_gain,
    )
    mine = lax.axis_index("seq").reshape(1).astype(jnp.int32)
    chunk_spec = pl.BlockSpec((CH * 8, CH), lambda i: (i, 0))
    out_spec = pl.BlockSpec((CH, D), lambda i: (i, 0))
    return pl.pallas_call(
        finish_kernel,
        grid=(nchunk,),
        out_shape=sds((length, D), BF16),
        in_specs=[sm, sm, vm, chunk_spec, chunk_spec, out_spec] + [vm] * 11,
        out_specs=out_spec,
        scratch_shapes=[
            pltpu.VMEM((7, rows, CH), F32),
            pltpu.VMEM((2, rows, CH), F32),
            pltpu.VMEM((2, CH, 2 * CH), BF16),
            pltpu.VMEM((2, 160, CH), F32),
            pltpu.VMEM((2 * SYM * 8, CH), F32),
            pltpu.VMEM((2 * 3 * 8, CH), F32),
            pltpu.VMEM((2 * SYM * 8, CH), F32),
            pltpu.VMEM((2 * 3 * 8, CH), F32),
            pltpu.VMEM((CH * 8, CH), F32),
            pltpu.VMEM((CH * 8, CH), F32),
            pltpu.VMEM((CH * 8, CH), F32),
        ],
        compiler_params=pltpu.CompilerParams(vmem_limit_bytes=40 * 1024 * 1024),
        cost_estimate=pl.CostEstimate(
            flops=4_000_000_000, bytes_accessed=16_000_000, transcendentals=1_000_000
        ),
        name="finish_chains",
    )(
        mine, token_ids, tok_all, yad, ybc, feat, atab, gtab, zg, cst, lac, tw, xch, xcl, pst,
        output_weight_matrix, wflip,
    )


def solution(mesh):
    placed = (P(("batch", "seq")), P(), P(), P(), P(), P(), P(), P(), P())
    return jax.shard_map(
        per_device, mesh=mesh, in_specs=placed, out_specs=P(("batch", "seq"), None), check_vma=False
    )
```

```python
import jax
import jax.numpy as jnp
from jax import lax
from jax.experimental import pallas as pl
from jax.experimental.pallas import tpu as pltpu
from jax.sharding import PartitionSpec as P

D = 256
E = 512
NS = 16
H = 8
KW = 4
SYM = 5
LOG2E = 1.4426950408889634
EPSILON = 1e-05
CH = 128

F32 = jnp.float32
BF16 = jnp.bfloat16

CHAINS = ((0, 0, 0), (0, 1, 1), (1, 0, 1), (1, 1, 0))


def iota(shape, dim):
    return lax.broadcasted_iota(jnp.int32, shape, dim)


def nn(a, b, **kw):
    return lax.dot_general(a, b, (((1,), (0,)), ((), ())), preferred_element_type=F32, **kw)


def nt(a, b, **kw):
    return lax.dot_general(a, b, (((1,), (1,)), ((), ())), preferred_element_type=F32, **kw)


def split(value):
    high = value.astype(BF16)
    low = (value - high.astype(F32)).astype(BF16)
    return high, low


def softplus(x):
    return jnp.maximum(x, 0.0) + jnp.log1p(jnp.exp(-jnp.abs(x)))


def silu_half(half):
    return half + half * jnp.tanh(half)


def tap_row(direction, j):
    return j if direction == 0 else 2 * (KW - 1) - j


def window_onehot(rows):
    sub = iota((8, CH), 0).astype(F32)
    blocks = [jnp.where(row == sub, 1.0, 0.0) for row in rows]
    blocks.append(jnp.zeros((8, CH), F32))
    stacked = jnp.concatenate(blocks + blocks, axis=0)
    return stacked.T.astype(BF16)


def shifted(tok, offset, rows):
    if offset == 0:
        return tok
    lane = iota((rows, CH), 1)
    row = iota((rows, CH), 0)
    moved = pltpu.roll(tok, (-offset) % CH, 1)
    if offset < 0:
        other = pltpu.roll(moved, 1, 0)
        crossing = lane < -offset
        outside = crossing & (row == 0)
    else:
        other = pltpu.roll(moved, rows - 1, 0)
        crossing = lane >= CH - offset
        outside = crossing & (row == rows - 1)
    return jnp.where(outside, 5.0, jnp.where(crossing, other, moved))


def pick(values, u):
    out = values[0]
    for k in range(1, SYM):
        out = jnp.where(u == k, values[k], out)
    return out


def tile_at(ref, row):
    return ref[pl.ds(pl.multiple_of(row, 8), 8), :]


def table_kernel(
    emb_h, w_in_h, w_out_h, cw_h, bias_h, rate_h, skip_h, gain_h,
    atab, gtab, zg, cst, lac, tw, xch, xcl, wflip, embk,
    emb, w_in, w_out, cw, bias, rate, skip, gain, emb16, sems,
):
    sources = (emb_h, w_in_h, w_out_h, cw_h, bias_h, rate_h, skip_h, gain_h)
    targets = (emb, w_in, w_out, cw, bias, rate, skip, gain)
    copies = [
        pltpu.make_async_copy(a, b, sems.at[i]) for i, (a, b) in enumerate(zip(sources, targets))
    ]
    for copy in copies:
        copy.start()
    for copy in copies:
        copy.wait()
    highest = lax.Precision.HIGHEST
    emb16[...] = jnp.zeros_like(emb16)
    e32 = emb[...].astype(F32)
    emb16[0:SYM, :] = e32
    for v in range(4):
        emb16[8 + v : 9 + v, :] = e32[3 - v : 4 - v, :]
    emb16[12:13, :] = e32[4:5, :]
    embs = emb16[...].astype(BF16)
    z16 = nt(embs, w_in[0:E, :]).astype(BF16).astype(F32)
    x16 = nt(embs, w_in[E : 2 * E, :]).astype(BF16).astype(F32)
    rest = nt(embs, w_in[2 * E :, :]).astype(BF16)
    nrest = 2 * NS + H
    expand = jnp.where(
        iota((nrest, E), 0) == (iota((nrest, E), 1) >> 6) + 2 * NS, 1.0, 0.0
    ).astype(BF16)
    heads = jnp.where(iota((H, E), 0) == (iota((H, E), 1) >> 6), 1.0, 0.0)
    r_exp = nn(rest, expand)
    bias_e = nn(bias[...], heads, precision=highest)
    rate_e = nn(rate[...], heads, precision=highest)
    skip_e = nn(skip[...], heads, precision=highest)
    shift = jnp.where(
        iota((nrest, nrest), 0) + NS == iota((nrest, nrest), 1),
        jnp.where(iota((nrest, nrest), 0) < NS, 1.0, 0.0),
        0.0,
    ).astype(BF16)
    rest_b = nn(rest, shift).astype(BF16)
    cb = nt(rest_b, rest)
    sz = z16 * (0.5 + 0.5 * jnp.tanh(0.5 * z16))
    for s in range(2):
        for i in range(4):
            zg[pl.ds(s * 4 + i, 8, stride=8), :] = sz[8 * s : 8 * s + 8, 128 * i : 128 * i + 128]
    pick_r = jnp.where(
        iota((H, nrest), 0) + 2 * NS == iota((H, nrest), 1), 1.0, 0.0
    ).astype(BF16)
    r_t = nt(pick_r, rest)
    eye = jnp.where(iota((H, H), 0) == iota((H, H), 1), 1.0, 0.0)
    bias_t = nt(eye, bias[...], precision=highest)
    rate_t = nt(eye, rate[...], precision=highest)
    for q, (d, s, k) in enumerate(CHAINS):
        dt = softplus(r_exp[8 * s : 8 * s + 8, :] + bias_e[k : k + 1, :])
        a = jnp.exp(-rate_e[k : k + 1, :] * dt)
        for i in range(4):
            lanes = slice(128 * i, 128 * i + 128)
            atab[pl.ds(d * 64 + s * 4 + i, 8, stride=8), :] = a[:, lanes]
            cst[d * 8 + s * 4 + i : d * 8 + s * 4 + i + 1, :] = skip_e[k : k + 1, lanes]
            cst[16 + d * 8 + s * 4 + i : 17 + d * 8 + s * 4 + i, :] = gain[k : k + 1, lanes]
        for u in range(SYM):
            g = cb[8 * s : 8 * s + 8, 8 * s + u : 8 * s + u + 1] * dt
            for i in range(4):
                gtab[pl.ds((d * SYM + u) * 64 + s * 4 + i, 8, stride=8), :] = g[
                    :, 128 * i : 128 * i + 128
                ]
        la = (
            -rate_t[:, k : k + 1] * softplus(r_t[:, 8 * s : 8 * s + 8] + bias_t[:, k : k + 1])
        ) * LOG2E
        for v in range(SYM):
            lac[(d * SYM + v) * 16 + s * 8 : (d * SYM + v) * 16 + s * 8 + 8, :] = jnp.broadcast_to(
                la[:, v : v + 1], (8, CH)
            )
        xs = x16[8 * s : 8 * s + 8, :]
        blocks = [jnp.zeros((8, E), F32)] * 8
        for j in range(KW):
            blocks[tap_row(d, j)] = (0.5 * cw[k, j : j + 1, :]) * xs
        high, low = split(jnp.concatenate(blocks, axis=0))
        tw[q, 0:64, :] = high
        tw[q, 64:128, :] = low
        code = iota((CH, CH), 0).astype(F32)
        lane = iota((CH, CH), 1) & 63
        slot = lane >> 3
        sym = (lane & 7).astype(F32)
        d0 = jnp.floor((code + 0.5) * (1.0 / 25.0))
        d01 = jnp.floor((code + 0.5) * (1.0 / 5.0))
        digits = (d0, d01 - 5.0 * d0, code - 5.0 * d01)
        hot = jnp.zeros((CH, CH), F32)
        for j in range(KW - 1):
            hot = jnp.where(
                slot == tap_row(d, j), jnp.where(sym == digits[j], 1.0, 0.0), hot
            )
        partial = nn(hot.astype(BF16), tw[q])
        last = blocks[tap_row(d, KW - 1)]
        for v in range(SYM):
            high, low = split(silu_half(partial + last[v : v + 1, :]))
            xch[(q * SYM + v) * CH : (q * SYM + v + 1) * CH, :] = high
            xcl[(q * SYM + v) * CH : (q * SYM + v + 1) * CH, :] = low
    flip = jnp.where(iota((D, D), 0) + iota((D, D), 1) == D - 1, 1.0, 0.0).astype(BF16)
    embk[...] = jnp.concatenate(
        [jnp.zeros((24, D), F32), emb16[0:8, :], jnp.zeros((96, D), F32)], axis=0
    ).astype(BF16)
    wflip[...] = nn(w_out[...], flip).astype(BF16)


def conv_kernel(tok_v, tw, embk, yad, ybc, feat):
    nchunk = tok_v.shape[0]
    tok = tok_v[...].astype(F32)
    shifts = [shifted(tok, o, nchunk) for o in range(-3, 4)]
    for c in range(nchunk):
        hot = window_onehot([sh[c : c + 1, :] for sh in shifts])
        feat[c * CH : (c + 1) * CH, :] = nn(hot, embk[...]).astype(BF16)
        for q, (d, s, k) in enumerate(CHAINS):
            x = silu_half(nn(hot, tw[q]))
            ref = (yad, ybc)[d]
            for i in range(4):
                ref[pl.ds(c * 8 * CH + s * 4 + i, CH, stride=8), :] = x[:, 128 * i : 128 * i + 128]
    total = nchunk * CH
    yad[0:24, :] = jnp.zeros((24, CH), F32)
    ybc[total * 8 - 24 : total * 8, :] = jnp.zeros((24, CH), F32)


def scan_kernel(tok_s, atab, gtab, cst, xad, xbc, yad, ybc, pst):
    total = tok_s.shape[0]
    nchunk = total // CH
    skip0 = cst[0:8, :]
    skip1 = cst[8:16, :]

    def advance(direction, src, ref, skip_t, t, state):
        u = tok_s[t]
        x = tile_at(src, t * 8)
        a = tile_at(atab, direction * 64 + u * 8)
        new = [
            a * state[w] + tile_at(gtab, (direction * SYM + w) * 64 + u * 8) * x
            for w in range(SYM)
        ]
        ref[pl.ds(pl.multiple_of(t * 8, 8), 8), :] = pick(new, u) + skip_t * x
        return new, a

    unroll = 8

    def group(g, carry):
        ya, yb, pa, pb = carry
        ya, yb = list(ya), list(yb)
        for i in range(unroll):
            n = g * unroll + i
            ya, a0 = advance(0, xad, yad, skip0, n, ya)
            yb, a1 = advance(1, xbc, ybc, skip1, total - 1 - n, yb)
            if i < 3:
                a0 = jnp.where(g == 0, 1.0, a0)
                a1 = jnp.where(g == 0, 1.0, a1)
            pa = pa * a0
            pb = pb * a1
        return tuple(ya), tuple(yb), pa, pb

    def chunk(c, carry):
        pst[pl.ds(pl.multiple_of(c * 8, 8), 8), :] = carry[2]
        pst[pl.ds(pl.multiple_of((2 * nchunk - 1 - c) * 8, 8), 8), :] = carry[3]
        per = CH // unroll
        return lax.fori_loop(c * per, (c + 1) * per, group, carry)

    zero = jnp.zeros((8, CH), F32)
    one = jnp.ones((8, CH), F32)
    lax.fori_loop(0, nchunk, chunk, ((zero,) * SYM, (zero,) * SYM, one, one))


def history_kernel(
    mine, tok_s, tok_all, atab, gtab, cst, lac, tw, xch, xcl,
    ycar, yrim,
    tok_f, code, tri, hist, svec, xrim,
):
    rows = tok_all.shape[0]
    own = rows // 8
    j = mine[0]
    for b in range(own):
        slot = (j ^ b) * 8
        tok_f[3, 8 * b : 8 * b + 8, :] = tok_all[pl.ds(pl.multiple_of(slot, 8), 8), :].astype(F32)
    tok = tok_f[3]
    for o in (-3, -2, -1, 1, 2, 3):
        tok_f[3 + o] = shifted(tok, o, rows)
    lane = iota((rows, CH), 1)
    row = iota((rows, CH), 0)
    lane_f = lane.astype(F32)
    before = 25.0 * tok_f[0] + 5.0 * tok_f[1] + tok_f[2]
    after = 25.0 * tok_f[6] + 5.0 * tok_f[5] + tok_f[4]
    code[0] = jnp.where((row == 0) & (lane < 3), 125.0 + lane_f, before)
    code[1] = jnp.where((row == rows - 1) & (lane >= CH - 3), lane_f, after)
    si = iota((CH, CH), 0)
    ri = iota((CH, CH), 1)
    ones = jnp.ones((CH, CH), F32)
    tri[0] = jnp.concatenate([jnp.where(si > ri, 1.0, 0.0), ones], axis=1).astype(BF16)
    tri[1] = jnp.concatenate([jnp.where(si < ri, 1.0, 0.0), ones], axis=1).astype(BF16)
    hist[...] = jnp.zeros_like(hist)
    sub8 = iota((8, CH), 0).astype(F32)
    subc = iota((CH, CH), 0).astype(F32)

    def block(b, off):
        side = jnp.where(b >= j, 1, 0)
        index = jnp.where(b >= j, b + 1, j - 1 - b)
        off = off * jnp.where(b == j, 0.0, 1.0)
        use_prefix = side.astype(F32)
        at = pl.ds(pl.multiple_of(index * 8, 8), 8)
        tk = tok_f[3, at, :]
        cd = code[side, at, :]
        hots = [jnp.where(tk[m : m + 1, :] == sub8, 1.0, 0.0) for m in range(8)]
        counts = nn(jnp.concatenate(hots, axis=0).astype(BF16), tri[side])
        totals = [counts[8 * m : 8 * m + 8, CH:] for m in range(8)]
        prefix = [jnp.zeros((8, CH), F32)]
        for m in range(8):
            prefix.append(prefix[-1] + totals[m])
        las = [lac[pl.ds(pl.multiple_of((side * SYM + v) * 16, 16), 16), :] for v in range(SYM)]
        acc = jnp.zeros((160, CH), F32)
        for pair in range(4):
            lefts, rights = [], []
            for m in (2 * pair, 2 * pair + 1):
                suffix = prefix[8] - prefix[m + 1]
                inside = suffix + use_prefix * (prefix[m] - suffix)
                count = counts[8 * m : 8 * m + 8, :CH] + off + inside
                exponent = las[0] * count[0:1, :]
                for v in range(1, SYM):
                    exponent = exponent + las[v] * count[v : v + 1, :]
                weight = jnp.exp2(exponent)
                masked = jnp.concatenate(
                    [jnp.where(tk[m : m + 1, :] == float(v), weight, 0.0) for v in range(SYM)],
                    axis=0,
                )
                high, low = split(masked)
                lefts.append(jnp.concatenate([high, low], axis=0))
                rights.append(jnp.where(cd[m : m + 1, :] == subc, 1.0, 0.0).astype(BF16))
            acc = acc + nt(
                jnp.concatenate(lefts, axis=1), jnp.concatenate(rights, axis=1)
            )
        hist[side] = hist[side] + acc
        return off + prefix[8]

    lax.fori_loop(0, own - 1, block, jnp.zeros((8, CH), F32))

    last8 = rows - 8
    mine8 = pl.ds(pl.multiple_of(j * 8, 8), 8)
    xs = {}
    for d in range(2):
        edge = 0 if d == 0 else 7
        seq_at = pl.ds(0 if d == 0 else last8, 8)
        hot_seq = window_onehot([tok_f[o, seq_at, :][edge : edge + 1, :] for o in range(7)])
        hot_own = window_onehot([tok_f[o, mine8, :][edge : edge + 1, :] for o in range(7)])
        for s in range(2):
            q = 2 * d + s
            xseq = silu_half(nn(hot_seq, tw[q]))
            xown = silu_half(nn(hot_own, tw[q]))
            if d == 0:
                xs[q] = pltpu.roll(xseq[0:8, :], 5, 0)
            else:
                xs[q] = xseq[CH - 8 :, :]
            for n in range(KW - 1):
                t = n if d == 0 else CH - 1 - n
                for i in range(4):
                    at = (d * 3 + n) * 8 + s * 4 + i
                    xrim[at : at + 1, :] = xown[t : t + 1, 128 * i : 128 * i + 128]
    diag = iota((H, E), 0) == (iota((H, E), 1) >> 6)
    sub16 = iota((16, E), 0)
    for q in range(4):
        d, s = q // 2, q % 2
        rim = jnp.concatenate([jnp.zeros((8, E), F32), xs[q]], axis=0)
        rim_h, rim_l = split(rim)
        for v in range(SYM):
            start = (q * SYM + v) * CH
            body = slice(start, start + CH - 16)
            tail = slice(start + CH - 16, start + CH)
            tail_h = jnp.where(sub16 >= 13, rim_h.astype(F32), xch[tail, :].astype(F32))
            tail_l = jnp.where(sub16 >= 13, rim_l.astype(F32), xcl[tail, :].astype(F32))
            table_h = jnp.concatenate([xch[body, :], tail_h.astype(BF16)], axis=0)
            table_l = jnp.concatenate([xcl[body, :], tail_l.astype(BF16)], axis=0)
            at = v * 16 + s * 8
            w = hist[d, at : at + 8, :] + hist[d, 80 + at : 88 + at, :]
            high, low = split(w)
            both = jnp.concatenate([high.astype(F32), low.astype(F32)], axis=0).astype(BF16)
            one = nn(both, table_h)
            two = nn(both, table_l)
            full = one[0:8, :] + one[8:16, :] + two[0:8, :]
            vec = jnp.sum(jnp.where(diag, full, 0.0), axis=0, keepdims=True)
            for i in range(4):
                at = (d * SYM + v) * 8 + s * 4 + i
                svec[at : at + 1, :] = vec[:, 128 * i : 128 * i + 128]
    total = tok_s.shape[0]
    for d in range(2):
        state = []
        for w in range(SYM):
            value = jnp.zeros((8, CH), F32)
            for v in range(SYM):
                at = (d * SYM + w) * 64 + v * 8
                sat = (d * SYM + v) * 8
                value = value + gtab[at : at + 8, :] * svec[sat : sat + 8, :]
            state.append(value)
        skip_t = cst[d * 8 : d * 8 + 8, :]
        for n in range(KW - 1):
            u = tok_s[n if d == 0 else total - 1 - n]
            x = xrim[(d * 3 + n) * 8 : (d * 3 + n) * 8 + 8, :]
            a = tile_at(atab, d * 64 + u * 8)
            state = [
                a * state[w] + tile_at(gtab, (d * SYM + w) * 64 + u * 8) * x
                for w in range(SYM)
            ]
            yrim[(d * 3 + n) * 8 : (d * 3 + n) * 8 + 8, :] = pick(state, u) + skip_t * x
        for w in range(SYM):
            ycar[(d * SYM + w) * 8 : (d * SYM + w) * 8 + 8, :] = state[w]


def finish_kernel(
    tok_s, yad, ybc, feat, atab, zg, cst, pst, ycar, yrim, w_out, wflip,
    out,
    gad, gbc, mix,
):
    step = pl.program_id(0)
    nchunk = pl.num_programs(0)
    first = step * CH
    unroll = 8

    def advance(d, ref, dest, n, decay, lead):
        local = n if d == 0 else CH - 1 - n
        u = tok_s[first + local]
        a = tile_at(atab, d * 64 + u * 8)
        if lead is not None:
            a = jnp.where(lead, 1.0, a)
        decay = decay * a
        y = tile_at(ref, local * 8) + decay * tile_at(ycar, d * SYM * 8 + u * 8)
        dest[pl.ds(pl.multiple_of(local * 8, 8), 8), :] = y * tile_at(zg, u * 8)
        return decay

    def group(g, carry):
        pa, pb = carry
        for i in range(unroll):
            n = g * unroll + i
            lead0 = (g == 0) & (step == 0) if i < 3 else None
            lead1 = (g == 0) & (step == nchunk - 1) if i < 3 else None
            pa = advance(0, yad, gad, n, pa, lead0)
            pb = advance(1, ybc, gbc, n, pb, lead1)
        return pa, pb

    lax.fori_loop(
        0, CH // unroll, group, (tile_at(pst, step * 8), tile_at(pst, (nchunk + step) * 8))
    )

    @pl.when(step == 0)
    def _():
        for n in range(3):
            gad[n * 8 : n * 8 + 8, :] = yrim[n * 8 : n * 8 + 8, :] * tile_at(zg, tok_s[n] * 8)

    @pl.when(step == nchunk - 1)
    def _():
        for n in range(3):
            at = (CH - 1 - n) * 8
            gbc[at : at + 8, :] = yrim[24 + n * 8 : 32 + n * 8, :] * tile_at(
                zg, tok_s[first + CH - 1 - n] * 8
            )

    mean = jnp.where(
        ((iota((2 * CH, CH), 0) & 127) >> 6) == (iota((2 * CH, CH), 1) >> 6), 1.0 / 64.0, 0.0
    ).astype(BF16)
    normed = None
    for d, ref in ((0, gad), (1, gbc)):
        g = ref[...]
        high, low = split(g * g)
        meansq = nn(jnp.concatenate([high, low], axis=1), mean)
        scaled = (g * lax.rsqrt(meansq + EPSILON)).reshape(CH, 8, CH) * cst[
            16 + d * 8 : 24 + d * 8, :
        ][None]
        normed = scaled if normed is None else normed + scaled
    mix[...] = normed.reshape(CH * 8, CH)
    parts = [mix[pl.ds(i, CH, stride=8), :].astype(BF16) for i in range(8)]
    mine_out = nn(jnp.concatenate(parts[0:4], axis=1), w_out[...]).astype(BF16).astype(F32)
    other = nn(jnp.concatenate(parts[4:8], axis=1), wflip[...]).astype(BF16).astype(F32)
    out[...] = (feat[...].astype(F32) + mine_out + other).astype(BF16)


def per_device(
    token_ids,
    embed_table,
    input_weight_matrix,
    output_weight_matrix,
    conv_weight,
    dt_bias,
    decay_rate,
    skip_gain,
    norm_gain,
):
    length = token_ids.shape[0]
    nchunk = length // CH
    own = lax.axis_size("seq")
    tok2 = token_ids.reshape(nchunk, CH)
    rounds = own.bit_length() - 1
    rows = own * nchunk
    vm = pl.BlockSpec(memory_space=pltpu.VMEM)
    sm = pl.BlockSpec(memory_space=pltpu.SMEM)
    hbm = pl.BlockSpec(memory_space=pl.ANY)
    sds = jax.ShapeDtypeStruct
    mib = 1024 * 1024

    def exchanged(blocks, bit):
        route = [(i, i ^ (1 << bit)) for i in range(own)]
        return jnp.concatenate([blocks, lax.ppermute(blocks, "seq", route)], axis=0)

    def params(limit):
        return pltpu.CompilerParams(vmem_limit_bytes=limit * mib)

    def cost(flops, moved):
        return pl.CostEstimate(flops=flops, bytes_accessed=moved, transcendentals=0)

    blocks = exchanged(tok2, 0)
    table_shapes = (
        sds((2 * 64, CH), F32),
        sds((2 * SYM * 64, CH), F32),
        sds((64, CH), F32),
        sds((32, CH), F32),
        sds((2 * SYM * 16, CH), F32),
        sds((4, CH, E), BF16),
        sds((4 * SYM * CH, E), BF16),
        sds((4 * SYM * CH, E), BF16),
        sds((E, D), BF16),
        sds((CH, D), BF16),
    )
    weights = (
        embed_table, input_weight_matrix.T, output_weight_matrix, conv_weight, dt_bias, decay_rate,
        skip_gain, norm_gain,
    )
    atab, gtab, zg, cst, lac, tw, xch, xcl, wflip, embk = pl.pallas_call(
        table_kernel,
        out_shape=table_shapes,
        in_specs=[hbm] * 8,
        out_specs=[vm] * len(table_shapes),
        scratch_shapes=[pltpu.VMEM(w.shape, w.dtype) for w in weights]
        + [pltpu.VMEM((16, D), F32), pltpu.SemaphoreType.DMA((8,))],
        compiler_params=params(56),
        cost_estimate=cost(1_000_000_000, 8_000_000),
        name="symbol_tables",
    )(*weights)
    blocks, tw, embk = lax.optimization_barrier((blocks, tw, embk))
    if rounds > 1:
        blocks = exchanged(blocks, 1)
    xad, xbc, feat = pl.pallas_call(
        conv_kernel,
        out_shape=(sds((length * 8, CH), F32), sds((length * 8, CH), F32), sds((length, D), BF16)),
        in_specs=[vm] * 3,
        out_specs=[vm] * 3,
        compiler_params=params(20),
        cost_estimate=cost(2_000_000_000, 9_000_000),
        name="convolve",
    )(tok2, tw, embk)
    blocks, xad, xbc = lax.optimization_barrier((blocks, xad, xbc))
    for bit in range(2, rounds):
        blocks = exchanged(blocks, bit)
    yad, ybc, pst = pl.pallas_call(
        scan_kernel,
        out_shape=(
            sds((length * 8, CH), F32),
            sds((length * 8, CH), F32),
            sds((2 * nchunk * 8, CH), F32),
        ),
        in_specs=[sm] + [vm] * 5,
        out_specs=[vm] * 3,
        input_output_aliases={4: 0, 5: 1},
        compiler_params=params(20),
        cost_estimate=cost(4_000_000_000, 16_000_000),
        name="scan_block",
    )(token_ids, atab, gtab, cst, xad, xbc)
    blocks, yad, ybc, pst = lax.optimization_barrier((blocks, yad, ybc, pst))
    mine = lax.axis_index("seq").reshape(1).astype(jnp.int32)
    ycar, yrim = pl.pallas_call(
        history_kernel,
        out_shape=(sds((2 * SYM * 8, CH), F32), sds((2 * 3 * 8, CH), F32)),
        in_specs=[sm, sm] + [vm] * 8,
        out_specs=[vm] * 2,
        scratch_shapes=[
            pltpu.VMEM((7, rows, CH), F32),
            pltpu.VMEM((2, rows, CH), F32),
            pltpu.VMEM((2, CH, 2 * CH), BF16),
            pltpu.VMEM((2, 160, CH), F32),
            pltpu.VMEM((2 * SYM * 8, CH), F32),
            pltpu.VMEM((2 * 3 * 8, CH), F32),
        ],
        compiler_params=params(20),
        cost_estimate=cost(2_000_000_000, 6_000_000),
        name="history",
    )(mine, token_ids, blocks, atab, gtab, cst, lac, tw, xch, xcl)
    chunk_spec = pl.BlockSpec((CH * 8, CH), lambda i: (i, 0))
    out_spec = pl.BlockSpec((CH, D), lambda i: (i, 0))
    return pl.pallas_call(
        finish_kernel,
        grid=(nchunk,),
        out_shape=sds((length, D), BF16),
        in_specs=[sm, chunk_spec, chunk_spec, out_spec] + [vm] * 8,
        out_specs=out_spec,
        scratch_shapes=[pltpu.VMEM((CH * 8, CH), F32)] * 3,
        compiler_params=params(20),
        cost_estimate=cost(4_000_000_000, 16_000_000),
        name="finish",
    )(
        token_ids, yad, ybc, feat, atab, zg, cst, pst, ycar, yrim, output_weight_matrix, wflip
    )


def solution(mesh):
    placed = (P(("batch", "seq")), P(), P(), P(), P(), P(), P(), P(), P())
    return jax.shard_map(
        per_device, mesh=mesh, in_specs=placed, out_specs=P(("batch", "seq"), None), check_vma=False
    )
```

```python
import jax
import jax.numpy as jnp
from jax import lax
from jax.experimental import pallas as pl
from jax.experimental.pallas import tpu as pltpu
from jax.sharding import PartitionSpec as P

D = 256
E = 512
NS = 16
H = 8
KW = 4
SYM = 5
LOG2E = 1.4426950408889634
EPSILON = 1e-05
CH = 128

F32 = jnp.float32
BF16 = jnp.bfloat16

CHAINS = ((0, 0, 0), (0, 1, 1), (1, 0, 1), (1, 1, 0))


def iota(shape, dim):
    return lax.broadcasted_iota(jnp.int32, shape, dim)


def nn(a, b, **kw):
    return lax.dot_general(a, b, (((1,), (0,)), ((), ())), preferred_element_type=F32, **kw)


def nt(a, b, **kw):
    return lax.dot_general(a, b, (((1,), (1,)), ((), ())), preferred_element_type=F32, **kw)


def split(value):
    high = value.astype(BF16)
    low = (value - high.astype(F32)).astype(BF16)
    return high, low


def softplus(x):
    return jnp.maximum(x, 0.0) + jnp.log1p(jnp.exp(-jnp.abs(x)))


def silu_half(half):
    return half + half * jnp.tanh(half)


def tap_row(direction, j):
    return j if direction == 0 else 2 * (KW - 1) - j


def window_onehot(rows):
    sub = iota((8, CH), 0).astype(F32)
    blocks = [jnp.where(row == sub, 1.0, 0.0) for row in rows]
    blocks.append(jnp.zeros((8, CH), F32))
    stacked = jnp.concatenate(blocks + blocks, axis=0)
    return stacked.T.astype(BF16)


def shifted(tok, offset, rows):
    if offset == 0:
        return tok
    lane = iota((rows, CH), 1)
    row = iota((rows, CH), 0)
    moved = pltpu.roll(tok, (-offset) % CH, 1)
    if offset < 0:
        other = pltpu.roll(moved, 1, 0)
        crossing = lane < -offset
        outside = crossing & (row == 0)
    else:
        other = pltpu.roll(moved, rows - 1, 0)
        crossing = lane >= CH - offset
        outside = crossing & (row == rows - 1)
    return jnp.where(outside, 5.0, jnp.where(crossing, other, moved))


def pick(values, u):
    low = (u & 1) == 1
    first = jnp.where(low, values[1], values[0])
    second = jnp.where(low, values[3], values[2])
    return jnp.where(u > 3, values[4], jnp.where((u & 2) == 2, second, first))


def tile_at(ref, row):
    return ref[pl.ds(pl.multiple_of(row, 8), 8), :]


def table_kernel(
    pack, w_in,
    atab, gtab, zg, cst, lac, tw, xch, xcl, embk,
    emb16,
):
    gain = pack[8:10, :]
    bias = pack[10:12, 0:H]
    rate = pack[12:14, 0:H]
    skip = pack[14:16, 0:H]
    e32 = pack[16:21, 0:D]
    highest = lax.Precision.HIGHEST
    emb16[...] = jnp.zeros_like(emb16)
    emb16[0:SYM, :] = e32
    for v in range(4):
        emb16[8 + v : 9 + v, :] = e32[3 - v : 4 - v, :]
    emb16[12:13, :] = e32[4:5, :]
    embs = emb16[...].astype(BF16)
    z16 = nt(embs, w_in[0:E, :]).astype(BF16).astype(F32)
    x16 = nt(embs, w_in[E : 2 * E, :]).astype(BF16).astype(F32)
    rest = nt(embs, w_in[2 * E :, :]).astype(BF16)
    nrest = 2 * NS + H
    expand = jnp.where(
        iota((nrest, E), 0) == (iota((nrest, E), 1) >> 6) + 2 * NS, 1.0, 0.0
    ).astype(BF16)
    heads = jnp.where(iota((H, E), 0) == (iota((H, E), 1) >> 6), 1.0, 0.0)
    r_exp = nn(rest, expand)
    bias_e = nn(bias, heads, precision=highest)
    rate_e = nn(rate, heads, precision=highest)
    skip_e = nn(skip, heads, precision=highest)
    shift = jnp.where(
        iota((nrest, nrest), 0) + NS == iota((nrest, nrest), 1),
        jnp.where(iota((nrest, nrest), 0) < NS, 1.0, 0.0),
        0.0,
    ).astype(BF16)
    rest_b = nn(rest, shift).astype(BF16)
    cb = nt(rest_b, rest)
    sz = z16 * (0.5 + 0.5 * jnp.tanh(0.5 * z16))
    for s in range(2):
        for i in range(4):
            zg[pl.ds(s * 4 + i, 8, stride=8), :] = sz[8 * s : 8 * s + 8, 128 * i : 128 * i + 128]
    pick_r = jnp.where(
        iota((H, nrest), 0) + 2 * NS == iota((H, nrest), 1), 1.0, 0.0
    ).astype(BF16)
    r_t = nt(pick_r, rest)
    eye = jnp.where(iota((H, H), 0) == iota((H, H), 1), 1.0, 0.0)
    bias_t = nt(eye, bias, precision=highest)
    rate_t = nt(eye, rate, precision=highest)
    for q, (d, s, k) in enumerate(CHAINS):
        dt = softplus(r_exp[8 * s : 8 * s + 8, :] + bias_e[k : k + 1, :])
        a = jnp.exp(-rate_e[k : k + 1, :] * dt)
        for i in range(4):
            lanes = slice(128 * i, 128 * i + 128)
            atab[pl.ds(d * 64 + s * 4 + i, 8, stride=8), :] = a[:, lanes]
            cst[d * 8 + s * 4 + i : d * 8 + s * 4 + i + 1, :] = skip_e[k : k + 1, lanes]
            cst[16 + d * 8 + s * 4 + i : 17 + d * 8 + s * 4 + i, :] = gain[k : k + 1, lanes]
        for u in range(SYM):
            g = cb[8 * s : 8 * s + 8, 8 * s + u : 8 * s + u + 1] * dt
            for i in range(4):
                gtab[pl.ds((d * SYM + u) * 64 + s * 4 + i, 8, stride=8), :] = g[
                    :, 128 * i : 128 * i + 128
                ]
        la = (
            -rate_t[:, k : k + 1] * softplus(r_t[:, 8 * s : 8 * s + 8] + bias_t[:, k : k + 1])
        ) * LOG2E
        for v in range(SYM):
            lac[(d * SYM + v) * 16 + s * 8 : (d * SYM + v) * 16 + s * 8 + 8, :] = jnp.broadcast_to(
                la[:, v : v + 1], (8, CH)
            )
        xs = x16[8 * s : 8 * s + 8, :]
        blocks = [jnp.zeros((8, E), F32)] * 8
        for j in range(KW):
            blocks[tap_row(d, j)] = (0.5 * pack[KW * k + j : KW * k + j + 1, :]) * xs
        high, low = split(jnp.concatenate(blocks, axis=0))
        tw[q, 0:64, :] = high
        tw[q, 64:128, :] = low
        code = iota((CH, CH), 0).astype(F32)
        lane = iota((CH, CH), 1) & 63
        slot = lane >> 3
        sym = (lane & 7).astype(F32)
        d0 = jnp.floor((code + 0.5) * (1.0 / 25.0))
        d01 = jnp.floor((code + 0.5) * (1.0 / 5.0))
        digits = (d0, d01 - 5.0 * d0, code - 5.0 * d01)
        hot = jnp.zeros((CH, CH), F32)
        for j in range(KW - 1):
            hot = jnp.where(
                slot == tap_row(d, j), jnp.where(sym == digits[j], 1.0, 0.0), hot
            )
        partial = nn(hot.astype(BF16), tw[q])
        last = blocks[tap_row(d, KW - 1)]
        for v in range(SYM):
            high, low = split(silu_half(partial + last[v : v + 1, :]))
            xch[(q * SYM + v) * CH : (q * SYM + v + 1) * CH, :] = high
            xcl[(q * SYM + v) * CH : (q * SYM + v + 1) * CH, :] = low
    embk[...] = jnp.concatenate(
        [jnp.zeros((24, D), F32), emb16[0:8, :], jnp.zeros((96, D), F32)], axis=0
    ).astype(BF16)


def conv_kernel(tok_v, tw, embk, yad, ybc, feat):
    nchunk = tok_v.shape[0]
    tok = tok_v[...].astype(F32)
    shifts = [shifted(tok, o, nchunk) for o in range(-3, 4)]
    for c in range(nchunk):
        hot = window_onehot([sh[c : c + 1, :] for sh in shifts])
        feat[c * CH : (c + 1) * CH, :] = nn(hot, embk[...]).astype(BF16)
        for q, (d, s, k) in enumerate(CHAINS):
            x = silu_half(nn(hot, tw[q]))
            ref = (yad, ybc)[d]
            for i in range(4):
                ref[pl.ds(c * 8 * CH + s * 4 + i, CH, stride=8), :] = x[:, 128 * i : 128 * i + 128]
    total = nchunk * CH
    yad[0:24, :] = jnp.zeros((24, CH), F32)
    ybc[total * 8 - 24 : total * 8, :] = jnp.zeros((24, CH), F32)


def scan_kernel(tok_s, atab, gtab, cst, xad, xbc, yad, ybc, pst):
    total = tok_s.shape[0]
    nchunk = total // CH
    skip0 = cst[0:8, :]
    skip1 = cst[8:16, :]

    def advance(direction, src, skip_t, t, state):
        u = tok_s[t]
        x = tile_at(src, t * 8)
        a = tile_at(atab, direction * 64 + u * 8)
        new = [
            a * state[w] + tile_at(gtab, (direction * SYM + w) * 64 + u * 8) * x
            for w in range(SYM)
        ]
        return new, a, pick(new, u) + skip_t * x

    unroll = 32
    held = 8

    def group(g, carry):
        ya, yb, pa, pb = carry
        ya, yb = list(ya), list(yb)
        for begin in range(0, unroll, held):
            done = []
            for i in range(begin, begin + held):
                n = g * unroll + i
                m = total - 1 - n
                ya, a0, out0 = advance(0, xad, skip0, n, ya)
                yb, a1, out1 = advance(1, xbc, skip1, m, yb)
                done.append((n, m, out0, out1))
                if i < 3:
                    a0 = jnp.where(g == 0, 1.0, a0)
                    a1 = jnp.where(g == 0, 1.0, a1)
                pa = pa * a0
                pb = pb * a1
            for n, m, out0, out1 in done:
                yad[pl.ds(pl.multiple_of(n * 8, 8), 8), :] = out0
                ybc[pl.ds(pl.multiple_of(m * 8, 8), 8), :] = out1
        return tuple(ya), tuple(yb), pa, pb

    def chunk(c, carry):
        pst[pl.ds(pl.multiple_of(c * 8, 8), 8), :] = carry[2]
        pst[pl.ds(pl.multiple_of((2 * nchunk - 1 - c) * 8, 8), 8), :] = carry[3]
        per = CH // unroll
        return lax.fori_loop(c * per, (c + 1) * per, group, carry)

    zero = jnp.zeros((8, CH), F32)
    one = jnp.ones((8, CH), F32)
    lax.fori_loop(0, nchunk, chunk, ((zero,) * SYM, (zero,) * SYM, one, one))


def history_kernel(
    mine, tok_s, tok_all, atab, gtab, cst, lac, tw, xch, xcl,
    ycar, yrim,
    tok_f, code, tri, hist, svec, xrim,
):
    rows = tok_all.shape[0]
    own = rows // 8
    j = mine[0]
    for b in range(own):
        slot = (j ^ b) * 8
        tok_f[3, 8 * b : 8 * b + 8, :] = tok_all[pl.ds(pl.multiple_of(slot, 8), 8), :].astype(F32)
    tok = tok_f[3]
    for o in (-3, -2, -1, 1, 2, 3):
        tok_f[3 + o] = shifted(tok, o, rows)
    lane = iota((rows, CH), 1)
    row = iota((rows, CH), 0)
    lane_f = lane.astype(F32)
    before = 25.0 * tok_f[0] + 5.0 * tok_f[1] + tok_f[2]
    after = 25.0 * tok_f[6] + 5.0 * tok_f[5] + tok_f[4]
    code[0] = jnp.where((row == 0) & (lane < 3), 125.0 + lane_f, before)
    code[1] = jnp.where((row == rows - 1) & (lane >= CH - 3), lane_f, after)
    si = iota((CH, CH), 0)
    ri = iota((CH, CH), 1)
    ones = jnp.ones((CH, CH), F32)
    tri[0] = jnp.concatenate([jnp.where(si > ri, 1.0, 0.0), ones], axis=1).astype(BF16)
    tri[1] = jnp.concatenate([jnp.where(si < ri, 1.0, 0.0), ones], axis=1).astype(BF16)
    hist[...] = jnp.zeros_like(hist)
    sub8 = iota((8, CH), 0).astype(F32)
    subc = iota((CH, CH), 0).astype(F32)

    def block(b, off):
        side = jnp.where(b >= j, 1, 0)
        index = jnp.where(b >= j, b + 1, j - 1 - b)
        off = off * jnp.where(b == j, 0.0, 1.0)
        use_prefix = side.astype(F32)
        at = pl.ds(pl.multiple_of(index * 8, 8), 8)
        tk = tok_f[3, at, :]
        cd = code[side, at, :]
        hots = [jnp.where(tk[m : m + 1, :] == sub8, 1.0, 0.0) for m in range(8)]
        counts = nn(jnp.concatenate(hots, axis=0).astype(BF16), tri[side])
        totals = [counts[8 * m : 8 * m + 8, CH:] for m in range(8)]
        prefix = [jnp.zeros((8, CH), F32)]
        for m in range(8):
            prefix.append(prefix[-1] + totals[m])
        las = [lac[pl.ds(pl.multiple_of((side * SYM + v) * 16, 16), 16), :] for v in range(SYM)]
        acc = jnp.zeros((160, CH), F32)
        for pair in range(4):
            lefts, rights = [], []
            for m in (2 * pair, 2 * pair + 1):
                suffix = prefix[8] - prefix[m + 1]
                inside = suffix + use_prefix * (prefix[m] - suffix)
                count = counts[8 * m : 8 * m + 8, :CH] + off + inside
                exponent = las[0] * count[0:1, :]
                for v in range(1, SYM):
                    exponent = exponent + las[v] * count[v : v + 1, :]
                weight = jnp.exp2(exponent)
                masked = jnp.concatenate(
                    [jnp.where(tk[m : m + 1, :] == float(v), weight, 0.0) for v in range(SYM)],
                    axis=0,
                )
                high, low = split(masked)
                lefts.append(jnp.concatenate([high, low], axis=0))
                rights.append(jnp.where(cd[m : m + 1, :] == subc, 1.0, 0.0).astype(BF16))
            acc = acc + nt(
                jnp.concatenate(lefts, axis=1), jnp.concatenate(rights, axis=1)
            )
        hist[side] = hist[side] + acc
        return off + prefix[8]

    lax.fori_loop(0, own - 1, block, jnp.zeros((8, CH), F32))

    last8 = rows - 8
    mine8 = pl.ds(pl.multiple_of(j * 8, 8), 8)
    xs = {}
    for d in range(2):
        edge = 0 if d == 0 else 7
        seq_at = pl.ds(0 if d == 0 else last8, 8)
        hot_seq = window_onehot([tok_f[o, seq_at, :][edge : edge + 1, :] for o in range(7)])
        hot_own = window_onehot([tok_f[o, mine8, :][edge : edge + 1, :] for o in range(7)])
        for s in range(2):
            q = 2 * d + s
            xseq = silu_half(nn(hot_seq, tw[q]))
            xown = silu_half(nn(hot_own, tw[q]))
            if d == 0:
                xs[q] = pltpu.roll(xseq[0:8, :], 5, 0)
            else:
                xs[q] = xseq[CH - 8 :, :]
            for n in range(KW - 1):
                t = n if d == 0 else CH - 1 - n
                for i in range(4):
                    at = (d * 3 + n) * 8 + s * 4 + i
                    xrim[at : at + 1, :] = xown[t : t + 1, 128 * i : 128 * i + 128]
    diag = iota((H, E), 0) == (iota((H, E), 1) >> 6)
    sub16 = iota((16, E), 0)
    for q in range(4):
        d, s = q // 2, q % 2
        rim = jnp.concatenate([jnp.zeros((8, E), F32), xs[q]], axis=0)
        rim_h, rim_l = split(rim)
        for v in range(SYM):
            start = (q * SYM + v) * CH
            body = slice(start, start + CH - 16)
            tail = slice(start + CH - 16, start + CH)
            tail_h = jnp.where(sub16 >= 13, rim_h.astype(F32), xch[tail, :].astype(F32))
            tail_l = jnp.where(sub16 >= 13, rim_l.astype(F32), xcl[tail, :].astype(F32))
            table_h = jnp.concatenate([xch[body, :], tail_h.astype(BF16)], axis=0)
            table_l = jnp.concatenate([xcl[body, :], tail_l.astype(BF16)], axis=0)
            at = v * 16 + s * 8
            w = hist[d, at : at + 8, :] + hist[d, 80 + at : 88 + at, :]
            high, low = split(w)
            both = jnp.concatenate([high.astype(F32), low.astype(F32)], axis=0).astype(BF16)
            one = nn(both, table_h)
            two = nn(both, table_l)
            full = one[0:8, :] + one[8:16, :] + two[0:8, :]
            vec = jnp.sum(jnp.where(diag, full, 0.0), axis=0, keepdims=True)
            for i in range(4):
                at = (d * SYM + v) * 8 + s * 4 + i
                svec[at : at + 1, :] = vec[:, 128 * i : 128 * i + 128]
    total = tok_s.shape[0]
    for d in range(2):
        state = []
        for w in range(SYM):
            value = jnp.zeros((8, CH), F32)
            for v in range(SYM):
                at = (d * SYM + w) * 64 + v * 8
                sat = (d * SYM + v) * 8
                value = value + gtab[at : at + 8, :] * svec[sat : sat + 8, :]
            state.append(value)
        skip_t = cst[d * 8 : d * 8 + 8, :]
        for n in range(KW - 1):
            u = tok_s[n if d == 0 else total - 1 - n]
            x = xrim[(d * 3 + n) * 8 : (d * 3 + n) * 8 + 8, :]
            a = tile_at(atab, d * 64 + u * 8)
            state = [
                a * state[w] + tile_at(gtab, (d * SYM + w) * 64 + u * 8) * x
                for w in range(SYM)
            ]
            yrim[(d * 3 + n) * 8 : (d * 3 + n) * 8 + 8, :] = pick(state, u) + skip_t * x
        for w in range(SYM):
            ycar[(d * SYM + w) * 8 : (d * SYM + w) * 8 + 8, :] = state[w]


def finish_kernel(
    tok_s, yad, ybc, feat, atab, zg, cst, pst, ycar, yrim, w_out,
    out,
    gad, gbc, mix, carry_g, wflip,
):
    nchunk = tok_s.shape[0] // CH
    for d in range(2):
        for u in range(SYM):
            at = slice((d * SYM + u) * 8, (d * SYM + u) * 8 + 8)
            carry_g[at, :] = ycar[at, :] * zg[u * 8 : u * 8 + 8, :]
    flip = jnp.where(iota((D, D), 0) + iota((D, D), 1) == D - 1, 1.0, 0.0).astype(BF16)
    wflip[...] = nn(w_out[...], flip).astype(BF16)
    unroll = 32
    held = 8
    mean = jnp.where(
        ((iota((2 * CH, CH), 0) & 127) >> 6) == (iota((2 * CH, CH), 1) >> 6), 1.0 / 64.0, 0.0
    ).astype(BF16)

    def advance(d, ref, first, n, decay, lead):
        local = n if d == 0 else CH - 1 - n
        u = tok_s[first + local]
        a = tile_at(atab, d * 64 + u * 8)
        if lead is not None:
            a = jnp.where(lead, 1.0, a)
        decay = decay * a
        part = tile_at(ref, (first + local) * 8) * tile_at(zg, u * 8)
        return decay, local, part + decay * tile_at(carry_g, d * SYM * 8 + u * 8)

    def chunk(step, _):
        first = step * CH

        def group(g, carry):
            pa, pb = carry
            for begin in range(0, unroll, held):
                done = []
                for i in range(begin, begin + held):
                    n = g * unroll + i
                    lead0 = (g == 0) & (step == 0) if i < 3 else None
                    lead1 = (g == 0) & (step == nchunk - 1) if i < 3 else None
                    pa, at0, out0 = advance(0, yad, first, n, pa, lead0)
                    pb, at1, out1 = advance(1, ybc, first, n, pb, lead1)
                    done.append((at0, at1, out0, out1))
                for at0, at1, out0, out1 in done:
                    gad[pl.ds(pl.multiple_of(at0 * 8, 8), 8), :] = out0
                    gbc[pl.ds(pl.multiple_of(at1 * 8, 8), 8), :] = out1
            return pa, pb

        lax.fori_loop(
            0, CH // unroll, group, (tile_at(pst, step * 8), tile_at(pst, (nchunk + step) * 8))
        )

        @pl.when(step == 0)
        def _():
            for n in range(3):
                gad[n * 8 : n * 8 + 8, :] = yrim[n * 8 : n * 8 + 8, :] * tile_at(zg, tok_s[n] * 8)

        @pl.when(step == nchunk - 1)
        def _():
            for n in range(3):
                at = (CH - 1 - n) * 8
                gbc[at : at + 8, :] = yrim[24 + n * 8 : 32 + n * 8, :] * tile_at(
                    zg, tok_s[first + CH - 1 - n] * 8
                )

        normed = None
        for d, ref in ((0, gad), (1, gbc)):
            g = ref[...]
            high, low = split(g * g)
            meansq = nn(jnp.concatenate([high, low], axis=1), mean)
            scaled = (g * lax.rsqrt(meansq + EPSILON)).reshape(CH, 8, CH) * cst[
                16 + d * 8 : 24 + d * 8, :
            ][None]
            normed = scaled if normed is None else normed + scaled
        mix[...] = normed.reshape(CH * 8, CH)
        parts = [mix[pl.ds(i, CH, stride=8), :].astype(BF16) for i in range(8)]
        mine_out = nn(jnp.concatenate(parts[0:4], axis=1), w_out[...]).astype(BF16).astype(F32)
        other = nn(jnp.concatenate(parts[4:8], axis=1), wflip[...]).astype(BF16).astype(F32)
        at = pl.ds(pl.multiple_of(step * CH, CH), CH)
        out[at, :] = (feat[at, :].astype(F32) + mine_out + other).astype(BF16)
        return 0

    lax.fori_loop(0, nchunk, chunk, 0)


def per_device(
    token_ids,
    embed_table,
    input_weight_matrix,
    output_weight_matrix,
    conv_weight,
    dt_bias,
    decay_rate,
    skip_gain,
    norm_gain,
):
    length = token_ids.shape[0]
    nchunk = length // CH
    own = lax.axis_size("seq")
    tok2 = token_ids.reshape(nchunk, CH)
    rounds = own.bit_length() - 1
    rows = own * nchunk
    vm = pl.BlockSpec(memory_space=pltpu.VMEM)
    sm = pl.BlockSpec(memory_space=pltpu.SMEM)
    sds = jax.ShapeDtypeStruct
    mib = 1024 * 1024

    def exchanged(blocks, bit):
        route = [(i, i ^ (1 << bit)) for i in range(own)]
        return jnp.concatenate([blocks, lax.ppermute(blocks, "seq", route)], axis=0)

    def params(limit):
        return pltpu.CompilerParams(vmem_limit_bytes=limit * mib)

    def cost(flops, moved):
        return pl.CostEstimate(flops=flops, bytes_accessed=moved, transcendentals=0)

    blocks = exchanged(tok2, 0)
    table_shapes = (
        sds((2 * 64, CH), F32),
        sds((2 * SYM * 64, CH), F32),
        sds((64, CH), F32),
        sds((32, CH), F32),
        sds((2 * SYM * 16, CH), F32),
        sds((4, CH, E), BF16),
        sds((4 * SYM * CH, E), BF16),
        sds((4 * SYM * CH, E), BF16),
        sds((CH, D), BF16),
    )
    heads = jnp.concatenate([dt_bias, decay_rate, skip_gain], axis=0)
    pack = jnp.concatenate(
        [
            conv_weight.reshape(2 * KW, E),
            norm_gain,
            jnp.pad(heads, ((0, 0), (0, E - H))),
            jnp.pad(embed_table.astype(F32), ((0, 3), (0, E - D))),
        ],
        axis=0,
    )
    atab, gtab, zg, cst, lac, tw, xch, xcl, embk = pl.pallas_call(
        table_kernel,
        out_shape=table_shapes,
        in_specs=[vm] * 2,
        out_specs=[vm] * len(table_shapes),
        scratch_shapes=[pltpu.VMEM((16, D), F32)],
        compiler_params=params(20),
        cost_estimate=cost(1_000_000_000, 8_000_000),
        name="symbol_tables",
    )(pack, input_weight_matrix.T)
    blocks, tw, embk = lax.optimization_barrier((blocks, tw, embk))
    if rounds > 1:
        blocks = exchanged(blocks, 1)
    xad, xbc, feat = pl.pallas_call(
        conv_kernel,
        out_shape=(sds((length * 8, CH), F32), sds((length * 8, CH), F32), sds((length, D), BF16)),
        in_specs=[vm] * 3,
        out_specs=[vm] * 3,
        compiler_params=params(20),
        cost_estimate=cost(2_000_000_000, 9_000_000),
        name="convolve",
    )(tok2, tw, embk)
    blocks, xad, xbc = lax.optimization_barrier((blocks, xad, xbc))
    for bit in range(2, rounds):
        blocks = exchanged(blocks, bit)
    yad, ybc, pst = pl.pallas_call(
        scan_kernel,
        out_shape=(
            sds((length * 8, CH), F32),
            sds((length * 8, CH), F32),
            sds((2 * nchunk * 8, CH), F32),
        ),
        in_specs=[sm] + [vm] * 5,
        out_specs=[vm] * 3,
        input_output_aliases={4: 0, 5: 1},
        compiler_params=params(20),
        cost_estimate=cost(4_000_000_000, 16_000_000),
        name="scan_block",
    )(token_ids, atab, gtab, cst, xad, xbc)
    blocks, yad, ybc, pst = lax.optimization_barrier((blocks, yad, ybc, pst))
    mine = lax.axis_index("seq").reshape(1).astype(jnp.int32)
    ycar, yrim = pl.pallas_call(
        history_kernel,
        out_shape=(sds((2 * SYM * 8, CH), F32), sds((2 * 3 * 8, CH), F32)),
        in_specs=[sm, sm] + [vm] * 8,
        out_specs=[vm] * 2,
        scratch_shapes=[
            pltpu.VMEM((7, rows, CH), F32),
            pltpu.VMEM((2, rows, CH), F32),
            pltpu.VMEM((2, CH, 2 * CH), BF16),
            pltpu.VMEM((2, 160, CH), F32),
            pltpu.VMEM((2 * SYM * 8, CH), F32),
            pltpu.VMEM((2 * 3 * 8, CH), F32),
        ],
        compiler_params=params(20),
        cost_estimate=cost(2_000_000_000, 6_000_000),
        name="history",
    )(mine, token_ids, blocks, atab, gtab, cst, lac, tw, xch, xcl)
    return pl.pallas_call(
        finish_kernel,
        out_shape=sds((length, D), BF16),
        in_specs=[sm] + [vm] * 10,
        out_specs=vm,
        scratch_shapes=[pltpu.VMEM((CH * 8, CH), F32)] * 3 + [pltpu.VMEM((2 * SYM * 8, CH), F32), pltpu.VMEM((E, D), BF16)],
        compiler_params=params(20),
        cost_estimate=cost(4_000_000_000, 16_000_000),
        name="finish",
    )(
        token_ids, yad, ybc, feat, atab, zg, cst, pst, ycar, yrim, output_weight_matrix
    )


def solution(mesh):
    placed = (P(("batch", "seq")), P(), P(), P(), P(), P(), P(), P(), P())
    return jax.shard_map(
        per_device, mesh=mesh, in_specs=placed, out_specs=P(("batch", "seq"), None), check_vma=False
    )
```

```python
import functools

import jax
import jax.numpy as jnp
from jax import lax
from jax.experimental import pallas as pl
from jax.experimental.pallas import tpu as pltpu
from jax.sharding import PartitionSpec as P

D = 256
E = 512
NS = 16
H = 8
KW = 4
SYM = 5
LOG2E = 1.4426950408889634
EPSILON = 1e-05
CH = 128
SUB = 16

F32 = jnp.float32
BF16 = jnp.bfloat16

CHAINS = ((0, 0, 0), (0, 1, 1), (1, 0, 1), (1, 1, 0))


def iota(shape, dim):
    return lax.broadcasted_iota(jnp.int32, shape, dim)


def nn(a, b, **kw):
    return lax.dot_general(a, b, (((1,), (0,)), ((), ())), preferred_element_type=F32, **kw)


def nt(a, b, **kw):
    return lax.dot_general(a, b, (((1,), (1,)), ((), ())), preferred_element_type=F32, **kw)


def split(value):
    high = value.astype(BF16)
    low = (value - high.astype(F32)).astype(BF16)
    return high, low


def softplus(x):
    return jnp.maximum(x, 0.0) + jnp.log1p(jnp.exp(-jnp.abs(x)))


def silu_half(half):
    return half + half * jnp.tanh(half)


def tap_row(direction, j):
    return j if direction == 0 else 2 * (KW - 1) - j


def window_onehot(rows):
    sub = iota((8, CH), 0).astype(F32)
    blocks = [jnp.where(row == sub, 1.0, 0.0) for row in rows]
    blocks.append(jnp.zeros((8, CH), F32))
    stacked = jnp.concatenate(blocks + blocks, axis=0)
    return stacked.T.astype(BF16)


def shifted(tok, offset, rows):
    if offset == 0:
        return tok
    lane = iota((rows, CH), 1)
    row = iota((rows, CH), 0)
    moved = pltpu.roll(tok, (-offset) % CH, 1)
    if offset < 0:
        other = pltpu.roll(moved, 1, 0)
        crossing = lane < -offset
        outside = crossing & (row == 0)
    else:
        other = pltpu.roll(moved, rows - 1, 0)
        crossing = lane >= CH - offset
        outside = crossing & (row == rows - 1)
    return jnp.where(outside, 5.0, jnp.where(crossing, other, moved))


def pick(values, u):
    low = (u & 1) == 1
    first = jnp.where(low, values[1], values[0])
    second = jnp.where(low, values[3], values[2])
    return jnp.where(u > 3, values[4], jnp.where((u & 2) == 2, second, first))


def tile_at(ref, row):
    return ref[pl.ds(pl.multiple_of(row, 8), 8), :]


def fetch(sources, targets, sems):
    copies = [
        pltpu.make_async_copy(a, b, sems.at[i]) for i, (a, b) in enumerate(zip(sources, targets))
    ]
    for copy in copies:
        copy.start()
    for copy in copies:
        copy.wait()


def symbol_tables(
    directions, full, emb, w_in, cw, bias, rate, skip, gain, emb16, atab, gtab, cst, tw
):
    highest = lax.Precision.HIGHEST
    emb16[...] = jnp.zeros_like(emb16)
    e32 = emb[...].astype(F32)
    emb16[0:SYM, :] = e32
    for v in range(4):
        emb16[8 + v : 9 + v, :] = e32[3 - v : 4 - v, :]
    emb16[12:13, :] = e32[4:5, :]
    embs = emb16[...].astype(BF16)
    x16 = nt(embs, w_in[E : 2 * E, :]).astype(BF16).astype(F32)
    rest = nt(embs, w_in[2 * E :, :]).astype(BF16)
    nrest = 2 * NS + H
    expand = jnp.where(
        iota((nrest, E), 0) == (iota((nrest, E), 1) >> 6) + 2 * NS, 1.0, 0.0
    ).astype(BF16)
    heads = jnp.where(iota((H, E), 0) == (iota((H, E), 1) >> 6), 1.0, 0.0)
    r_exp = nn(rest, expand)
    bias_e = nn(bias[...], heads, precision=highest)
    rate_e = nn(rate[...], heads, precision=highest)
    skip_e = nn(skip[...], heads, precision=highest)
    shift = jnp.where(
        iota((nrest, nrest), 0) + NS == iota((nrest, nrest), 1),
        jnp.where(iota((nrest, nrest), 0) < NS, 1.0, 0.0),
        0.0,
    ).astype(BF16)
    rest_b = nn(rest, shift).astype(BF16)
    cb = nt(rest_b, rest)
    if full is not None:
        zg, lac, xch, xcl = full
        z16 = nt(embs, w_in[0:E, :]).astype(BF16).astype(F32)
        sz = z16 * (0.5 + 0.5 * jnp.tanh(0.5 * z16))
        for s in range(2):
            for i in range(4):
                zg[pl.ds(s * 4 + i, 8, stride=8), :] = sz[8 * s : 8 * s + 8, 128 * i : 128 * i + 128]
        pick_r = jnp.where(
            iota((H, nrest), 0) + 2 * NS == iota((H, nrest), 1), 1.0, 0.0
        ).astype(BF16)
        r_t = nt(pick_r, rest)
        eye = jnp.where(iota((H, H), 0) == iota((H, H), 1), 1.0, 0.0)
        bias_t = nt(eye, bias[...], precision=highest)
        rate_t = nt(eye, rate[...], precision=highest)
    for q, (d, s, k) in enumerate(CHAINS):
        if d not in directions:
            continue
        dt = softplus(r_exp[8 * s : 8 * s + 8, :] + bias_e[k : k + 1, :])
        a = jnp.exp(-rate_e[k : k + 1, :] * dt)
        for i in range(4):
            lanes = slice(128 * i, 128 * i + 128)
            atab[pl.ds(d * 64 + s * 4 + i, 8, stride=8), :] = a[:, lanes]
            cst[d * 8 + s * 4 + i : d * 8 + s * 4 + i + 1, :] = skip_e[k : k + 1, lanes]
            cst[16 + d * 8 + s * 4 + i : 17 + d * 8 + s * 4 + i, :] = gain[k : k + 1, lanes]
        for u in range(SYM):
            g = cb[8 * s : 8 * s + 8, 8 * s + u : 8 * s + u + 1] * dt
            for i in range(4):
                gtab[pl.ds((d * SYM + u) * 64 + s * 4 + i, 8, stride=8), :] = g[
                    :, 128 * i : 128 * i + 128
                ]
        xs = x16[8 * s : 8 * s + 8, :]
        blocks = [jnp.zeros((8, E), F32)] * 8
        for j in range(KW):
            blocks[tap_row(d, j)] = (0.5 * cw[k, j : j + 1, :]) * xs
        high, low = split(jnp.concatenate(blocks, axis=0))
        tw[q, 0:64, :] = high
        tw[q, 64:128, :] = low
        if full is None:
            continue
        la = (
            -rate_t[:, k : k + 1] * softplus(r_t[:, 8 * s : 8 * s + 8] + bias_t[:, k : k + 1])
        ) * LOG2E
        for v in range(SYM):
            lac[(d * SYM + v) * 16 + s * 8 : (d * SYM + v) * 16 + s * 8 + 8, :] = jnp.broadcast_to(
                la[:, v : v + 1], (8, CH)
            )
        code = iota((CH, CH), 0).astype(F32)
        lane = iota((CH, CH), 1) & 63
        slot = lane >> 3
        sym = (lane & 7).astype(F32)
        d0 = jnp.floor((code + 0.5) * (1.0 / 25.0))
        d01 = jnp.floor((code + 0.5) * (1.0 / 5.0))
        digits = (d0, d01 - 5.0 * d0, code - 5.0 * d01)
        hot = jnp.zeros((CH, CH), F32)
        for j in range(KW - 1):
            hot = jnp.where(
                slot == tap_row(d, j), jnp.where(sym == digits[j], 1.0, 0.0), hot
            )
        partial = nn(hot.astype(BF16), tw[q])
        last = blocks[tap_row(d, KW - 1)]
        for v in range(SYM):
            high, low = split(silu_half(partial + last[v : v + 1, :]))
            xch[(q * SYM + v) * CH : (q * SYM + v + 1) * CH, :] = high
            xcl[(q * SYM + v) * CH : (q * SYM + v + 1) * CH, :] = low


def direction_kernel(
    direction, tok_s, tok_v, emb_h, w_in_h, cw_h, bias_h, rate_h, skip_h, gain_h,
    y_h, pst,
    emb, w_in, cw, bias, rate, skip, gain, emb16, atab, gtab, cst, tw, x_v, y_v, sems, y_sems,
):
    total = tok_s.shape[0]
    nchunk = total // CH
    fetch((emb_h, w_in_h, cw_h, bias_h, rate_h, skip_h, gain_h),
          (emb, w_in, cw, bias, rate, skip, gain), sems)
    symbol_tables(
        (direction,), None, emb, w_in, cw, bias, rate, skip, gain, emb16, atab, gtab, cst, tw
    )
    tok = tok_v[...].astype(F32)
    shifts = [shifted(tok, o, nchunk) for o in range(1 - KW, KW)]
    for c in range(nchunk):
        hot = window_onehot([sh[c : c + 1, :] for sh in shifts])
        for s in range(2):
            x = silu_half(nn(hot, tw[2 * direction + s]))
            for i in range(4):
                x_v[pl.ds(c * 8 * CH + s * 4 + i, CH, stride=8), :] = x[:, 128 * i : 128 * i + 128]
    rim = (KW - 1) * 8
    if direction == 0:
        x_v[0:rim, :] = jnp.zeros((rim, CH), F32)
    else:
        x_v[total * 8 - rim : total * 8, :] = jnp.zeros((rim, CH), F32)

    skip_t = cst[8 * direction : 8 * direction + 8, :]
    unroll = 32
    held = 8

    def group(g, carry):
        state, decay = list(carry[0]), carry[1]
        for begin in range(0, unroll, held):
            done = []
            for i in range(begin, begin + held):
                n = g * unroll + i
                t = n if direction == 0 else total - 1 - n
                if i % SUB == 0:
                    first = n if direction == 0 else t - SUB + 1
                    pst[pl.ds(pl.multiple_of((first // SUB) * 8, 8), 8), :] = decay
                u = tok_s[t]
                x = tile_at(x_v, t * 8)
                a = tile_at(atab, direction * 64 + u * 8)
                state = [
                    a * state[w] + tile_at(gtab, (direction * SYM + w) * 64 + u * 8) * x
                    for w in range(SYM)
                ]
                done.append((t, pick(state, u) + skip_t * x))
                if i < KW - 1:
                    a = jnp.where(g == 0, 1.0, a)
                decay = decay * a
            for t, y in done:
                y_v[pl.ds(pl.multiple_of(t * 8, 8), 8), :] = y
        return tuple(state), decay

    def stream(c):
        at = c if direction == 0 else nchunk - 1 - c
        rows = pl.ds(pl.multiple_of(at * (CH * 8), CH * 8), CH * 8)
        return pltpu.make_async_copy(y_v.at[rows, :], y_h.at[rows, :], y_sems.at[c])

    def chunk(c, carry):
        per = CH // unroll
        carry = lax.fori_loop(c * per, (c + 1) * per, group, carry)
        stream(c).start()
        return carry

    zero = jnp.zeros((8, CH), F32)
    lax.fori_loop(0, nchunk, chunk, ((zero,) * SYM, jnp.ones((8, CH), F32)))
    for c in range(nchunk):
        stream(c).wait()


def last_kernel(
    mine, tok_s, near, far, yad_h, ybc_h, psta, pstb,
    emb_h, w_in_h, cw_h, bias_h, rate_h, skip_h, gain_h, w_out_h,
    out,
    emb, w_in, cw, bias, rate, skip, gain, w_out, emb16, atab, gtab, cst, tw, zg, lac, xch, xcl,
    tok_x, tok_f, code, tri, hist, svec, xrim, ycar, yrim, carry_g, yad, ybc, mix, sems, y_sems,
):
    half = near.shape[0]
    rows = 2 * half
    own = rows // 8
    nchunk = tok_s.shape[0] // CH
    j = mine[0]

    def incoming(d, c):
        at = pl.ds(pl.multiple_of(c * (CH * 8), CH * 8), CH * 8)
        source, target = ((yad_h, yad), (ybc_h, ybc))[d]
        return pltpu.make_async_copy(source.at[at, :], target.at[at, :], y_sems.at[d, c])

    fetch((emb_h, w_in_h, cw_h, bias_h, rate_h, skip_h, gain_h, w_out_h),
          (emb, w_in, cw, bias, rate, skip, gain, w_out), sems)
    for c in range(nchunk):
        for d in range(2):
            incoming(d, c).start()
    symbol_tables(
        (0, 1), (zg, lac, xch, xcl),
        emb, w_in, cw, bias, rate, skip, gain, emb16, atab, gtab, cst, tw,
    )
    tok_x[0:half, :] = near[...]
    tok_x[half:rows, :] = far[...]
    for b in range(own):
        slot = (j ^ b) * 8
        tok_f[3, 8 * b : 8 * b + 8, :] = tok_x[pl.ds(pl.multiple_of(slot, 8), 8), :].astype(F32)
    tok = tok_f[3]
    for o in (-3, -2, -1, 1, 2, 3):
        tok_f[3 + o] = shifted(tok, o, rows)
    lane = iota((rows, CH), 1)
    row = iota((rows, CH), 0)
    lane_f = lane.astype(F32)
    before = 25.0 * tok_f[0] + 5.0 * tok_f[1] + tok_f[2]
    after = 25.0 * tok_f[6] + 5.0 * tok_f[5] + tok_f[4]
    code[0] = jnp.where((row == 0) & (lane < 3), 125.0 + lane_f, before)
    code[1] = jnp.where((row == rows - 1) & (lane >= CH - 3), lane_f, after)
    si = iota((CH, CH), 0)
    ri = iota((CH, CH), 1)
    ones = jnp.ones((CH, CH), F32)
    tri[0] = jnp.concatenate([jnp.where(si > ri, 1.0, 0.0), ones], axis=1).astype(BF16)
    tri[1] = jnp.concatenate([jnp.where(si < ri, 1.0, 0.0), ones], axis=1).astype(BF16)
    hist[...] = jnp.zeros_like(hist)
    sub8 = iota((8, CH), 0).astype(F32)
    subc = iota((CH, CH), 0).astype(F32)

    def block(b, off):
        side = jnp.where(b >= j, 1, 0)
        index = jnp.where(b >= j, b + 1, j - 1 - b)
        off = off * jnp.where(b == j, 0.0, 1.0)
        use_prefix = side.astype(F32)
        at = pl.ds(pl.multiple_of(index * 8, 8), 8)
        tk = tok_f[3, at, :]
        cd = code[side, at, :]
        hots = [jnp.where(tk[m : m + 1, :] == sub8, 1.0, 0.0) for m in range(8)]
        counts = nn(jnp.concatenate(hots, axis=0).astype(BF16), tri[side])
        totals = [counts[8 * m : 8 * m + 8, CH:] for m in range(8)]
        prefix = [jnp.zeros((8, CH), F32)]
        for m in range(8):
            prefix.append(prefix[-1] + totals[m])
        las = [lac[pl.ds(pl.multiple_of((side * SYM + v) * 16, 16), 16), :] for v in range(SYM)]
        acc = jnp.zeros((160, CH), F32)
        for pair in range(4):
            lefts, rights = [], []
            for m in (2 * pair, 2 * pair + 1):
                suffix = prefix[8] - prefix[m + 1]
                inside = suffix + use_prefix * (prefix[m] - suffix)
                count = counts[8 * m : 8 * m + 8, :CH] + off + inside
                exponent = las[0] * count[0:1, :]
                for v in range(1, SYM):
                    exponent = exponent + las[v] * count[v : v + 1, :]
                weight = jnp.exp2(exponent)
                masked = jnp.concatenate(
                    [jnp.where(tk[m : m + 1, :] == float(v), weight, 0.0) for v in range(SYM)],
                    axis=0,
                )
                high, low = split(masked)
                lefts.append(jnp.concatenate([high, low], axis=0))
                rights.append(jnp.where(cd[m : m + 1, :] == subc, 1.0, 0.0).astype(BF16))
            acc = acc + nt(
                jnp.concatenate(lefts, axis=1), jnp.concatenate(rights, axis=1)
            )
        hist[side] = hist[side] + acc
        return off + prefix[8]

    lax.fori_loop(0, own - 1, block, jnp.zeros((8, CH), F32))

    last8 = rows - 8
    mine8 = pl.ds(pl.multiple_of(j * 8, 8), 8)
    xs = {}
    for d in range(2):
        edge = 0 if d == 0 else 7
        seq_at = pl.ds(0 if d == 0 else last8, 8)
        hot_seq = window_onehot([tok_f[o, seq_at, :][edge : edge + 1, :] for o in range(7)])
        hot_own = window_onehot([tok_f[o, mine8, :][edge : edge + 1, :] for o in range(7)])
        for s in range(2):
            q = 2 * d + s
            xseq = silu_half(nn(hot_seq, tw[q]))
            xown = silu_half(nn(hot_own, tw[q]))
            if d == 0:
                xs[q] = pltpu.roll(xseq[0:8, :], 5, 0)
            else:
                xs[q] = xseq[CH - 8 :, :]
            for n in range(KW - 1):
                t = n if d == 0 else CH - 1 - n
                for i in range(4):
                    at = (d * 3 + n) * 8 + s * 4 + i
                    xrim[at : at + 1, :] = xown[t : t + 1, 128 * i : 128 * i + 128]
    diag = iota((H, E), 0) == (iota((H, E), 1) >> 6)
    sub16 = iota((16, E), 0)
    for q in range(4):
        d, s = q // 2, q % 2
        rim = jnp.concatenate([jnp.zeros((8, E), F32), xs[q]], axis=0)
        rim_h, rim_l = split(rim)
        for v in range(SYM):
            start = (q * SYM + v) * CH
            body = slice(start, start + CH - 16)
            tail = slice(start + CH - 16, start + CH)
            tail_h = jnp.where(sub16 >= 13, rim_h.astype(F32), xch[tail, :].astype(F32))
            tail_l = jnp.where(sub16 >= 13, rim_l.astype(F32), xcl[tail, :].astype(F32))
            table_h = jnp.concatenate([xch[body, :], tail_h.astype(BF16)], axis=0)
            table_l = jnp.concatenate([xcl[body, :], tail_l.astype(BF16)], axis=0)
            at = v * 16 + s * 8
            w = hist[d, at : at + 8, :] + hist[d, 80 + at : 88 + at, :]
            high, low = split(w)
            both = jnp.concatenate([high.astype(F32), low.astype(F32)], axis=0).astype(BF16)
            one = nn(both, table_h)
            two = nn(both, table_l)
            full = one[0:8, :] + one[8:16, :] + two[0:8, :]
            vec = jnp.sum(jnp.where(diag, full, 0.0), axis=0, keepdims=True)
            for i in range(4):
                at = (d * SYM + v) * 8 + s * 4 + i
                svec[at : at + 1, :] = vec[:, 128 * i : 128 * i + 128]
    total = tok_s.shape[0]
    for d in range(2):
        state = []
        for w in range(SYM):
            value = jnp.zeros((8, CH), F32)
            for v in range(SYM):
                at = (d * SYM + w) * 64 + v * 8
                sat = (d * SYM + v) * 8
                value = value + gtab[at : at + 8, :] * svec[sat : sat + 8, :]
            state.append(value)
        skip_t = cst[d * 8 : d * 8 + 8, :]
        for n in range(KW - 1):
            u = tok_s[n if d == 0 else total - 1 - n]
            x = xrim[(d * 3 + n) * 8 : (d * 3 + n) * 8 + 8, :]
            a = tile_at(atab, d * 64 + u * 8)
            state = [
                a * state[w] + tile_at(gtab, (d * SYM + w) * 64 + u * 8) * x
                for w in range(SYM)
            ]
            yrim[(d * 3 + n) * 8 : (d * 3 + n) * 8 + 8, :] = pick(state, u) + skip_t * x
        for w in range(SYM):
            ycar[(d * SYM + w) * 8 : (d * SYM + w) * 8 + 8, :] = state[w]

    for d in range(2):
        for u in range(SYM):
            at = slice((d * SYM + u) * 8, (d * SYM + u) * 8 + 8)
            carry_g[at, :] = ycar[at, :] * zg[u * 8 : u * 8 + 8, :]
    for d in range(2):
        for n in range(KW - 1):
            t = n if d == 0 else nchunk * CH - 1 - n
            at = slice((d * 3 + n) * 8, (d * 3 + n) * 8 + 8)
            yrim[at, :] = yrim[at, :] * tile_at(zg, tok_s[t] * 8)
    flip = jnp.where(iota((D, D), 0) + iota((D, D), 1) == D - 1, 1.0, 0.0).astype(BF16)
    wout = w_out[...]
    wflip = nn(wout, flip).astype(BF16)
    mean = jnp.where(
        (iota((2 * CH, 2 * CH), 0) >> 6) == (iota((2 * CH, 2 * CH), 1) >> 6), 1.0 / 64.0, 0.0
    ).astype(BF16)
    emb_rows = jnp.concatenate(
        [emb16[0:8, :], jnp.zeros((CH - 8, D), F32)], axis=0
    ).astype(BF16)
    gains = (cst[16:24, :], cst[24:32, :])
    sub = iota((8, CH), 0).astype(F32)
    mix[...] = jnp.zeros_like(mix)
    tiles = CH // SUB

    def project(c):
        base = (c & 1) * (CH * 8)
        row = tok_f[3, pl.ds(j * 8 + c, 1), :]
        hot = jnp.concatenate(
            [jnp.where(row == sub, 1.0, 0.0), jnp.zeros((CH - 8, CH), F32)], axis=0
        ).T.astype(BF16)
        parts = [mix[pl.ds(base + i, CH, stride=8), :].astype(BF16) for i in range(8)]
        one = nn(jnp.concatenate(parts[0:4], axis=1), wout).astype(BF16).astype(F32)
        two = nn(jnp.concatenate(parts[4:8], axis=1), wflip).astype(BF16).astype(F32)
        out[pl.ds(pl.multiple_of(c * CH, CH), CH), :] = (nn(hot, emb_rows) + one + two).astype(BF16)

    def tile(c, k):
        base = c * CH + k * SUB
        found = []
        for d, ref, pst in ((0, yad, psta), (1, ybc, pstb)):
            decay = tile_at(pst, (c * tiles + k) * 8)
            edge = c == (0 if d == 0 else nchunk - 1)
            values = [None] * SUB
            for n in range(SUB):
                local = n if d == 0 else SUB - 1 - n
                u = tok_s[base + local]
                a = tile_at(atab, d * 64 + u * 8)
                rim = n < KW - 1 and k == (0 if d == 0 else tiles - 1)
                if rim:
                    a = jnp.where(edge, 1.0, a)
                decay = decay * a
                g = tile_at(ref, (base + local) * 8) * tile_at(zg, u * 8) + decay * tile_at(
                    carry_g, d * SYM * 8 + u * 8
                )
                if rim:
                    at = slice((d * 3 + n) * 8, (d * 3 + n) * 8 + 8)
                    g = jnp.where(edge, yrim[at, :], g)
                values[local] = g
            found.append(jnp.concatenate(values, axis=0))
        high, low = split(jnp.concatenate([g * g for g in found], axis=1))
        scale = lax.rsqrt(nn(high, mean) + nn(low, mean) + EPSILON)
        normed = None
        for d in range(2):
            scaled = (found[d] * scale[:, CH * d : CH * d + CH]).reshape(SUB, 8, CH) * gains[d][None]
            normed = scaled if normed is None else normed + scaled
        at = (c & 1) * (CH * 8) + k * SUB * 8
        mix[pl.ds(pl.multiple_of(at, 8), SUB * 8), :] = normed.reshape(SUB * 8, CH)

    def chunk(c, _):
        for d in range(2):
            incoming(d, c).wait()
        project(jnp.maximum(c - 1, 0))
        for k in range(tiles):
            tile(c, k)
        return 0

    lax.fori_loop(0, nchunk, chunk, 0)
    project(nchunk - 1)


def per_device(
    token_ids,
    embed_table,
    input_weight_matrix,
    output_weight_matrix,
    conv_weight,
    dt_bias,
    decay_rate,
    skip_gain,
    norm_gain,
):
    length = token_ids.shape[0]
    nchunk = length // CH
    own = lax.axis_size("seq")
    tok2 = token_ids.reshape(nchunk, CH)
    rounds = own.bit_length() - 1
    rows = own * nchunk
    vm = pl.BlockSpec(memory_space=pltpu.VMEM)
    sm = pl.BlockSpec(memory_space=pltpu.SMEM)
    hbm = pl.BlockSpec(memory_space=pl.ANY)
    sds = jax.ShapeDtypeStruct
    limit = pltpu.CompilerParams(vmem_limit_bytes=56 * 1024 * 1024)
    weights = (
        embed_table, input_weight_matrix.T, conv_weight, dt_bias, decay_rate, skip_gain, norm_gain,
    )
    dma = pltpu.SemaphoreType.DMA
    table_scratch = [
        pltpu.VMEM((16, D), F32),
        pltpu.VMEM((2 * 64, CH), F32),
        pltpu.VMEM((2 * SYM * 64, CH), F32),
        pltpu.VMEM((32, CH), F32),
        pltpu.VMEM((4, CH, E), BF16),
    ]

    def sent(blocks, bit):
        return lax.ppermute(blocks, "seq", [(i, i ^ (1 << bit)) for i in range(own)])

    def chains(direction):
        return pl.pallas_call(
            functools.partial(direction_kernel, direction),
            out_shape=(sds((length * 8, CH), F32), sds((length // SUB * 8, CH), F32)),
            in_specs=[sm, vm] + [hbm] * 7,
            out_specs=(hbm, vm),
            scratch_shapes=[pltpu.VMEM(w.shape, w.dtype) for w in weights]
            + table_scratch
            + [pltpu.VMEM((length * 8, CH), F32)] * 2
            + [dma((7,)), dma((nchunk,))],
            compiler_params=limit,
            cost_estimate=pl.CostEstimate(
                flops=3_000_000_000, bytes_accessed=16_000_000, transcendentals=0
            ),
            name=("increasing", "decreasing")[direction],
        )(token_ids, tok2, *weights)

    near, far = tok2, sent(tok2, 0)
    if rounds > 1:
        near = jnp.concatenate([near, far], axis=0)
        far = sent(near, 1)
    yad, psta = chains(0)
    near, far, yad, psta = lax.optimization_barrier((near, far, yad, psta))
    for bit in range(2, rounds):
        near = jnp.concatenate([near, far], axis=0)
        far = sent(near, bit)
    ybc, pstb = chains(1)
    near, far, yad, ybc = lax.optimization_barrier((near, far, yad, ybc))
    mine = lax.axis_index("seq").reshape(1).astype(jnp.int32)
    big = pltpu.VMEM((4 * SYM * CH, E), BF16)
    return pl.pallas_call(
        last_kernel,
        out_shape=sds((length, D), BF16),
        in_specs=[sm, sm, vm, vm, hbm, hbm, vm, vm] + [hbm] * 8,
        out_specs=vm,
        scratch_shapes=[pltpu.VMEM(w.shape, w.dtype) for w in weights]
        + [pltpu.VMEM((E, D), BF16)]
        + table_scratch
        + [
            pltpu.VMEM((64, CH), F32),
            pltpu.VMEM((2 * SYM * 16, CH), F32),
            big,
            big,
            pltpu.VMEM((rows, CH), jnp.int32),
            pltpu.VMEM((7, rows, CH), F32),
            pltpu.VMEM((2, rows, CH), F32),
            pltpu.VMEM((2, CH, 2 * CH), BF16),
            pltpu.VMEM((2, 160, CH), F32),
            pltpu.VMEM((2 * SYM * 8, CH), F32),
            pltpu.VMEM((2 * 3 * 8, CH), F32),
            pltpu.VMEM((2 * SYM * 8, CH), F32),
            pltpu.VMEM((2 * 3 * 8, CH), F32),
            pltpu.VMEM((2 * SYM * 8, CH), F32),
            pltpu.VMEM((length * 8, CH), F32),
            pltpu.VMEM((length * 8, CH), F32),
            pltpu.VMEM((2 * CH * 8, CH), F32),
            dma((8,)),
            dma((2, nchunk)),
        ],
        compiler_params=limit,
        cost_estimate=pl.CostEstimate(
            flops=6_000_000_000, bytes_accessed=16_000_000, transcendentals=0
        ),
        name="history_finish",
    )(mine, token_ids, near, far, yad, ybc, psta, pstb, *weights, output_weight_matrix)


def solution(mesh):
    placed = (P(("batch", "seq")), P(), P(), P(), P(), P(), P(), P(), P())
    return jax.shard_map(
        per_device, mesh=mesh, in_specs=placed, out_specs=P(("batch", "seq"), None), check_vma=False
    )
```

```python
import functools

import jax
import jax.numpy as jnp
from jax import lax
from jax.experimental import pallas as pl
from jax.experimental.pallas import tpu as pltpu
from jax.sharding import PartitionSpec as P

D = 256
E = 512
NS = 16
H = 8
KW = 4
SYM = 5
LOG2E = 1.4426950408889634
EPSILON = 1e-05
CH = 128
SUB = 16

F32 = jnp.float32
BF16 = jnp.bfloat16

CHAINS = ((0, 0, 0), (0, 1, 1), (1, 0, 1), (1, 1, 0))


def iota(shape, dim):
    return lax.broadcasted_iota(jnp.int32, shape, dim)


def nn(a, b, **kw):
    return lax.dot_general(a, b, (((1,), (0,)), ((), ())), preferred_element_type=F32, **kw)


def nt(a, b, **kw):
    return lax.dot_general(a, b, (((1,), (1,)), ((), ())), preferred_element_type=F32, **kw)


def split(value):
    high = value.astype(BF16)
    low = (value - high.astype(F32)).astype(BF16)
    return high, low


def softplus(x):
    return jnp.maximum(x, 0.0) + jnp.log1p(jnp.exp(-jnp.abs(x)))


def silu_half(half):
    return half + half * jnp.tanh(half)


def tap_row(direction, j):
    return j if direction == 0 else 2 * (KW - 1) - j


def window_onehot(rows):
    sub = iota((8, CH), 0).astype(F32)
    blocks = [jnp.where(row == sub, 1.0, 0.0) for row in rows]
    blocks.append(jnp.zeros((8, CH), F32))
    stacked = jnp.concatenate(blocks + blocks, axis=0)
    return stacked.T.astype(BF16)


def shifted(tok, offset, rows):
    if offset == 0:
        return tok
    lane = iota((rows, CH), 1)
    row = iota((rows, CH), 0)
    moved = pltpu.roll(tok, (-offset) % CH, 1)
    if offset < 0:
        other = pltpu.roll(moved, 1, 0)
        crossing = lane < -offset
        outside = crossing & (row == 0)
    else:
        other = pltpu.roll(moved, rows - 1, 0)
        crossing = lane >= CH - offset
        outside = crossing & (row == rows - 1)
    return jnp.where(outside, 5.0, jnp.where(crossing, other, moved))


def pick(values, u):
    low = (u & 1) == 1
    first = jnp.where(low, values[1], values[0])
    second = jnp.where(low, values[3], values[2])
    return jnp.where(u > 3, values[4], jnp.where((u & 2) == 2, second, first))


def tile_at(ref, row):
    return ref[pl.ds(pl.multiple_of(row, 8), 8), :]


def fetch(sources, targets, sems):
    copies = [
        pltpu.make_async_copy(a, b, sems.at[i]) for i, (a, b) in enumerate(zip(sources, targets))
    ]
    for copy in copies:
        copy.start()
    for copy in copies:
        copy.wait()


def symbol_tables(
    directions, full, emb, w_in, cw, bias, rate, skip, gain, emb16, atab, gtab, cst, tw
):
    highest = lax.Precision.HIGHEST
    emb16[...] = jnp.zeros_like(emb16)
    e32 = emb[...].astype(F32)
    emb16[0:SYM, :] = e32
    for v in range(4):
        emb16[8 + v : 9 + v, :] = e32[3 - v : 4 - v, :]
    emb16[12:13, :] = e32[4:5, :]
    embs = emb16[...].astype(BF16)
    x16 = nt(embs, w_in[E : 2 * E, :]).astype(BF16).astype(F32)
    rest = nt(embs, w_in[2 * E :, :]).astype(BF16)
    nrest = 2 * NS + H
    expand = jnp.where(
        iota((nrest, E), 0) == (iota((nrest, E), 1) >> 6) + 2 * NS, 1.0, 0.0
    ).astype(BF16)
    heads = jnp.where(iota((H, E), 0) == (iota((H, E), 1) >> 6), 1.0, 0.0)
    r_exp = nn(rest, expand)
    bias_e = nn(bias[...], heads, precision=highest)
    rate_e = nn(rate[...], heads, precision=highest)
    skip_e = nn(skip[...], heads, precision=highest)
    shift = jnp.where(
        iota((nrest, nrest), 0) + NS == iota((nrest, nrest), 1),
        jnp.where(iota((nrest, nrest), 0) < NS, 1.0, 0.0),
        0.0,
    ).astype(BF16)
    rest_b = nn(rest, shift).astype(BF16)
    cb = nt(rest_b, rest)
    if full is not None:
        zg, lac, xch, xcl = full
        z16 = nt(embs, w_in[0:E, :]).astype(BF16).astype(F32)
        sz = z16 * (0.5 + 0.5 * jnp.tanh(0.5 * z16))
        for s in range(2):
            for i in range(4):
                zg[pl.ds(s * 4 + i, 8, stride=8), :] = sz[8 * s : 8 * s + 8, 128 * i : 128 * i + 128]
        pick_r = jnp.where(
            iota((H, nrest), 0) + 2 * NS == iota((H, nrest), 1), 1.0, 0.0
        ).astype(BF16)
        r_t = nt(pick_r, rest)
        eye = jnp.where(iota((H, H), 0) == iota((H, H), 1), 1.0, 0.0)
        bias_t = nt(eye, bias[...], precision=highest)
        rate_t = nt(eye, rate[...], precision=highest)
    for q, (d, s, k) in enumerate(CHAINS):
        if d not in directions:
            continue
        dt = softplus(r_exp[8 * s : 8 * s + 8, :] + bias_e[k : k + 1, :])
        a = jnp.exp(-rate_e[k : k + 1, :] * dt)
        for i in range(4):
            lanes = slice(128 * i, 128 * i + 128)
            atab[pl.ds(d * 64 + s * 4 + i, 8, stride=8), :] = a[:, lanes]
            cst[d * 8 + s * 4 + i : d * 8 + s * 4 + i + 1, :] = skip_e[k : k + 1, lanes]
            cst[16 + d * 8 + s * 4 + i : 17 + d * 8 + s * 4 + i, :] = gain[k : k + 1, lanes]
        for u in range(SYM):
            g = cb[8 * s : 8 * s + 8, 8 * s + u : 8 * s + u + 1] * dt
            for i in range(4):
                gtab[pl.ds((d * SYM + u) * 64 + s * 4 + i, 8, stride=8), :] = g[
                    :, 128 * i : 128 * i + 128
                ]
        xs = x16[8 * s : 8 * s + 8, :]
        blocks = [jnp.zeros((8, E), F32)] * 8
        for j in range(KW):
            blocks[tap_row(d, j)] = (0.5 * cw[k, j : j + 1, :]) * xs
        high, low = split(jnp.concatenate(blocks, axis=0))
        tw[q, 0:64, :] = high
        tw[q, 64:128, :] = low
        if full is None:
            continue
        la = (
            -rate_t[:, k : k + 1] * softplus(r_t[:, 8 * s : 8 * s + 8] + bias_t[:, k : k + 1])
        ) * LOG2E
        for v in range(SYM):
            lac[(d * SYM + v) * 16 + s * 8 : (d * SYM + v) * 16 + s * 8 + 8, :] = jnp.broadcast_to(
                la[:, v : v + 1], (8, CH)
            )
        code = iota((CH, CH), 0).astype(F32)
        lane = iota((CH, CH), 1) & 63
        slot = lane >> 3
        sym = (lane & 7).astype(F32)
        d0 = jnp.floor((code + 0.5) * (1.0 / 25.0))
        d01 = jnp.floor((code + 0.5) * (1.0 / 5.0))
        digits = (d0, d01 - 5.0 * d0, code - 5.0 * d01)
        hot = jnp.zeros((CH, CH), F32)
        for j in range(KW - 1):
            hot = jnp.where(
                slot == tap_row(d, j), jnp.where(sym == digits[j], 1.0, 0.0), hot
            )
        partial = nn(hot.astype(BF16), tw[q])
        last = blocks[tap_row(d, KW - 1)]
        for v in range(SYM):
            high, low = split(silu_half(partial + last[v : v + 1, :]))
            xch[(q * SYM + v) * CH : (q * SYM + v + 1) * CH, :] = high
            xcl[(q * SYM + v) * CH : (q * SYM + v + 1) * CH, :] = low


def layer_kernel(
    count, mine, tok_s, emb_h, w_in_h, cw_h, bias_h, rate_h, skip_h, gain_h, w_out_h, *others
):
    finish_layer(
        others[:count], mine, tok_s, emb_h, w_in_h, cw_h, bias_h, rate_h, skip_h, gain_h, w_out_h,
        *others[count:]
    )


def finish_layer(
    blocks, mine, tok_s, emb_h, w_in_h, cw_h, bias_h, rate_h, skip_h, gain_h, w_out_h,
    out,
    emb, w_in, cw, bias, rate, skip, gain, w_out, emb16, atab, gtab, cst, tw, zg, lac, xch, xcl,
    tok_x, tok_f, code, tri, hist, svec, xad, xbc, yad, ybc, mix, sems,
):
    rows = tok_x.shape[0]
    own = rows // 8
    total = tok_s.shape[0]
    nchunk = total // CH
    j = mine[0]
    size = rows // len(blocks)
    fetch((emb_h, w_in_h, cw_h, bias_h, rate_h, skip_h, gain_h, w_out_h, *blocks),
          (emb, w_in, cw, bias, rate, skip, gain, w_out,
           *[tok_x.at[size * m : size * m + size, :] for m in range(len(blocks))]), sems)
    symbol_tables(
        (0, 1), (zg, lac, xch, xcl),
        emb, w_in, cw, bias, rate, skip, gain, emb16, atab, gtab, cst, tw,
    )
    for b in range(own):
        slot = (j ^ b) * 8
        tok_f[3, 8 * b : 8 * b + 8, :] = tok_x[pl.ds(pl.multiple_of(slot, 8), 8), :].astype(F32)
    tok = tok_f[3]
    for o in (-3, -2, -1, 1, 2, 3):
        tok_f[3 + o] = shifted(tok, o, rows)
    lane = iota((rows, CH), 1)
    row = iota((rows, CH), 0)
    lane_f = lane.astype(F32)
    before = 25.0 * tok_f[0] + 5.0 * tok_f[1] + tok_f[2]
    after = 25.0 * tok_f[6] + 5.0 * tok_f[5] + tok_f[4]
    code[0] = jnp.where((row == 0) & (lane < 3), 125.0 + lane_f, before)
    code[1] = jnp.where((row == rows - 1) & (lane >= CH - 3), lane_f, after)
    si = iota((CH, CH), 0)
    ri = iota((CH, CH), 1)
    ones = jnp.ones((CH, CH), F32)
    tri[0] = jnp.concatenate([jnp.where(si > ri, 1.0, 0.0), ones], axis=1).astype(BF16)
    tri[1] = jnp.concatenate([jnp.where(si < ri, 1.0, 0.0), ones], axis=1).astype(BF16)
    hist[...] = jnp.zeros_like(hist)
    sub8 = iota((8, CH), 0).astype(F32)
    subc = iota((CH, CH), 0).astype(F32)

    def block(b, off):
        side = jnp.where(b >= j, 1, 0)
        index = jnp.where(b >= j, b + 1, j - 1 - b)
        off = off * jnp.where(b == j, 0.0, 1.0)
        use_prefix = side.astype(F32)
        at = pl.ds(pl.multiple_of(index * 8, 8), 8)
        tk = tok_f[3, at, :]
        cd = code[side, at, :]
        hots = [jnp.where(tk[m : m + 1, :] == sub8, 1.0, 0.0) for m in range(8)]
        counts = nn(jnp.concatenate(hots, axis=0).astype(BF16), tri[side])
        totals = [counts[8 * m : 8 * m + 8, CH:] for m in range(8)]
        prefix = [jnp.zeros((8, CH), F32)]
        for m in range(8):
            prefix.append(prefix[-1] + totals[m])
        las = [lac[pl.ds(pl.multiple_of((side * SYM + v) * 16, 16), 16), :] for v in range(SYM)]
        acc = jnp.zeros((160, CH), F32)
        for pair in range(4):
            lefts, rights = [], []
            for m in (2 * pair, 2 * pair + 1):
                suffix = prefix[8] - prefix[m + 1]
                inside = suffix + use_prefix * (prefix[m] - suffix)
                count = counts[8 * m : 8 * m + 8, :CH] + off + inside
                exponent = las[0] * count[0:1, :]
                for v in range(1, SYM):
                    exponent = exponent + las[v] * count[v : v + 1, :]
                weight = jnp.exp2(exponent)
                masked = jnp.concatenate(
                    [jnp.where(tk[m : m + 1, :] == float(v), weight, 0.0) for v in range(SYM)],
                    axis=0,
                )
                high, low = split(masked)
                lefts.append(jnp.concatenate([high, low], axis=0))
                rights.append(jnp.where(cd[m : m + 1, :] == subc, 1.0, 0.0).astype(BF16))
            acc = acc + nt(
                jnp.concatenate(lefts, axis=1), jnp.concatenate(rights, axis=1)
            )
        hist[side] = hist[side] + acc
        return off + prefix[8]

    lax.fori_loop(0, own - 1, block, jnp.zeros((8, CH), F32))

    last8 = rows - 8
    mine8 = pl.ds(pl.multiple_of(j * 8, 8), 8)
    xs = {}
    for d in range(2):
        edge = 0 if d == 0 else 7
        seq_at = pl.ds(0 if d == 0 else last8, 8)
        hot = window_onehot([tok_f[o, seq_at, :][edge : edge + 1, :] for o in range(7)])
        for s in range(2):
            if d == 0:
                xs[s] = pltpu.roll(silu_half(nn(hot[0:16, :], tw[s]))[0:8, :], 5, 0)
            else:
                xs[2 + s] = silu_half(nn(hot[CH - 16 :, :], tw[2 + s]))[8:16, :]
    diag = iota((H, E), 0) == (iota((H, E), 1) >> 6)
    sub16 = iota((16, E), 0)
    for q in range(4):
        d, s = q // 2, q % 2
        rim = jnp.concatenate([jnp.zeros((8, E), F32), xs[q]], axis=0)
        rim_h, rim_l = split(rim)
        for v in range(SYM):
            start = (q * SYM + v) * CH
            body = slice(start, start + CH - 16)
            tail = slice(start + CH - 16, start + CH)
            tail_h = jnp.where(sub16 >= 13, rim_h.astype(F32), xch[tail, :].astype(F32))
            tail_l = jnp.where(sub16 >= 13, rim_l.astype(F32), xcl[tail, :].astype(F32))
            table_h = jnp.concatenate([xch[body, :], tail_h.astype(BF16)], axis=0)
            table_l = jnp.concatenate([xcl[body, :], tail_l.astype(BF16)], axis=0)
            at = v * 16 + s * 8
            w = hist[d, at : at + 8, :] + hist[d, 80 + at : 88 + at, :]
            high, low = split(w)
            both = jnp.concatenate([high.astype(F32), low.astype(F32)], axis=0).astype(BF16)
            one = nn(both, table_h)
            two = nn(both, table_l)
            full = one[0:8, :] + one[8:16, :] + two[0:8, :]
            vec = jnp.sum(jnp.where(diag, full, 0.0), axis=0, keepdims=True)
            for i in range(4):
                at = (d * SYM + v) * 8 + s * 4 + i
                svec[at : at + 1, :] = vec[:, 128 * i : 128 * i + 128]
    starts = []
    for d in range(2):
        for w in range(SYM):
            value = jnp.zeros((8, CH), F32)
            for v in range(SYM):
                at = (d * SYM + w) * 64 + v * 8
                sat = (d * SYM + v) * 8
                value = value + gtab[at : at + 8, :] * svec[sat : sat + 8, :]
            starts.append(value)

    shifts = [tok_f[o, mine8, :] for o in range(7)]
    for c in range(nchunk):
        hot = window_onehot([sh[c : c + 1, :] for sh in shifts])
        for q, (d, s, k) in enumerate(CHAINS):
            x = silu_half(nn(hot, tw[q]))
            ref = (xad, xbc)[d]
            for i in range(4):
                ref[pl.ds(c * 8 * CH + s * 4 + i, CH, stride=8), :] = x[:, 128 * i : 128 * i + 128]

    skips = (cst[0:8, :], cst[8:16, :])

    def advance(d, src, t, state):
        u = tok_s[t]
        x = tile_at(src, t * 8)
        a = tile_at(atab, d * 64 + u * 8)
        new = [
            a * state[w] + tile_at(gtab, (d * SYM + w) * 64 + u * 8) * x for w in range(SYM)
        ]
        return new, (pick(new, u) + skips[d] * x) * tile_at(zg, u * 8)

    unroll = 32
    held = 8

    def group(g, carry):
        ya, yb = list(carry[:SYM]), list(carry[SYM:])
        for begin in range(0, unroll, held):
            done = []
            for i in range(begin, begin + held):
                n = g * unroll + i
                m = total - 1 - n
                ya, out0 = advance(0, xad, n, ya)
                yb, out1 = advance(1, xbc, m, yb)
                done.append((n, m, out0, out1))
            for n, m, out0, out1 in done:
                yad[pl.ds(pl.multiple_of(n * 8, 8), 8), :] = out0
                ybc[pl.ds(pl.multiple_of(m * 8, 8), 8), :] = out1
        return tuple(ya + yb)

    lax.fori_loop(0, total // unroll, group, tuple(starts))

    flip = jnp.where(iota((D, D), 0) + iota((D, D), 1) == D - 1, 1.0, 0.0).astype(BF16)
    wout = w_out[...]
    wflip = nn(wout, flip).astype(BF16)
    mean = jnp.where(
        (iota((2 * CH, 2 * CH), 0) >> 6) == (iota((2 * CH, 2 * CH), 1) >> 6), 1.0 / 64.0, 0.0
    ).astype(BF16)
    emb_rows = jnp.concatenate(
        [emb16[0:8, :], jnp.zeros((CH - 8, D), F32)], axis=0
    ).astype(BF16)
    gains = (cst[16:24, :], cst[24:32, :])
    sub = iota((8, CH), 0).astype(F32)
    mix[...] = jnp.zeros_like(mix)
    tiles = CH // SUB

    def project(c):
        base = (c & 1) * (CH * 8)
        row = tok_f[3, pl.ds(j * 8 + c, 1), :]
        hot = jnp.concatenate(
            [jnp.where(row == sub, 1.0, 0.0), jnp.zeros((CH - 8, CH), F32)], axis=0
        ).T.astype(BF16)
        parts = [mix[pl.ds(base + i, CH, stride=8), :].astype(BF16) for i in range(8)]
        one = nn(jnp.concatenate(parts[0:4], axis=1), wout).astype(BF16).astype(F32)
        two = nn(jnp.concatenate(parts[4:8], axis=1), wflip).astype(BF16).astype(F32)
        out[pl.ds(pl.multiple_of(c * CH, CH), CH), :] = (nn(hot, emb_rows) + one + two).astype(BF16)

    def tile(c, k):
        at = pl.ds(pl.multiple_of((c * CH + k * SUB) * 8, SUB * 8), SUB * 8)
        found = (yad[at, :], ybc[at, :])
        high, low = split(jnp.concatenate([g * g for g in found], axis=1))
        scale = lax.rsqrt(nn(high, mean) + nn(low, mean) + EPSILON)
        normed = None
        for d in range(2):
            scaled = (found[d] * scale[:, CH * d : CH * d + CH]).reshape(SUB, 8, CH) * gains[d][None]
            normed = scaled if normed is None else normed + scaled
        at = (c & 1) * (CH * 8) + k * SUB * 8
        mix[pl.ds(pl.multiple_of(at, 8), SUB * 8), :] = normed.reshape(SUB * 8, CH)

    def chunk(c, _):
        project(jnp.maximum(c - 1, 0))
        for k in range(tiles):
            tile(c, k)
        return 0

    lax.fori_loop(0, nchunk, chunk, 0)
    project(nchunk - 1)


def per_device(
    token_ids,
    embed_table,
    input_weight_matrix,
    output_weight_matrix,
    conv_weight,
    dt_bias,
    decay_rate,
    skip_gain,
    norm_gain,
):
    length = token_ids.shape[0]
    nchunk = length // CH
    own = lax.axis_size("seq")
    tok2 = token_ids.reshape(nchunk, CH)
    rounds = own.bit_length() - 1
    rows = own * nchunk
    vm = pl.BlockSpec(memory_space=pltpu.VMEM)
    sm = pl.BlockSpec(memory_space=pltpu.SMEM)
    hbm = pl.BlockSpec(memory_space=pl.ANY)
    sds = jax.ShapeDtypeStruct
    weights = (
        embed_table, input_weight_matrix.T, conv_weight, dt_bias, decay_rate, skip_gain, norm_gain,
        output_weight_matrix,
    )

    def sent(blocks, mask):
        return lax.ppermute(blocks, "seq", [(i, i ^ mask) for i in range(own)])

    gathered = tok2
    low = max(rounds - 3, 0)
    for bit in range(low):
        gathered = jnp.concatenate([gathered, sent(gathered, 1 << bit)], axis=0)
    blocks = [gathered] + [sent(gathered, m << low) for m in range(1, own >> low)]
    mine = lax.axis_index("seq").reshape(1).astype(jnp.int32)
    table = pltpu.VMEM((4 * SYM * CH, E), BF16)
    steps = pltpu.VMEM((length * 8, CH), F32)
    return pl.pallas_call(
        functools.partial(layer_kernel, len(blocks)),
        out_shape=sds((length, D), BF16),
        in_specs=[sm, sm] + [hbm] * 8 + [hbm] * len(blocks),
        out_specs=vm,
        scratch_shapes=[pltpu.VMEM(w.shape, w.dtype) for w in weights]
        + [
            pltpu.VMEM((16, D), F32),
            pltpu.VMEM((2 * 64, CH), F32),
            pltpu.VMEM((2 * SYM * 64, CH), F32),
            pltpu.VMEM((32, CH), F32),
            pltpu.VMEM((4, CH, E), BF16),
            pltpu.VMEM((64, CH), F32),
            pltpu.VMEM((2 * SYM * 16, CH), F32),
            table,
            table,
            pltpu.VMEM((rows, CH), jnp.int32),
            pltpu.VMEM((7, rows, CH), F32),
            pltpu.VMEM((2, rows, CH), F32),
            pltpu.VMEM((2, CH, 2 * CH), BF16),
            pltpu.VMEM((2, 160, CH), F32),
            pltpu.VMEM((2 * SYM * 8, CH), F32),
            steps,
            steps,
            steps,
            steps,
            pltpu.VMEM((2 * CH * 8, CH), F32),
            pltpu.SemaphoreType.DMA((8 + len(blocks),)),
        ],
        compiler_params=pltpu.CompilerParams(vmem_limit_bytes=56 * 1024 * 1024),
        cost_estimate=pl.CostEstimate(
            flops=9_000_000_000, bytes_accessed=4_000_000, transcendentals=0
        ),
        name="bidirectional_layer",
    )(mine, token_ids, *weights, *blocks)


def solution(mesh):
    placed = (P(("batch", "seq")), P(), P(), P(), P(), P(), P(), P(), P())
    return jax.shard_map(
        per_device, mesh=mesh, in_specs=placed, out_specs=P(("batch", "seq"), None), check_vma=False
    )
```

```python
import functools

import jax
import jax.numpy as jnp
from jax import lax
from jax.experimental import pallas as pl
from jax.experimental.pallas import tpu as pltpu
from jax.sharding import PartitionSpec as P

D = 256
E = 512
NS = 16
H = 8
KW = 4
SYM = 5
LOG2E = 1.4426950408889634
EPSILON = 1e-05
CH = 128
SUB = 32

F32 = jnp.float32
BF16 = jnp.bfloat16

CHAINS = ((0, 0, 0), (0, 1, 1), (1, 0, 1), (1, 1, 0))


def iota(shape, dim):
    return lax.broadcasted_iota(jnp.int32, shape, dim)


def nn(a, b, **kw):
    return lax.dot_general(a, b, (((1,), (0,)), ((), ())), preferred_element_type=F32, **kw)


def nt(a, b, **kw):
    return lax.dot_general(a, b, (((1,), (1,)), ((), ())), preferred_element_type=F32, **kw)


def split(value):
    high = value.astype(BF16)
    low = (value - high.astype(F32)).astype(BF16)
    return high, low


def softplus(x):
    return jnp.maximum(x, 0.0) + jnp.log1p(jnp.exp(-jnp.abs(x)))


def silu_half(half):
    return half + half * jnp.tanh(half)


def tap_row(direction, j):
    return j if direction == 0 else 2 * (KW - 1) - j


def window_onehot(rows):
    sub = iota((8, CH), 0).astype(F32)
    blocks = [jnp.where(row == sub, 1.0, 0.0) for row in rows]
    blocks.append(jnp.zeros((8, CH), F32))
    stacked = jnp.concatenate(blocks + blocks, axis=0)
    return stacked.T.astype(BF16)


def shifted(tok, offset, rows):
    if offset == 0:
        return tok
    lane = iota((rows, CH), 1)
    row = iota((rows, CH), 0)
    moved = pltpu.roll(tok, (-offset) % CH, 1)
    if offset < 0:
        other = pltpu.roll(moved, 1, 0)
        crossing = lane < -offset
        outside = crossing & (row == 0)
    else:
        other = pltpu.roll(moved, rows - 1, 0)
        crossing = lane >= CH - offset
        outside = crossing & (row == rows - 1)
    return jnp.where(outside, 5.0, jnp.where(crossing, other, moved))


def pick(values, u):
    low = (u & 1) == 1
    first = jnp.where(low, values[1], values[0])
    second = jnp.where(low, values[3], values[2])
    return jnp.where(u > 3, values[4], jnp.where((u & 2) == 2, second, first))


def tile_at(ref, row):
    return ref[pl.ds(pl.multiple_of(row, 8), 8), :]


def fetch(sources, targets, sems):
    copies = [
        pltpu.make_async_copy(a, b, sems.at[i]) for i, (a, b) in enumerate(zip(sources, targets))
    ]
    for copy in copies:
        copy.start()
    for copy in copies:
        copy.wait()


def symbol_tables(
    directions, full, emb, w_in, cw, bias, rate, skip, gain, emb16, atab, gtab, cst, tw
):
    highest = lax.Precision.HIGHEST
    emb16[...] = jnp.zeros_like(emb16)
    e32 = emb[...].astype(F32)
    emb16[0:SYM, :] = e32
    for v in range(4):
        emb16[8 + v : 9 + v, :] = e32[3 - v : 4 - v, :]
    emb16[12:13, :] = e32[4:5, :]
    embs = emb16[...].astype(BF16)
    x16 = nt(embs, w_in[E : 2 * E, :]).astype(BF16).astype(F32)
    rest = nt(embs, w_in[2 * E :, :]).astype(BF16)
    nrest = 2 * NS + H
    expand = jnp.where(
        iota((nrest, E), 0) == (iota((nrest, E), 1) >> 6) + 2 * NS, 1.0, 0.0
    ).astype(BF16)
    heads = jnp.where(iota((H, E), 0) == (iota((H, E), 1) >> 6), 1.0, 0.0)
    r_exp = nn(rest, expand)
    bias_e = nn(bias[...], heads, precision=highest)
    rate_e = nn(rate[...], heads, precision=highest)
    skip_e = nn(skip[...], heads, precision=highest)
    shift = jnp.where(
        iota((nrest, nrest), 0) + NS == iota((nrest, nrest), 1),
        jnp.where(iota((nrest, nrest), 0) < NS, 1.0, 0.0),
        0.0,
    ).astype(BF16)
    rest_b = nn(rest, shift).astype(BF16)
    cb = nt(rest_b, rest)
    if full is not None:
        zg, lac, xch, xcl = full
        z16 = nt(embs, w_in[0:E, :]).astype(BF16).astype(F32)
        sz = z16 * (0.5 + 0.5 * jnp.tanh(0.5 * z16))
        for s in range(2):
            for i in range(4):
                zg[pl.ds(s * 4 + i, 8, stride=8), :] = sz[8 * s : 8 * s + 8, 128 * i : 128 * i + 128]
        pick_r = jnp.where(
            iota((H, nrest), 0) + 2 * NS == iota((H, nrest), 1), 1.0, 0.0
        ).astype(BF16)
        r_t = nt(pick_r, rest)
        eye = jnp.where(iota((H, H), 0) == iota((H, H), 1), 1.0, 0.0)
        bias_t = nt(eye, bias[...], precision=highest)
        rate_t = nt(eye, rate[...], precision=highest)
    for q, (d, s, k) in enumerate(CHAINS):
        if d not in directions:
            continue
        dt = softplus(r_exp[8 * s : 8 * s + 8, :] + bias_e[k : k + 1, :])
        a = jnp.exp(-rate_e[k : k + 1, :] * dt)
        for i in range(4):
            lanes = slice(128 * i, 128 * i + 128)
            atab[pl.ds(d * 64 + s * 4 + i, 8, stride=8), :] = a[:, lanes]
            cst[d * 8 + s * 4 + i : d * 8 + s * 4 + i + 1, :] = skip_e[k : k + 1, lanes]
            cst[16 + d * 8 + s * 4 + i : 17 + d * 8 + s * 4 + i, :] = gain[k : k + 1, lanes]
        for u in range(SYM):
            g = cb[8 * s : 8 * s + 8, 8 * s + u : 8 * s + u + 1] * dt
            for i in range(4):
                gtab[pl.ds((d * SYM + u) * 64 + s * 4 + i, 8, stride=8), :] = g[
                    :, 128 * i : 128 * i + 128
                ]
        xs = x16[8 * s : 8 * s + 8, :]
        blocks = [jnp.zeros((8, E), F32)] * 8
        for j in range(KW):
            blocks[tap_row(d, j)] = (0.5 * cw[k, j : j + 1, :]) * xs
        high, low = split(jnp.concatenate(blocks, axis=0))
        tw[q, 0:64, :] = high
        tw[q, 64:128, :] = low
        if full is None:
            continue
        la = (
            -rate_t[:, k : k + 1] * softplus(r_t[:, 8 * s : 8 * s + 8] + bias_t[:, k : k + 1])
        ) * LOG2E
        for v in range(SYM):
            lac[(d * SYM + v) * 16 + s * 8 : (d * SYM + v) * 16 + s * 8 + 8, :] = jnp.broadcast_to(
                la[:, v : v + 1], (8, CH)
            )
        code = iota((CH, CH), 0).astype(F32)
        lane = iota((CH, CH), 1) & 63
        slot = lane >> 3
        sym = (lane & 7).astype(F32)
        d0 = jnp.floor((code + 0.5) * (1.0 / 25.0))
        d01 = jnp.floor((code + 0.5) * (1.0 / 5.0))
        digits = (d0, d01 - 5.0 * d0, code - 5.0 * d01)
        hot = jnp.zeros((CH, CH), F32)
        for j in range(KW - 1):
            hot = jnp.where(
                slot == tap_row(d, j), jnp.where(sym == digits[j], 1.0, 0.0), hot
            )
        partial = nn(hot.astype(BF16), tw[q])
        last = blocks[tap_row(d, KW - 1)]
        for v in range(SYM):
            high, low = split(silu_half(partial + last[v : v + 1, :]))
            xch[(q * SYM + v) * CH : (q * SYM + v + 1) * CH, :] = high
            xcl[(q * SYM + v) * CH : (q * SYM + v + 1) * CH, :] = low


def layer_kernel(
    count, mine, tok_s, emb_h, w_in_h, cw_h, bias_h, rate_h, skip_h, gain_h, w_out_h, *others
):
    finish_layer(
        others[:count], mine, tok_s, emb_h, w_in_h, cw_h, bias_h, rate_h, skip_h, gain_h, w_out_h,
        *others[count:]
    )


def finish_layer(
    blocks, mine, tok_s, emb_h, w_in_h, cw_h, bias_h, rate_h, skip_h, gain_h, w_out_h,
    out,
    emb, w_in, cw, bias, rate, skip, gain, w_out, emb16, atab, gtab, cst, tw, zg, lac, xch, xcl,
    tok_x, tok_f, code, tri, hist, svec, xad, xbc, yad, ybc, mix,
    ring0, ring1, ring2, ring3, sems,
):
    rows = tok_x.shape[0]
    own = rows // 8
    total = tok_s.shape[0]
    nchunk = total // CH
    j = mine[0]
    size = rows // len(blocks)
    fetch((emb_h, w_in_h, cw_h, bias_h, rate_h, skip_h, gain_h, w_out_h, *blocks),
          (emb, w_in, cw, bias, rate, skip, gain, w_out,
           *[tok_x.at[size * m : size * m + size, :] for m in range(len(blocks))]), sems)
    symbol_tables(
        (0, 1), (zg, lac, xch, xcl),
        emb, w_in, cw, bias, rate, skip, gain, emb16, atab, gtab, cst, tw,
    )
    for b in range(own):
        slot = (j ^ b) * 8
        tok_f[3, 8 * b : 8 * b + 8, :] = tok_x[pl.ds(pl.multiple_of(slot, 8), 8), :].astype(F32)
    tok = tok_f[3]
    for o in (-3, -2, -1, 1, 2, 3):
        tok_f[3 + o] = shifted(tok, o, rows)
    lane = iota((rows, CH), 1)
    row = iota((rows, CH), 0)
    lane_f = lane.astype(F32)
    before = 25.0 * tok_f[0] + 5.0 * tok_f[1] + tok_f[2]
    after = 25.0 * tok_f[6] + 5.0 * tok_f[5] + tok_f[4]
    code[0] = jnp.where((row == 0) & (lane < 3), 125.0 + lane_f, before)
    code[1] = jnp.where((row == rows - 1) & (lane >= CH - 3), lane_f, after)
    si = iota((CH, CH), 0)
    ri = iota((CH, CH), 1)
    ones = jnp.ones((CH, CH), F32)
    tri[0] = jnp.concatenate([jnp.where(si > ri, 1.0, 0.0), ones], axis=1).astype(BF16)
    tri[1] = jnp.concatenate([jnp.where(si < ri, 1.0, 0.0), ones], axis=1).astype(BF16)
    hist[...] = jnp.zeros_like(hist)
    sub8 = iota((8, CH), 0).astype(F32)
    subc = iota((CH, CH), 0).astype(F32)

    def block(b, off):
        side = jnp.where(b >= j, 1, 0)
        index = jnp.where(b >= j, b + 1, j - 1 - b)
        off = off * jnp.where(b == j, 0.0, 1.0)
        use_prefix = side.astype(F32)
        at = pl.ds(pl.multiple_of(index * 8, 8), 8)
        tk = tok_f[3, at, :]
        cd = code[side, at, :]
        hots = [jnp.where(tk[m : m + 1, :] == sub8, 1.0, 0.0) for m in range(8)]
        counts = nn(jnp.concatenate(hots, axis=0).astype(BF16), tri[side])
        totals = [counts[8 * m : 8 * m + 8, CH:] for m in range(8)]
        prefix = [jnp.zeros((8, CH), F32)]
        for m in range(8):
            prefix.append(prefix[-1] + totals[m])
        las = [lac[pl.ds(pl.multiple_of((side * SYM + v) * 16, 16), 16), :] for v in range(SYM)]
        acc = jnp.zeros((160, CH), F32)
        for pair in range(4):
            lefts, rights = [], []
            for m in (2 * pair, 2 * pair + 1):
                suffix = prefix[8] - prefix[m + 1]
                inside = suffix + use_prefix * (prefix[m] - suffix)
                count = counts[8 * m : 8 * m + 8, :CH] + off + inside
                exponent = las[0] * count[0:1, :]
                for v in range(1, SYM):
                    exponent = exponent + las[v] * count[v : v + 1, :]
                weight = jnp.exp2(exponent)
                masked = jnp.concatenate(
                    [jnp.where(tk[m : m + 1, :] == float(v), weight, 0.0) for v in range(SYM)],
                    axis=0,
                )
                high, low = split(masked)
                lefts.append(jnp.concatenate([high, low], axis=0))
                rights.append(jnp.where(cd[m : m + 1, :] == subc, 1.0, 0.0).astype(BF16))
            acc = acc + nt(
                jnp.concatenate(lefts, axis=1), jnp.concatenate(rights, axis=1)
            )
        hist[side] = hist[side] + acc
        return off + prefix[8]

    if own <= 8:
        seen = jnp.zeros((8, CH), F32)
        for b in range(own - 1):
            seen = block(jnp.int32(b), seen)
    else:
        lax.fori_loop(0, own - 1, block, jnp.zeros((8, CH), F32))

    last8 = rows - 8
    mine8 = pl.ds(pl.multiple_of(j * 8, 8), 8)
    xs = {}
    for d in range(2):
        edge = 0 if d == 0 else 7
        seq_at = pl.ds(0 if d == 0 else last8, 8)
        hot = window_onehot([tok_f[o, seq_at, :][edge : edge + 1, :] for o in range(7)])
        for s in range(2):
            if d == 0:
                xs[s] = pltpu.roll(silu_half(nn(hot[0:16, :], tw[s]))[0:8, :], 5, 0)
            else:
                xs[2 + s] = silu_half(nn(hot[CH - 16 :, :], tw[2 + s]))[8:16, :]
    diag = iota((H, E), 0) == (iota((H, E), 1) >> 6)
    sub16 = iota((16, E), 0)
    for q in range(4):
        d, s = q // 2, q % 2
        rim = jnp.concatenate([jnp.zeros((8, E), F32), xs[q]], axis=0)
        rim_h, rim_l = split(rim)
        for v in range(SYM):
            start = (q * SYM + v) * CH
            body = slice(start, start + CH - 16)
            tail = slice(start + CH - 16, start + CH)
            tail_h = jnp.where(sub16 >= 13, rim_h.astype(F32), xch[tail, :].astype(F32))
            tail_l = jnp.where(sub16 >= 13, rim_l.astype(F32), xcl[tail, :].astype(F32))
            table_h = jnp.concatenate([xch[body, :], tail_h.astype(BF16)], axis=0)
            table_l = jnp.concatenate([xcl[body, :], tail_l.astype(BF16)], axis=0)
            at = v * 16 + s * 8
            w = hist[d, at : at + 8, :] + hist[d, 80 + at : 88 + at, :]
            high, low = split(w)
            both = jnp.concatenate([high.astype(F32), low.astype(F32)], axis=0).astype(BF16)
            one = nn(both, table_h)
            two = nn(both, table_l)
            full = one[0:8, :] + one[8:16, :] + two[0:8, :]
            vec = jnp.sum(jnp.where(diag, full, 0.0), axis=0, keepdims=True)
            for i in range(4):
                at = (d * SYM + v) * 8 + s * 4 + i
                svec[at : at + 1, :] = vec[:, 128 * i : 128 * i + 128]
    starts = []
    for d in range(2):
        for w in range(SYM):
            value = jnp.zeros((8, CH), F32)
            for v in range(SYM):
                at = (d * SYM + w) * 64 + v * 8
                sat = (d * SYM + v) * 8
                value = value + gtab[at : at + 8, :] * svec[sat : sat + 8, :]
            starts.append(value)

    shifts = [tok_f[o, mine8, :] for o in range(7)]
    for c in range(nchunk):
        hot = window_onehot([sh[c : c + 1, :] for sh in shifts])
        for q, (d, s, k) in enumerate(CHAINS):
            x = silu_half(nn(hot, tw[q]))
            ref = (xad, xbc)[d]
            for i in range(4):
                ref[pl.ds(c * 8 * CH + s * 4 + i, CH, stride=8), :] = x[:, 128 * i : 128 * i + 128]

    skips = (cst[0:8, :], cst[8:16, :])

    def advance(d, src, t, state, ring, slot):
        u = tok_s[t]
        x = tile_at(src, t * 8)
        a = tile_at(atab, d * 64 + u * 8)
        new = [
            a * state[w] + tile_at(gtab, (d * SYM + w) * 64 + u * 8) * x for w in range(SYM)
        ]
        for w in range(SYM):
            ring[(slot * SYM + w) * 8 : (slot * SYM + w) * 8 + 8, :] = new[w]
        return new, x, u

    unroll = 32
    held = 8
    rings = ((ring0, ring1), (ring2, ring3))

    def group(g, carry):
        ya, yb = list(carry[:SYM]), list(carry[SYM:])
        for begin in range(0, unroll, held):
            ra, rb = rings[(begin // held) % 2]
            done = []
            for i in range(held):
                n = g * unroll + begin + i
                m = total - 1 - n
                ya, x0, u0 = advance(0, xad, n, ya, ra, i)
                yb, x1, u1 = advance(1, xbc, m, yb, rb, i)
                done.append((n, m, x0, x1, u0, u1))
            for i, (n, m, x0, x1, u0, u1) in enumerate(done):
                for d, ring, dest, t, x, u in ((0, ra, yad, n, x0, u0), (1, rb, ybc, m, x1, u1)):
                    y = tile_at(ring, i * SYM * 8 + u * 8) + skips[d] * x
                    dest[pl.ds(pl.multiple_of(t * 8, 8), 8), :] = y * tile_at(zg, u * 8)
        return tuple(ya + yb)

    lax.fori_loop(0, total // unroll, group, tuple(starts))

    flip = jnp.where(iota((D, D), 0) + iota((D, D), 1) == D - 1, 1.0, 0.0).astype(BF16)
    wout = w_out[...]
    wflip = nn(wout, flip).astype(BF16)
    mean = jnp.where(
        ((iota((4 * CH, 2 * CH), 0) & 255) >> 6) == (iota((4 * CH, 2 * CH), 1) >> 6), 1.0 / 64.0, 0.0
    ).astype(BF16)
    emb_rows = jnp.concatenate(
        [emb16[0:8, :], jnp.zeros((CH - 8, D), F32)], axis=0
    ).astype(BF16)
    gains = (cst[16:24, :], cst[24:32, :])
    sub = iota((8, CH), 0).astype(F32)
    mix[...] = jnp.zeros_like(mix)
    tiles = CH // SUB

    def project(c):
        base = (c & 1) * (CH * 8)
        row = tok_f[3, pl.ds(j * 8 + c, 1), :]
        hot = jnp.concatenate(
            [jnp.where(row == sub, 1.0, 0.0), jnp.zeros((CH - 8, CH), F32)], axis=0
        ).T.astype(BF16)
        parts = [mix[pl.ds(base + i, CH, stride=8), :].astype(BF16) for i in range(8)]
        one = nn(jnp.concatenate(parts[0:4], axis=1), wout).astype(BF16).astype(F32)
        two = nn(jnp.concatenate(parts[4:8], axis=1), wflip).astype(BF16).astype(F32)
        out[pl.ds(pl.multiple_of(c * CH, CH), CH), :] = (nn(hot, emb_rows) + one + two).astype(BF16)

    def tile(c, k):
        at = pl.ds(pl.multiple_of((c * CH + k * SUB) * 8, SUB * 8), SUB * 8)
        found = (yad[at, :], ybc[at, :])
        high, low = split(jnp.concatenate([g * g for g in found], axis=1))
        scale = lax.rsqrt(nn(jnp.concatenate([high, low], axis=1), mean) + EPSILON)
        normed = None
        for d in range(2):
            scaled = (found[d] * scale[:, CH * d : CH * d + CH]).reshape(SUB, 8, CH) * gains[d][None]
            normed = scaled if normed is None else normed + scaled
        at = (c & 1) * (CH * 8) + k * SUB * 8
        mix[pl.ds(pl.multiple_of(at, 8), SUB * 8), :] = normed.reshape(SUB * 8, CH)

    def chunk(c, _):
        project(jnp.maximum(c - 1, 0))
        for k in range(tiles):
            tile(c, k)
        return 0

    lax.fori_loop(0, nchunk, chunk, 0)
    project(nchunk - 1)


def per_device(
    token_ids,
    embed_table,
    input_weight_matrix,
    output_weight_matrix,
    conv_weight,
    dt_bias,
    decay_rate,
    skip_gain,
    norm_gain,
):
    length = token_ids.shape[0]
    nchunk = length // CH
    own = lax.axis_size("seq")
    tok2 = token_ids.reshape(nchunk, CH)
    rounds = own.bit_length() - 1
    rows = own * nchunk
    vm = pl.BlockSpec(memory_space=pltpu.VMEM)
    sm = pl.BlockSpec(memory_space=pltpu.SMEM)
    hbm = pl.BlockSpec(memory_space=pl.ANY)
    sds = jax.ShapeDtypeStruct
    weights = (
        embed_table, input_weight_matrix.T, conv_weight, dt_bias, decay_rate, skip_gain, norm_gain,
        output_weight_matrix,
    )

    def sent(blocks, mask):
        return lax.ppermute(blocks, "seq", [(i, i ^ mask) for i in range(own)])

    gathered = tok2
    low = max(rounds - 3, 0)
    for bit in range(low):
        gathered = jnp.concatenate([gathered, sent(gathered, 1 << bit)], axis=0)
    blocks = [gathered] + [sent(gathered, m << low) for m in range(1, own >> low)]
    mine = lax.axis_index("seq").reshape(1).astype(jnp.int32)
    table = pltpu.VMEM((4 * SYM * CH, E), BF16)
    steps = pltpu.VMEM((length * 8, CH), F32)
    ring = pltpu.VMEM((8 * SYM * 8, CH), F32)
    return pl.pallas_call(
        functools.partial(layer_kernel, len(blocks)),
        out_shape=sds((length, D), BF16),
        in_specs=[sm, sm] + [hbm] * 8 + [hbm] * len(blocks),
        out_specs=vm,
        scratch_shapes=[pltpu.VMEM(w.shape, w.dtype) for w in weights]
        + [
            pltpu.VMEM((16, D), F32),
            pltpu.VMEM((2 * 64, CH), F32),
            pltpu.VMEM((2 * SYM * 64, CH), F32),
            pltpu.VMEM((32, CH), F32),
            pltpu.VMEM((4, CH, E), BF16),
            pltpu.VMEM((64, CH), F32),
            pltpu.VMEM((2 * SYM * 16, CH), F32),
            table,
            table,
            pltpu.VMEM((rows, CH), jnp.int32),
            pltpu.VMEM((7, rows, CH), F32),
            pltpu.VMEM((2, rows, CH), F32),
            pltpu.VMEM((2, CH, 2 * CH), BF16),
            pltpu.VMEM((2, 160, CH), F32),
            pltpu.VMEM((2 * SYM * 8, CH), F32),
            steps,
            steps,
            steps,
            steps,
            pltpu.VMEM((2 * CH * 8, CH), F32),
            ring,
            ring,
            ring,
            ring,
            pltpu.SemaphoreType.DMA((8 + len(blocks),)),
        ],
        compiler_params=pltpu.CompilerParams(vmem_limit_bytes=56 * 1024 * 1024),
        cost_estimate=pl.CostEstimate(
            flops=9_000_000_000, bytes_accessed=4_000_000, transcendentals=0
        ),
        name="bidirectional_layer",
    )(mine, token_ids, *weights, *blocks)


def solution(mesh):
    placed = (P(("batch", "seq")), P(), P(), P(), P(), P(), P(), P(), P())
    return jax.shard_map(
        per_device, mesh=mesh, in_specs=placed, out_specs=P(("batch", "seq"), None), check_vma=False
    )
```

```python
import functools

import jax
import jax.numpy as jnp
from jax import lax
from jax.experimental import pallas as pl
from jax.experimental.pallas import tpu as pltpu
from jax.sharding import PartitionSpec as P

D = 256
E = 512
NS = 16
H = 8
KW = 4
SYM = 5
LOG2E = 1.4426950408889634
EPSILON = 1e-05
CH = 128
SUB = 32

F32 = jnp.float32
BF16 = jnp.bfloat16

CHAINS = ((0, 0, 0), (0, 1, 1), (1, 0, 1), (1, 1, 0))


def iota(shape, dim):
    return lax.broadcasted_iota(jnp.int32, shape, dim)


def nn(a, b, **kw):
    return lax.dot_general(a, b, (((1,), (0,)), ((), ())), preferred_element_type=F32, **kw)


def nt(a, b, **kw):
    return lax.dot_general(a, b, (((1,), (1,)), ((), ())), preferred_element_type=F32, **kw)


def split(value):
    high = value.astype(BF16)
    low = (value - high.astype(F32)).astype(BF16)
    return high, low


def softplus(x):
    return jnp.maximum(x, 0.0) + jnp.log1p(jnp.exp(-jnp.abs(x)))


def silu_half(half):
    return half + half * jnp.tanh(half)


def tap_row(direction, j):
    return j if direction == 0 else 2 * (KW - 1) - j


def window_onehot(rows):
    sub = iota((8, CH), 0).astype(F32)
    blocks = [jnp.where(row == sub, 1.0, 0.0) for row in rows]
    blocks.append(jnp.zeros((8, CH), F32))
    stacked = jnp.concatenate(blocks + blocks, axis=0)
    return stacked.T.astype(BF16)


def shifted(tok, offset, rows):
    if offset == 0:
        return tok
    lane = iota((rows, CH), 1)
    row = iota((rows, CH), 0)
    moved = pltpu.roll(tok, (-offset) % CH, 1)
    if offset < 0:
        other = pltpu.roll(moved, 1, 0)
        crossing = lane < -offset
        outside = crossing & (row == 0)
    else:
        other = pltpu.roll(moved, rows - 1, 0)
        crossing = lane >= CH - offset
        outside = crossing & (row == rows - 1)
    return jnp.where(outside, 5.0, jnp.where(crossing, other, moved))


def pick(values, u):
    low = (u & 1) == 1
    first = jnp.where(low, values[1], values[0])
    second = jnp.where(low, values[3], values[2])
    return jnp.where(u > 3, values[4], jnp.where((u & 2) == 2, second, first))


def tile_at(ref, row):
    return ref[pl.ds(pl.multiple_of(row, 8), 8), :]


def begin(sources, targets, sems):
    copies = [
        pltpu.make_async_copy(a, b, sems.at[i]) for i, (a, b) in enumerate(zip(sources, targets))
    ]
    for copy in copies:
        copy.start()
    return copies


def symbol_tables(
    directions, full, emb, w_in, cw, bias, rate, skip, gain, emb16, atab, gtab, cst, tw
):
    highest = lax.Precision.HIGHEST
    emb16[...] = jnp.zeros_like(emb16)
    e32 = emb[...].astype(F32)
    emb16[0:SYM, :] = e32
    for v in range(4):
        emb16[8 + v : 9 + v, :] = e32[3 - v : 4 - v, :]
    emb16[12:13, :] = e32[4:5, :]
    embs = emb16[...].astype(BF16)
    x16 = nt(embs, w_in[E : 2 * E, :]).astype(BF16).astype(F32)
    rest = nt(embs, w_in[2 * E :, :]).astype(BF16)
    nrest = 2 * NS + H
    expand = jnp.where(
        iota((nrest, E), 0) == (iota((nrest, E), 1) >> 6) + 2 * NS, 1.0, 0.0
    ).astype(BF16)
    heads = jnp.where(iota((H, E), 0) == (iota((H, E), 1) >> 6), 1.0, 0.0)
    r_exp = nn(rest, expand)
    bias_e = nn(bias[...], heads, precision=highest)
    rate_e = nn(rate[...], heads, precision=highest)
    skip_e = nn(skip[...], heads, precision=highest)
    shift = jnp.where(
        iota((nrest, nrest), 0) + NS == iota((nrest, nrest), 1),
        jnp.where(iota((nrest, nrest), 0) < NS, 1.0, 0.0),
        0.0,
    ).astype(BF16)
    rest_b = nn(rest, shift).astype(BF16)
    cb = nt(rest_b, rest)
    if full is not None:
        zg, lac, xch, xcl = full
        z16 = nt(embs, w_in[0:E, :]).astype(BF16).astype(F32)
        sz = z16 * (0.5 + 0.5 * jnp.tanh(0.5 * z16))
        for s in range(2):
            for i in range(4):
                zg[pl.ds(s * 4 + i, 8, stride=8), :] = sz[8 * s : 8 * s + 8, 128 * i : 128 * i + 128]
        pick_r = jnp.where(
            iota((H, nrest), 0) + 2 * NS == iota((H, nrest), 1), 1.0, 0.0
        ).astype(BF16)
        r_t = nt(pick_r, rest)
        eye = jnp.where(iota((H, H), 0) == iota((H, H), 1), 1.0, 0.0)
        bias_t = nt(eye, bias[...], precision=highest)
        rate_t = nt(eye, rate[...], precision=highest)
    for q, (d, s, k) in enumerate(CHAINS):
        if d not in directions:
            continue
        dt = softplus(r_exp[8 * s : 8 * s + 8, :] + bias_e[k : k + 1, :])
        a = jnp.exp(-rate_e[k : k + 1, :] * dt)
        for i in range(4):
            lanes = slice(128 * i, 128 * i + 128)
            atab[pl.ds(d * 64 + s * 4 + i, 8, stride=8), :] = a[:, lanes]
            cst[d * 8 + s * 4 + i : d * 8 + s * 4 + i + 1, :] = skip_e[k : k + 1, lanes]
            cst[16 + d * 8 + s * 4 + i : 17 + d * 8 + s * 4 + i, :] = gain[k : k + 1, lanes]
        for u in range(SYM):
            g = cb[8 * s : 8 * s + 8, 8 * s + u : 8 * s + u + 1] * dt
            for i in range(4):
                gtab[pl.ds((d * SYM + u) * 64 + s * 4 + i, 8, stride=8), :] = g[
                    :, 128 * i : 128 * i + 128
                ]
        xs = x16[8 * s : 8 * s + 8, :]
        blocks = [jnp.zeros((8, E), F32)] * 8
        for j in range(KW):
            blocks[tap_row(d, j)] = (0.5 * cw[k, j : j + 1, :]) * xs
        high, low = split(jnp.concatenate(blocks, axis=0))
        tw[q, 0:64, :] = high
        tw[q, 64:128, :] = low
        if full is None:
            continue
        la = (
            -rate_t[:, k : k + 1] * softplus(r_t[:, 8 * s : 8 * s + 8] + bias_t[:, k : k + 1])
        ) * LOG2E
        for v in range(SYM):
            lac[(d * SYM + v) * 16 + s * 8 : (d * SYM + v) * 16 + s * 8 + 8, :] = jnp.broadcast_to(
                la[:, v : v + 1], (8, CH)
            )
        code = iota((CH, CH), 0).astype(F32)
        lane = iota((CH, CH), 1) & 63
        slot = lane >> 3
        sym = (lane & 7).astype(F32)
        d0 = jnp.floor((code + 0.5) * (1.0 / 25.0))
        d01 = jnp.floor((code + 0.5) * (1.0 / 5.0))
        digits = (d0, d01 - 5.0 * d0, code - 5.0 * d01)
        hot = jnp.zeros((CH, CH), F32)
        for j in range(KW - 1):
            hot = jnp.where(
                slot == tap_row(d, j), jnp.where(sym == digits[j], 1.0, 0.0), hot
            )
        partial = nn(hot.astype(BF16), tw[q])
        last = blocks[tap_row(d, KW - 1)]
        for v in range(SYM):
            high, low = split(silu_half(partial + last[v : v + 1, :]))
            xch[(q * SYM + v) * CH : (q * SYM + v + 1) * CH, :] = high
            xcl[(q * SYM + v) * CH : (q * SYM + v + 1) * CH, :] = low


def layer_kernel(
    count, mine, tok_s, emb_h, w_in_h, cw_h, bias_h, rate_h, skip_h, gain_h, w_out_h, *others
):
    finish_layer(
        others[:count], mine, tok_s, emb_h, w_in_h, cw_h, bias_h, rate_h, skip_h, gain_h, w_out_h,
        *others[count:]
    )


def finish_layer(
    blocks, mine, tok_s, emb_h, w_in_h, cw_h, bias_h, rate_h, skip_h, gain_h, w_out_h,
    out,
    emb, w_in, cw, bias, rate, skip, gain, w_out, emb16, atab, gtab, cst, tw, zg, lac, xch, xcl,
    tok_x, tok_f, code, tri, hist, svec, xad, xbc, yad, ybc, mix,
    ring0, ring1, ring2, ring3, sems,
):
    rows = tok_x.shape[0]
    own = rows // 8
    total = tok_s.shape[0]
    nchunk = total // CH
    j = mine[0]
    size = rows // len(blocks)
    arriving = begin(
        (*blocks, emb_h, w_in_h, cw_h, bias_h, rate_h, skip_h, gain_h, w_out_h),
        (*[tok_x.at[size * m : size * m + size, :] for m in range(len(blocks))],
         emb, w_in, cw, bias, rate, skip, gain, w_out), sems)
    for copy in arriving[: len(blocks)]:
        copy.wait()
    for b in range(own):
        slot = (j ^ b) * 8
        tok_f[3, 8 * b : 8 * b + 8, :] = tok_x[pl.ds(pl.multiple_of(slot, 8), 8), :].astype(F32)
    tok = tok_f[3]
    for o in (-3, -2, -1, 1, 2, 3):
        tok_f[3 + o] = shifted(tok, o, rows)
    lane = iota((rows, CH), 1)
    row = iota((rows, CH), 0)
    lane_f = lane.astype(F32)
    before = 25.0 * tok_f[0] + 5.0 * tok_f[1] + tok_f[2]
    after = 25.0 * tok_f[6] + 5.0 * tok_f[5] + tok_f[4]
    code[0] = jnp.where((row == 0) & (lane < 3), 125.0 + lane_f, before)
    code[1] = jnp.where((row == rows - 1) & (lane >= CH - 3), lane_f, after)
    si = iota((CH, CH), 0)
    ri = iota((CH, CH), 1)
    ones = jnp.ones((CH, CH), F32)
    tri[0] = jnp.concatenate([jnp.where(si > ri, 1.0, 0.0), ones], axis=1).astype(BF16)
    tri[1] = jnp.concatenate([jnp.where(si < ri, 1.0, 0.0), ones], axis=1).astype(BF16)
    hist[...] = jnp.zeros_like(hist)
    sub8 = iota((8, CH), 0).astype(F32)
    subc = iota((CH, CH), 0).astype(F32)

    for copy in arriving[len(blocks) :]:
        copy.wait()
    symbol_tables(
        (0, 1), (zg, lac, xch, xcl),
        emb, w_in, cw, bias, rate, skip, gain, emb16, atab, gtab, cst, tw,
    )

    def block(b, off):
        side = jnp.where(b >= j, 1, 0)
        index = jnp.where(b >= j, b + 1, j - 1 - b)
        off = off * jnp.where(b == j, 0.0, 1.0)
        use_prefix = side.astype(F32)
        at = pl.ds(pl.multiple_of(index * 8, 8), 8)
        tk = tok_f[3, at, :]
        cd = code[side, at, :]
        hots = [jnp.where(tk[m : m + 1, :] == sub8, 1.0, 0.0) for m in range(8)]
        counts = nn(jnp.concatenate(hots, axis=0).astype(BF16), tri[side])
        totals = [counts[8 * m : 8 * m + 8, CH:] for m in range(8)]
        prefix = [jnp.zeros((8, CH), F32)]
        for m in range(8):
            prefix.append(prefix[-1] + totals[m])
        las = [lac[pl.ds(pl.multiple_of((side * SYM + v) * 16, 16), 16), :] for v in range(SYM)]
        acc = jnp.zeros((160, CH), F32)
        for pair in range(4):
            lefts, rights = [], []
            for m in (2 * pair, 2 * pair + 1):
                suffix = prefix[8] - prefix[m + 1]
                inside = suffix + use_prefix * (prefix[m] - suffix)
                count = counts[8 * m : 8 * m + 8, :CH] + off + inside
                exponent = las[0] * count[0:1, :]
                for v in range(1, SYM):
                    exponent = exponent + las[v] * count[v : v + 1, :]
                weight = jnp.exp2(exponent)
                masked = jnp.concatenate(
                    [jnp.where(tk[m : m + 1, :] == float(v), weight, 0.0) for v in range(SYM)],
                    axis=0,
                )
                high, low = split(masked)
                lefts.append(jnp.concatenate([high, low], axis=0))
                rights.append(jnp.where(cd[m : m + 1, :] == subc, 1.0, 0.0).astype(BF16))
            acc = acc + nt(
                jnp.concatenate(lefts, axis=1), jnp.concatenate(rights, axis=1)
            )
        hist[side] = hist[side] + acc
        return off + prefix[8]

    mine8 = pl.ds(pl.multiple_of(j * 8, 8), 8)
    shifts = [tok_f[o, mine8, :] for o in range(7)]

    def convolve(c):
        hot = window_onehot([sh[c : c + 1, :] for sh in shifts])
        for q, (d, s, k) in enumerate(CHAINS):
            x = silu_half(nn(hot, tw[q]))
            ref = (xad, xbc)[d]
            for i in range(4):
                ref[pl.ds(c * 8 * CH + s * 4 + i, CH, stride=8), :] = x[:, 128 * i : 128 * i + 128]

    if own <= 8:
        seen = jnp.zeros((8, CH), F32)
        for b in range(own - 1):
            seen = block(jnp.int32(b), seen)
            if b < nchunk:
                convolve(b)
        for c in range(own - 1, nchunk):
            convolve(c)
    else:
        lax.fori_loop(0, own - 1, block, jnp.zeros((8, CH), F32))
        for c in range(nchunk):
            convolve(c)

    last8 = rows - 8
    xs = {}
    for d in range(2):
        edge = 0 if d == 0 else 7
        seq_at = pl.ds(0 if d == 0 else last8, 8)
        hot = window_onehot([tok_f[o, seq_at, :][edge : edge + 1, :] for o in range(7)])
        for s in range(2):
            if d == 0:
                xs[s] = pltpu.roll(silu_half(nn(hot[0:16, :], tw[s]))[0:8, :], 5, 0)
            else:
                xs[2 + s] = silu_half(nn(hot[CH - 16 :, :], tw[2 + s]))[8:16, :]
    diag = iota((H, E), 0) == (iota((H, E), 1) >> 6)
    sub16 = iota((16, E), 0)
    for q in range(4):
        d, s = q // 2, q % 2
        rim = jnp.concatenate([jnp.zeros((8, E), F32), xs[q]], axis=0)
        rim_h, rim_l = split(rim)
        for v in range(SYM):
            start = (q * SYM + v) * CH
            body = slice(start, start + CH - 16)
            tail = slice(start + CH - 16, start + CH)
            tail_h = jnp.where(sub16 >= 13, rim_h.astype(F32), xch[tail, :].astype(F32))
            tail_l = jnp.where(sub16 >= 13, rim_l.astype(F32), xcl[tail, :].astype(F32))
            table_h = jnp.concatenate([xch[body, :], tail_h.astype(BF16)], axis=0)
            table_l = jnp.concatenate([xcl[body, :], tail_l.astype(BF16)], axis=0)
            at = v * 16 + s * 8
            w = hist[d, at : at + 8, :] + hist[d, 80 + at : 88 + at, :]
            high, low = split(w)
            both = jnp.concatenate([high.astype(F32), low.astype(F32)], axis=0).astype(BF16)
            one = nn(both, table_h)
            two = nn(both, table_l)
            full = one[0:8, :] + one[8:16, :] + two[0:8, :]
            vec = jnp.sum(jnp.where(diag, full, 0.0), axis=0, keepdims=True)
            for i in range(4):
                at = (d * SYM + v) * 8 + s * 4 + i
                svec[at : at + 1, :] = vec[:, 128 * i : 128 * i + 128]
    starts = []
    for d in range(2):
        for w in range(SYM):
            value = jnp.zeros((8, CH), F32)
            for v in range(SYM):
                at = (d * SYM + w) * 64 + v * 8
                sat = (d * SYM + v) * 8
                value = value + gtab[at : at + 8, :] * svec[sat : sat + 8, :]
            starts.append(value)

    skips = (cst[0:8, :], cst[8:16, :])

    def advance(d, src, t, state, ring, slot):
        u = tok_s[t]
        x = tile_at(src, t * 8)
        a = tile_at(atab, d * 64 + u * 8)
        new = [
            a * state[w] + tile_at(gtab, (d * SYM + w) * 64 + u * 8) * x for w in range(SYM)
        ]
        for w in range(SYM):
            ring[(slot * SYM + w) * 8 : (slot * SYM + w) * 8 + 8, :] = new[w]
        return new, x, u

    unroll = 128
    held = 8
    rings = ((ring0, ring1), (ring2, ring3))

    def group(g, carry):
        ya, yb = list(carry[:SYM]), list(carry[SYM:])
        for begin in range(0, unroll, held):
            ra, rb = rings[(begin // held) % 2]
            done = []
            for i in range(held):
                n = g * unroll + begin + i
                m = total - 1 - n
                ya, x0, u0 = advance(0, xad, n, ya, ra, i)
                yb, x1, u1 = advance(1, xbc, m, yb, rb, i)
                done.append((n, m, x0, x1, u0, u1))
            for i, (n, m, x0, x1, u0, u1) in enumerate(done):
                for d, ring, dest, t, x, u in ((0, ra, yad, n, x0, u0), (1, rb, ybc, m, x1, u1)):
                    y = tile_at(ring, i * SYM * 8 + u * 8) + skips[d] * x
                    dest[pl.ds(pl.multiple_of(t * 8, 8), 8), :] = y * tile_at(zg, u * 8)
        return tuple(ya + yb)

    lax.fori_loop(0, total // unroll, group, tuple(starts))

    flip = jnp.where(iota((D, D), 0) + iota((D, D), 1) == D - 1, 1.0, 0.0).astype(BF16)
    wout = w_out[...]
    wflip = nn(wout, flip).astype(BF16)
    mean = jnp.where(
        ((iota((4 * CH, 2 * CH), 0) & 255) >> 6) == (iota((4 * CH, 2 * CH), 1) >> 6), 1.0 / 64.0, 0.0
    ).astype(BF16)
    emb_rows = jnp.concatenate(
        [emb16[0:8, :], jnp.zeros((CH - 8, D), F32)], axis=0
    ).astype(BF16)
    gains = (cst[16:24, :], cst[24:32, :])
    sub = iota((8, CH), 0).astype(F32)
    mix[...] = jnp.zeros_like(mix)
    tiles = CH // SUB

    def project(c):
        base = (c & 1) * (CH * 8)
        row = tok_f[3, pl.ds(j * 8 + c, 1), :]
        hot = jnp.concatenate(
            [jnp.where(row == sub, 1.0, 0.0), jnp.zeros((CH - 8, CH), F32)], axis=0
        ).T.astype(BF16)
        parts = [mix[pl.ds(base + i, CH, stride=8), :].astype(BF16) for i in range(8)]
        one = nn(jnp.concatenate(parts[0:4], axis=1), wout).astype(BF16).astype(F32)
        two = nn(jnp.concatenate(parts[4:8], axis=1), wflip).astype(BF16).astype(F32)
        out[pl.ds(pl.multiple_of(c * CH, CH), CH), :] = (nn(hot, emb_rows) + one + two).astype(BF16)

    def tile(c, k):
        at = pl.ds(pl.multiple_of((c * CH + k * SUB) * 8, SUB * 8), SUB * 8)
        found = (yad[at, :], ybc[at, :])
        high, low = split(jnp.concatenate([g * g for g in found], axis=1))
        scale = lax.rsqrt(nn(jnp.concatenate([high, low], axis=1), mean) + EPSILON)
        normed = None
        for d in range(2):
            scaled = (found[d] * scale[:, CH * d : CH * d + CH]).reshape(SUB, 8, CH) * gains[d][None]
            normed = scaled if normed is None else normed + scaled
        at = (c & 1) * (CH * 8) + k * SUB * 8
        mix[pl.ds(pl.multiple_of(at, 8), SUB * 8), :] = normed.reshape(SUB * 8, CH)

    def chunk(c, _):
        project(jnp.maximum(c - 1, 0))
        for k in range(tiles):
            tile(c, k)
        return 0

    lax.fori_loop(0, nchunk, chunk, 0)
    project(nchunk - 1)


def per_device(
    token_ids,
    embed_table,
    input_weight_matrix,
    output_weight_matrix,
    conv_weight,
    dt_bias,
    decay_rate,
    skip_gain,
    norm_gain,
):
    length = token_ids.shape[0]
    nchunk = length // CH
    own = lax.axis_size("seq")
    tok2 = token_ids.reshape(nchunk, CH)
    rounds = own.bit_length() - 1
    rows = own * nchunk
    vm = pl.BlockSpec(memory_space=pltpu.VMEM)
    sm = pl.BlockSpec(memory_space=pltpu.SMEM)
    hbm = pl.BlockSpec(memory_space=pl.ANY)
    sds = jax.ShapeDtypeStruct
    weights = (
        embed_table, input_weight_matrix.T, conv_weight, dt_bias, decay_rate, skip_gain, norm_gain,
        output_weight_matrix,
    )

    def sent(blocks, mask):
        return lax.ppermute(blocks, "seq", [(i, i ^ mask) for i in range(own)])

    gathered = tok2
    low = max(rounds - 3, 0)
    for bit in range(low):
        gathered = jnp.concatenate([gathered, sent(gathered, 1 << bit)], axis=0)
    blocks = [gathered] + [sent(gathered, m << low) for m in range(1, own >> low)]
    mine = lax.axis_index("seq").reshape(1).astype(jnp.int32)
    table = pltpu.VMEM((4 * SYM * CH, E), BF16)
    steps = pltpu.VMEM((length * 8, CH), F32)
    ring = pltpu.VMEM((8 * SYM * 8, CH), F32)
    return pl.pallas_call(
        functools.partial(layer_kernel, len(blocks)),
        out_shape=sds((length, D), BF16),
        in_specs=[sm, sm] + [hbm] * 8 + [hbm] * len(blocks),
        out_specs=vm,
        scratch_shapes=[pltpu.VMEM(w.shape, w.dtype) for w in weights]
        + [
            pltpu.VMEM((16, D), F32),
            pltpu.VMEM((2 * 64, CH), F32),
            pltpu.VMEM((2 * SYM * 64, CH), F32),
            pltpu.VMEM((32, CH), F32),
            pltpu.VMEM((4, CH, E), BF16),
            pltpu.VMEM((64, CH), F32),
            pltpu.VMEM((2 * SYM * 16, CH), F32),
            table,
            table,
            pltpu.VMEM((rows, CH), jnp.int32),
            pltpu.VMEM((7, rows, CH), F32),
            pltpu.VMEM((2, rows, CH), F32),
            pltpu.VMEM((2, CH, 2 * CH), BF16),
            pltpu.VMEM((2, 160, CH), F32),
            pltpu.VMEM((2 * SYM * 8, CH), F32),
            steps,
            steps,
            steps,
            steps,
            pltpu.VMEM((2 * CH * 8, CH), F32),
            ring,
            ring,
            ring,
            ring,
            pltpu.SemaphoreType.DMA((8 + len(blocks),)),
        ],
        compiler_params=pltpu.CompilerParams(vmem_limit_bytes=56 * 1024 * 1024),
        cost_estimate=pl.CostEstimate(
            flops=9_000_000_000, bytes_accessed=4_000_000, transcendentals=0
        ),
        name="bidirectional_layer",
    )(mine, token_ids, *weights, *blocks)


def solution(mesh):
    placed = (P(("batch", "seq")), P(), P(), P(), P(), P(), P(), P(), P())
    return jax.shard_map(
        per_device, mesh=mesh, in_specs=placed, out_specs=P(("batch", "seq"), None), check_vma=False
    )
```

```python
import functools

import jax
import jax.numpy as jnp
from jax import lax
from jax.experimental import pallas as pl
from jax.experimental.pallas import tpu as pltpu
from jax.sharding import PartitionSpec as P

D = 256
E = 512
NS = 16
H = 8
KW = 4
SYM = 5
LOG2E = 1.4426950408889634
EPSILON = 1e-05
CH = 128
SUB = 32

F32 = jnp.float32
BF16 = jnp.bfloat16

CHAINS = ((0, 0, 0), (0, 1, 1), (1, 0, 1), (1, 1, 0))


def iota(shape, dim):
    return lax.broadcasted_iota(jnp.int32, shape, dim)


def nn(a, b, **kw):
    return lax.dot_general(a, b, (((1,), (0,)), ((), ())), preferred_element_type=F32, **kw)


def nt(a, b, **kw):
    return lax.dot_general(a, b, (((1,), (1,)), ((), ())), preferred_element_type=F32, **kw)


def split(value):
    high = value.astype(BF16)
    low = (value - high.astype(F32)).astype(BF16)
    return high, low


def softplus(x):
    return jnp.maximum(x, 0.0) + jnp.log1p(jnp.exp(-jnp.abs(x)))


def silu_half(half):
    return half + half * jnp.tanh(half)


def tap_row(direction, j):
    return j if direction == 0 else 2 * (KW - 1) - j


def window_onehot(rows):
    sub = iota((8, CH), 0).astype(F32)
    blocks = [jnp.where(row == sub, 1.0, 0.0) for row in rows]
    blocks.append(jnp.zeros((8, CH), F32))
    stacked = jnp.concatenate(blocks + blocks, axis=0)
    return stacked.T.astype(BF16)


def shifted(tok, offset, rows):
    if offset == 0:
        return tok
    lane = iota((rows, CH), 1)
    row = iota((rows, CH), 0)
    moved = pltpu.roll(tok, (-offset) % CH, 1)
    if offset < 0:
        other = pltpu.roll(moved, 1, 0)
        crossing = lane < -offset
        outside = crossing & (row == 0)
    else:
        other = pltpu.roll(moved, rows - 1, 0)
        crossing = lane >= CH - offset
        outside = crossing & (row == rows - 1)
    return jnp.where(outside, 5.0, jnp.where(crossing, other, moved))


def pick(values, u):
    low = (u & 1) == 1
    first = jnp.where(low, values[1], values[0])
    second = jnp.where(low, values[3], values[2])
    return jnp.where(u > 3, values[4], jnp.where((u & 2) == 2, second, first))


def tile_at(ref, row):
    return ref[pl.ds(pl.multiple_of(row, 8), 8), :]


def begin(sources, targets, sems):
    copies = [
        pltpu.make_async_copy(a, b, sems.at[i]) for i, (a, b) in enumerate(zip(sources, targets))
    ]
    for copy in copies:
        copy.start()
    return copies


def symbol_tables(
    directions, full, emb, w_in, cw, bias, rate, skip, gain, emb16, atab, gtab, cst, tw
):
    highest = lax.Precision.HIGHEST
    emb16[...] = jnp.zeros_like(emb16)
    e32 = emb[...].astype(F32)
    emb16[0:SYM, :] = e32
    for v in range(4):
        emb16[8 + v : 9 + v, :] = e32[3 - v : 4 - v, :]
    emb16[12:13, :] = e32[4:5, :]
    embs = emb16[...].astype(BF16)
    x16 = nt(embs, w_in[E : 2 * E, :]).astype(BF16).astype(F32)
    rest = nt(embs, w_in[2 * E :, :]).astype(BF16)
    nrest = 2 * NS + H
    expand = jnp.where(
        iota((nrest, E), 0) == (iota((nrest, E), 1) >> 6) + 2 * NS, 1.0, 0.0
    ).astype(BF16)
    heads = jnp.where(iota((H, E), 0) == (iota((H, E), 1) >> 6), 1.0, 0.0)
    r_exp = nn(rest, expand)
    bias_e = nn(bias[...], heads, precision=highest)
    rate_e = nn(rate[...], heads, precision=highest)
    skip_e = nn(skip[...], heads, precision=highest)
    shift = jnp.where(
        iota((nrest, nrest), 0) + NS == iota((nrest, nrest), 1),
        jnp.where(iota((nrest, nrest), 0) < NS, 1.0, 0.0),
        0.0,
    ).astype(BF16)
    rest_b = nn(rest, shift).astype(BF16)
    cb = nt(rest_b, rest)
    if full is not None:
        zg, lac, xch, xcl = full
        z16 = nt(embs, w_in[0:E, :]).astype(BF16).astype(F32)
        sz = z16 * (0.5 + 0.5 * jnp.tanh(0.5 * z16))
        for s in range(2):
            for i in range(4):
                zg[pl.ds(s * 4 + i, 8, stride=8), :] = sz[8 * s : 8 * s + 8, 128 * i : 128 * i + 128]
        pick_r = jnp.where(
            iota((H, nrest), 0) + 2 * NS == iota((H, nrest), 1), 1.0, 0.0
        ).astype(BF16)
        r_t = nt(pick_r, rest)
        eye = jnp.where(iota((H, H), 0) == iota((H, H), 1), 1.0, 0.0)
        bias_t = nt(eye, bias[...], precision=highest)
        rate_t = nt(eye, rate[...], precision=highest)
    for q, (d, s, k) in enumerate(CHAINS):
        if d not in directions:
            continue
        dt = softplus(r_exp[8 * s : 8 * s + 8, :] + bias_e[k : k + 1, :])
        a = jnp.exp(-rate_e[k : k + 1, :] * dt)
        for i in range(4):
            lanes = slice(128 * i, 128 * i + 128)
            atab[pl.ds(d * 64 + s * 4 + i, 8, stride=8), :] = a[:, lanes]
            cst[d * 8 + s * 4 + i : d * 8 + s * 4 + i + 1, :] = skip_e[k : k + 1, lanes]
            cst[16 + d * 8 + s * 4 + i : 17 + d * 8 + s * 4 + i, :] = gain[k : k + 1, lanes]
        for u in range(SYM):
            g = cb[8 * s : 8 * s + 8, 8 * s + u : 8 * s + u + 1] * dt
            for i in range(4):
                gtab[pl.ds((d * SYM + u) * 64 + s * 4 + i, 8, stride=8), :] = g[
                    :, 128 * i : 128 * i + 128
                ]
        xs = x16[8 * s : 8 * s + 8, :]
        blocks = [jnp.zeros((8, E), F32)] * 8
        for j in range(KW):
            blocks[tap_row(d, j)] = (0.5 * cw[k, j : j + 1, :]) * xs
        high, low = split(jnp.concatenate(blocks, axis=0))
        tw[q, 0:64, :] = high
        tw[q, 64:128, :] = low
        if full is None:
            continue
        la = (
            -rate_t[:, k : k + 1] * softplus(r_t[:, 8 * s : 8 * s + 8] + bias_t[:, k : k + 1])
        ) * LOG2E
        for v in range(SYM):
            lac[(d * SYM + v) * 16 + s * 8 : (d * SYM + v) * 16 + s * 8 + 8, :] = jnp.broadcast_to(
                la[:, v : v + 1], (8, CH)
            )
        code = iota((CH, CH), 0).astype(F32)
        lane = iota((CH, CH), 1) & 63
        slot = lane >> 3
        sym = (lane & 7).astype(F32)
        d0 = jnp.floor((code + 0.5) * (1.0 / 25.0))
        d01 = jnp.floor((code + 0.5) * (1.0 / 5.0))
        digits = (d0, d01 - 5.0 * d0, code - 5.0 * d01)
        hot = jnp.zeros((CH, CH), F32)
        for j in range(KW - 1):
            hot = jnp.where(
                slot == tap_row(d, j), jnp.where(sym == digits[j], 1.0, 0.0), hot
            )
        partial = nn(hot.astype(BF16), tw[q])
        last = blocks[tap_row(d, KW - 1)]
        for v in range(SYM):
            high, low = split(silu_half(partial + last[v : v + 1, :]))
            xch[(q * SYM + v) * CH : (q * SYM + v + 1) * CH, :] = high
            xcl[(q * SYM + v) * CH : (q * SYM + v + 1) * CH, :] = low


def layer_kernel(
    count, mine, tok_s, emb_h, w_in_h, cw_h, bias_h, rate_h, skip_h, gain_h, w_out_h, *others
):
    finish_layer(
        others[:count], mine, tok_s, emb_h, w_in_h, cw_h, bias_h, rate_h, skip_h, gain_h, w_out_h,
        *others[count:]
    )


def finish_layer(
    blocks, mine, tok_s, emb_h, w_in_h, cw_h, bias_h, rate_h, skip_h, gain_h, w_out_h,
    out,
    emb, w_in, cw, bias, rate, skip, gain, w_out, emb16, atab, gtab, cst, tw, zg, lac, xch, xcl,
    tok_x, tok_f, code, tri, hist, svec, xad, xbc, yad, ybc, mix,
    tab, ring0, ring1, ring2, ring3, sems,
):
    rows = tok_x.shape[0]
    own = rows // 8
    total = tok_s.shape[0]
    nchunk = total // CH
    j = mine[0]
    size = rows // len(blocks)
    arriving = begin(
        (*blocks, emb_h, w_in_h, cw_h, bias_h, rate_h, skip_h, gain_h, w_out_h),
        (*[tok_x.at[size * m : size * m + size, :] for m in range(len(blocks))],
         emb, w_in, cw, bias, rate, skip, gain, w_out), sems)
    for copy in arriving[: len(blocks)]:
        copy.wait()
    for b in range(own):
        slot = (j ^ b) * 8
        tok_f[3, 8 * b : 8 * b + 8, :] = tok_x[pl.ds(pl.multiple_of(slot, 8), 8), :].astype(F32)
    tok = tok_f[3]
    for o in (-3, -2, -1, 1, 2, 3):
        tok_f[3 + o] = shifted(tok, o, rows)
    lane = iota((rows, CH), 1)
    row = iota((rows, CH), 0)
    lane_f = lane.astype(F32)
    before = 25.0 * tok_f[0] + 5.0 * tok_f[1] + tok_f[2]
    after = 25.0 * tok_f[6] + 5.0 * tok_f[5] + tok_f[4]
    code[0] = jnp.where((row == 0) & (lane < 3), 125.0 + lane_f, before)
    code[1] = jnp.where((row == rows - 1) & (lane >= CH - 3), lane_f, after)
    si = iota((CH, CH), 0)
    ri = iota((CH, CH), 1)
    ones = jnp.ones((CH, CH), F32)
    tri[0] = jnp.concatenate([jnp.where(si > ri, 1.0, 0.0), ones], axis=1).astype(BF16)
    tri[1] = jnp.concatenate([jnp.where(si < ri, 1.0, 0.0), ones], axis=1).astype(BF16)
    hist[...] = jnp.zeros_like(hist)
    sub8 = iota((8, CH), 0).astype(F32)
    subc = iota((CH, CH), 0).astype(F32)

    for copy in arriving[len(blocks) :]:
        copy.wait()
    symbol_tables(
        (0, 1), (zg, lac, xch, xcl),
        emb, w_in, cw, bias, rate, skip, gain, emb16, atab, gtab, cst, tw,
    )

    def block(b, off):
        side = jnp.where(b >= j, 1, 0)
        index = jnp.where(b >= j, b + 1, j - 1 - b)
        off = off * jnp.where(b == j, 0.0, 1.0)
        use_prefix = side.astype(F32)
        at = pl.ds(pl.multiple_of(index * 8, 8), 8)
        tk = tok_f[3, at, :]
        cd = code[side, at, :]
        hots = [jnp.where(tk[m : m + 1, :] == sub8, 1.0, 0.0) for m in range(8)]
        counts = nn(jnp.concatenate(hots, axis=0).astype(BF16), tri[side])
        totals = [counts[8 * m : 8 * m + 8, CH:] for m in range(8)]
        prefix = [jnp.zeros((8, CH), F32)]
        for m in range(8):
            prefix.append(prefix[-1] + totals[m])
        las = [lac[pl.ds(pl.multiple_of((side * SYM + v) * 16, 16), 16), :] for v in range(SYM)]
        acc = jnp.zeros((160, CH), F32)
        for pair in range(4):
            lefts, rights = [], []
            for m in (2 * pair, 2 * pair + 1):
                suffix = prefix[8] - prefix[m + 1]
                inside = suffix + use_prefix * (prefix[m] - suffix)
                count = counts[8 * m : 8 * m + 8, :CH] + off + inside
                exponent = las[0] * count[0:1, :]
                for v in range(1, SYM):
                    exponent = exponent + las[v] * count[v : v + 1, :]
                weight = jnp.exp2(exponent)
                masked = jnp.concatenate(
                    [jnp.where(tk[m : m + 1, :] == float(v), weight, 0.0) for v in range(SYM)],
                    axis=0,
                )
                high, low = split(masked)
                lefts.append(jnp.concatenate([high, low], axis=0))
                rights.append(jnp.where(cd[m : m + 1, :] == subc, 1.0, 0.0).astype(BF16))
            acc = acc + nt(
                jnp.concatenate(lefts, axis=1), jnp.concatenate(rights, axis=1)
            )
        hist[side] = hist[side] + acc
        return off + prefix[8]

    mine8 = pl.ds(pl.multiple_of(j * 8, 8), 8)
    shifts = [tok_f[o, mine8, :] for o in range(7)]

    def convolve(c):
        hot = window_onehot([sh[c : c + 1, :] for sh in shifts])
        for q, (d, s, k) in enumerate(CHAINS):
            x = silu_half(nn(hot, tw[q]))
            ref = (xad, xbc)[d]
            for i in range(4):
                ref[pl.ds(c * 8 * CH + s * 4 + i, CH, stride=8), :] = x[:, 128 * i : 128 * i + 128]

    if own <= 8:
        seen = jnp.zeros((8, CH), F32)
        for b in range(own - 1):
            seen = block(jnp.int32(b), seen)
            if b < nchunk:
                convolve(b)
        for c in range(own - 1, nchunk):
            convolve(c)
    else:
        lax.fori_loop(0, own - 1, block, jnp.zeros((8, CH), F32))
        for c in range(nchunk):
            convolve(c)

    last8 = rows - 8
    xs = {}
    for d in range(2):
        edge = 0 if d == 0 else 7
        seq_at = pl.ds(0 if d == 0 else last8, 8)
        hot = window_onehot([tok_f[o, seq_at, :][edge : edge + 1, :] for o in range(7)])
        for s in range(2):
            if d == 0:
                xs[s] = pltpu.roll(silu_half(nn(hot[0:16, :], tw[s]))[0:8, :], 5, 0)
            else:
                xs[2 + s] = silu_half(nn(hot[CH - 16 :, :], tw[2 + s]))[8:16, :]
    diag = iota((H, E), 0) == (iota((H, E), 1) >> 6)
    sub16 = iota((16, E), 0)
    for q in range(4):
        d, s = q // 2, q % 2
        rim = jnp.concatenate([jnp.zeros((8, E), F32), xs[q]], axis=0)
        rim_h, rim_l = split(rim)
        for v in range(SYM):
            start = (q * SYM + v) * CH
            body = slice(start, start + CH - 16)
            tail = slice(start + CH - 16, start + CH)
            tail_h = jnp.where(sub16 >= 13, rim_h.astype(F32), xch[tail, :].astype(F32))
            tail_l = jnp.where(sub16 >= 13, rim_l.astype(F32), xcl[tail, :].astype(F32))
            table_h = jnp.concatenate([xch[body, :], tail_h.astype(BF16)], axis=0)
            table_l = jnp.concatenate([xcl[body, :], tail_l.astype(BF16)], axis=0)
            at = v * 16 + s * 8
            w = hist[d, at : at + 8, :] + hist[d, 80 + at : 88 + at, :]
            high, low = split(w)
            both = jnp.concatenate([high.astype(F32), low.astype(F32)], axis=0).astype(BF16)
            one = nn(both, table_h)
            two = nn(both, table_l)
            full = one[0:8, :] + one[8:16, :] + two[0:8, :]
            vec = jnp.sum(jnp.where(diag, full, 0.0), axis=0, keepdims=True)
            for i in range(4):
                at = (d * SYM + v) * 8 + s * 4 + i
                svec[at : at + 1, :] = vec[:, 128 * i : 128 * i + 128]
    starts = []
    for d in range(2):
        for w in range(SYM):
            value = jnp.zeros((8, CH), F32)
            for v in range(SYM):
                at = (d * SYM + w) * 64 + v * 8
                sat = (d * SYM + v) * 8
                value = value + gtab[at : at + 8, :] * svec[sat : sat + 8, :]
            starts.append(value)

    skips = (cst[0:8, :], cst[8:16, :])

    for d in range(2):
        for u in range(SYM):
            at = (d * SYM + u) * 64
            tab[at : at + 8, :] = atab[d * 64 + u * 8 : d * 64 + u * 8 + 8, :]
            for w in range(SYM):
                row = (d * SYM + w) * 64 + u * 8
                tab[at + 8 + w * 8 : at + 16 + w * 8, :] = gtab[row : row + 8, :]
            tab[at + 48 : at + 56, :] = zg[u * 8 : u * 8 + 8, :]

    def rows8(ref, k):
        return ref[k * 8 : k * 8 + 8, :]

    unroll = 128
    held = 8
    rings = ((ring0, ring1), (ring2, ring3))

    def group(g, carry):
        states = [list(carry[:SYM]), list(carry[SYM:])]
        firsts = (g * unroll, total - (g + 1) * unroll)
        spans = [pl.ds(pl.multiple_of(f * 8, unroll * 8), unroll * 8) for f in firsts]
        sources = (xad.at[spans[0], :], xbc.at[spans[1], :])
        targets = (yad.at[spans[0], :], ybc.at[spans[1], :])
        for begin in range(0, unroll, held):
            pair = rings[(begin // held) % 2]
            done = []
            for i in range(held):
                for d in range(2):
                    n = begin + i
                    local = n if d == 0 else unroll - 1 - n
                    u = tok_s[firsts[d] + local]
                    part = tab.at[pl.ds(pl.multiple_of((d * SYM + u) * 64, 64), 64), :]
                    x = rows8(sources[d], local)
                    a = rows8(part, 0)
                    states[d] = [a * states[d][w] + rows8(part, 1 + w) * x for w in range(SYM)]
                    for w in range(SYM):
                        pair[d][(i * SYM + w) * 8 : (i * SYM + w) * 8 + 8, :] = states[d][w]
                    done.append((d, i, local, x, u, part))
            for d, i, local, x, u, part in done:
                y = tile_at(pair[d], i * SYM * 8 + u * 8) + skips[d] * x
                targets[d][local * 8 : local * 8 + 8, :] = y * rows8(part, 6)
        return tuple(states[0] + states[1])

    lax.fori_loop(0, total // unroll, group, tuple(starts))

    flip = jnp.where(iota((D, D), 0) + iota((D, D), 1) == D - 1, 1.0, 0.0).astype(BF16)
    wout = w_out[...]
    wflip = nn(wout, flip).astype(BF16)
    mean = jnp.where(
        ((iota((4 * CH, 2 * CH), 0) & 255) >> 6) == (iota((4 * CH, 2 * CH), 1) >> 6), 1.0 / 64.0, 0.0
    ).astype(BF16)
    emb_rows = jnp.concatenate(
        [emb16[0:8, :], jnp.zeros((CH - 8, D), F32)], axis=0
    ).astype(BF16)
    gains = (cst[16:24, :], cst[24:32, :])
    sub = iota((8, CH), 0).astype(F32)
    mix[...] = jnp.zeros_like(mix)
    tiles = CH // SUB

    def project(c):
        base = (c & 1) * (CH * 8)
        row = tok_f[3, pl.ds(j * 8 + c, 1), :]
        hot = jnp.concatenate(
            [jnp.where(row == sub, 1.0, 0.0), jnp.zeros((CH - 8, CH), F32)], axis=0
        ).T.astype(BF16)
        parts = [mix[pl.ds(base + i, CH, stride=8), :].astype(BF16) for i in range(8)]
        one = nn(jnp.concatenate(parts[0:4], axis=1), wout).astype(BF16).astype(F32)
        two = nn(jnp.concatenate(parts[4:8], axis=1), wflip).astype(BF16).astype(F32)
        out[pl.ds(pl.multiple_of(c * CH, CH), CH), :] = (nn(hot, emb_rows) + one + two).astype(BF16)

    def tile(c, k):
        at = pl.ds(pl.multiple_of((c * CH + k * SUB) * 8, SUB * 8), SUB * 8)
        found = (yad[at, :], ybc[at, :])
        high, low = split(jnp.concatenate([g * g for g in found], axis=1))
        scale = lax.rsqrt(nn(jnp.concatenate([high, low], axis=1), mean) + EPSILON)
        normed = None
        for d in range(2):
            scaled = (found[d] * scale[:, CH * d : CH * d + CH]).reshape(SUB, 8, CH) * gains[d][None]
            normed = scaled if normed is None else normed + scaled
        at = (c & 1) * (CH * 8) + k * SUB * 8
        mix[pl.ds(pl.multiple_of(at, 8), SUB * 8), :] = normed.reshape(SUB * 8, CH)

    def chunk(c, _):
        project(jnp.maximum(c - 1, 0))
        for k in range(tiles):
            tile(c, k)
        return 0

    lax.fori_loop(0, nchunk, chunk, 0)
    project(nchunk - 1)


def per_device(
    token_ids,
    embed_table,
    input_weight_matrix,
    output_weight_matrix,
    conv_weight,
    dt_bias,
    decay_rate,
    skip_gain,
    norm_gain,
):
    length = token_ids.shape[0]
    nchunk = length // CH
    own = lax.axis_size("seq")
    tok2 = token_ids.reshape(nchunk, CH)
    rounds = own.bit_length() - 1
    rows = own * nchunk
    vm = pl.BlockSpec(memory_space=pltpu.VMEM)
    sm = pl.BlockSpec(memory_space=pltpu.SMEM)
    hbm = pl.BlockSpec(memory_space=pl.ANY)
    sds = jax.ShapeDtypeStruct
    weights = (
        embed_table, input_weight_matrix.T, conv_weight, dt_bias, decay_rate, skip_gain, norm_gain,
        output_weight_matrix,
    )

    def sent(blocks, mask):
        return lax.ppermute(blocks, "seq", [(i, i ^ mask) for i in range(own)])

    gathered = tok2
    low = max(rounds - 3, 0)
    for bit in range(low):
        gathered = jnp.concatenate([gathered, sent(gathered, 1 << bit)], axis=0)
    blocks = [gathered] + [sent(gathered, m << low) for m in range(1, own >> low)]
    mine = lax.axis_index("seq").reshape(1).astype(jnp.int32)
    table = pltpu.VMEM((4 * SYM * CH, E), BF16)
    steps = pltpu.VMEM((length * 8, CH), F32)
    ring = pltpu.VMEM((8 * SYM * 8, CH), F32)
    return pl.pallas_call(
        functools.partial(layer_kernel, len(blocks)),
        out_shape=sds((length, D), BF16),
        in_specs=[sm, sm] + [hbm] * 8 + [hbm] * len(blocks),
        out_specs=vm,
        scratch_shapes=[pltpu.VMEM(w.shape, w.dtype) for w in weights]
        + [
            pltpu.VMEM((16, D), F32),
            pltpu.VMEM((2 * 64, CH), F32),
            pltpu.VMEM((2 * SYM * 64, CH), F32),
            pltpu.VMEM((32, CH), F32),
            pltpu.VMEM((4, CH, E), BF16),
            pltpu.VMEM((64, CH), F32),
            pltpu.VMEM((2 * SYM * 16, CH), F32),
            table,
            table,
            pltpu.VMEM((rows, CH), jnp.int32),
            pltpu.VMEM((7, rows, CH), F32),
            pltpu.VMEM((2, rows, CH), F32),
            pltpu.VMEM((2, CH, 2 * CH), BF16),
            pltpu.VMEM((2, 160, CH), F32),
            pltpu.VMEM((2 * SYM * 8, CH), F32),
            steps,
            steps,
            steps,
            steps,
            pltpu.VMEM((2 * CH * 8, CH), F32),
            pltpu.VMEM((2 * SYM * 64, CH), F32),
            ring,
            ring,
            ring,
            ring,
            pltpu.SemaphoreType.DMA((8 + len(blocks),)),
        ],
        compiler_params=pltpu.CompilerParams(vmem_limit_bytes=56 * 1024 * 1024),
        cost_estimate=pl.CostEstimate(
            flops=9_000_000_000, bytes_accessed=4_000_000, transcendentals=0
        ),
        name="bidirectional_layer",
    )(mine, token_ids, *weights, *blocks)


def solution(mesh):
    placed = (P(("batch", "seq")), P(), P(), P(), P(), P(), P(), P(), P())
    return jax.shard_map(
        per_device, mesh=mesh, in_specs=placed, out_specs=P(("batch", "seq"), None), check_vma=False
    )
```

```python
import functools

import jax
import jax.numpy as jnp
from jax import lax
from jax.experimental import pallas as pl
from jax.experimental.pallas import tpu as pltpu
from jax.sharding import PartitionSpec as P

D = 256
E = 512
NS = 16
H = 8
KW = 4
SYM = 5
LOG2E = 1.4426950408889634
EPSILON = 1e-05
CH = 128
SUB = 32

F32 = jnp.float32
BF16 = jnp.bfloat16

CHAINS = ((0, 0, 0), (0, 1, 1), (1, 0, 1), (1, 1, 0))


def iota(shape, dim):
    return lax.broadcasted_iota(jnp.int32, shape, dim)


def nn(a, b, **kw):
    return lax.dot_general(a, b, (((1,), (0,)), ((), ())), preferred_element_type=F32, **kw)


def nt(a, b, **kw):
    return lax.dot_general(a, b, (((1,), (1,)), ((), ())), preferred_element_type=F32, **kw)


def split(value):
    high = value.astype(BF16)
    low = (value - high.astype(F32)).astype(BF16)
    return high, low


def softplus(x):
    return jnp.maximum(x, 0.0) + jnp.log1p(jnp.exp(-jnp.abs(x)))


def silu_half(half):
    return half + half * jnp.tanh(half)


def tap_row(direction, j):
    return j if direction == 0 else 2 * (KW - 1) - j


def window_onehot(rows):
    sub = iota((8, CH), 0).astype(F32)
    blocks = [jnp.where(row == sub, 1.0, 0.0) for row in rows]
    blocks.append(jnp.zeros((8, CH), F32))
    stacked = jnp.concatenate(blocks + blocks, axis=0)
    return stacked.T.astype(BF16)


def shifted(tok, offset, rows):
    if offset == 0:
        return tok
    lane = iota((rows, CH), 1)
    row = iota((rows, CH), 0)
    moved = pltpu.roll(tok, (-offset) % CH, 1)
    if offset < 0:
        other = pltpu.roll(moved, 1, 0)
        crossing = lane < -offset
        outside = crossing & (row == 0)
    else:
        other = pltpu.roll(moved, rows - 1, 0)
        crossing = lane >= CH - offset
        outside = crossing & (row == rows - 1)
    return jnp.where(outside, 5.0, jnp.where(crossing, other, moved))


def pick(values, u):
    low = (u & 1) == 1
    first = jnp.where(low, values[1], values[0])
    second = jnp.where(low, values[3], values[2])
    return jnp.where(u > 3, values[4], jnp.where((u & 2) == 2, second, first))


def tile_at(ref, row):
    return ref[pl.ds(pl.multiple_of(row, 8), 8), :]


def begin(sources, targets, sems):
    copies = [
        pltpu.make_async_copy(a, b, sems.at[i]) for i, (a, b) in enumerate(zip(sources, targets))
    ]
    for copy in copies:
        copy.start()
    return copies


def symbol_tables(
    directions, full, emb, w_in, cw, bias, rate, skip, gain, emb16, atab, gtab, cst, tw
):
    highest = lax.Precision.HIGHEST
    emb16[...] = jnp.zeros_like(emb16)
    e32 = emb[...].astype(F32)
    emb16[0:SYM, :] = e32
    for v in range(4):
        emb16[8 + v : 9 + v, :] = e32[3 - v : 4 - v, :]
    emb16[12:13, :] = e32[4:5, :]
    embs = emb16[...].astype(BF16)
    x16 = nt(embs, w_in[E : 2 * E, :]).astype(BF16).astype(F32)
    rest = nt(embs, w_in[2 * E :, :]).astype(BF16)
    nrest = 2 * NS + H
    expand = jnp.where(
        iota((nrest, E), 0) == (iota((nrest, E), 1) >> 6) + 2 * NS, 1.0, 0.0
    ).astype(BF16)
    heads = jnp.where(iota((H, E), 0) == (iota((H, E), 1) >> 6), 1.0, 0.0)
    r_exp = nn(rest, expand)
    bias_e = nn(bias[...], heads, precision=highest)
    rate_e = nn(rate[...], heads, precision=highest)
    skip_e = nn(skip[...], heads, precision=highest)
    shift = jnp.where(
        iota((nrest, nrest), 0) + NS == iota((nrest, nrest), 1),
        jnp.where(iota((nrest, nrest), 0) < NS, 1.0, 0.0),
        0.0,
    ).astype(BF16)
    rest_b = nn(rest, shift).astype(BF16)
    cb = nt(rest_b, rest)
    if full is not None:
        zg, lac, xch, xcl, done = full
        z16 = nt(embs, w_in[0:E, :]).astype(BF16).astype(F32)
        sz = z16 * (0.5 + 0.5 * jnp.tanh(0.5 * z16))
        for s in range(2):
            for i in range(4):
                zg[pl.ds(s * 4 + i, 8, stride=8), :] = sz[8 * s : 8 * s + 8, 128 * i : 128 * i + 128]
        pick_r = jnp.where(
            iota((H, nrest), 0) + 2 * NS == iota((H, nrest), 1), 1.0, 0.0
        ).astype(BF16)
        r_t = nt(pick_r, rest)
        eye = jnp.where(iota((H, H), 0) == iota((H, H), 1), 1.0, 0.0)
        bias_t = nt(eye, bias[...], precision=highest)
        rate_t = nt(eye, rate[...], precision=highest)
    for q, (d, s, k) in enumerate(CHAINS):
        if d not in directions:
            continue
        dt = softplus(r_exp[8 * s : 8 * s + 8, :] + bias_e[k : k + 1, :])
        a = jnp.exp(-rate_e[k : k + 1, :] * dt)
        for i in range(4):
            lanes = slice(128 * i, 128 * i + 128)
            atab[pl.ds(d * 64 + s * 4 + i, 8, stride=8), :] = a[:, lanes]
            cst[d * 8 + s * 4 + i : d * 8 + s * 4 + i + 1, :] = skip_e[k : k + 1, lanes]
            cst[16 + d * 8 + s * 4 + i : 17 + d * 8 + s * 4 + i, :] = gain[k : k + 1, lanes]
        for u in range(SYM):
            g = cb[8 * s : 8 * s + 8, 8 * s + u : 8 * s + u + 1] * dt
            for i in range(4):
                gtab[pl.ds((d * SYM + u) * 64 + s * 4 + i, 8, stride=8), :] = g[
                    :, 128 * i : 128 * i + 128
                ]
        xs = x16[8 * s : 8 * s + 8, :]
        blocks = [jnp.zeros((8, E), F32)] * 8
        for j in range(KW):
            blocks[tap_row(d, j)] = (0.5 * cw[k, j : j + 1, :]) * xs
        high, low = split(jnp.concatenate(blocks, axis=0))
        tw[q, 0:64, :] = high
        tw[q, 64:128, :] = low
        if full is None:
            continue
        la = (
            -rate_t[:, k : k + 1] * softplus(r_t[:, 8 * s : 8 * s + 8] + bias_t[:, k : k + 1])
        ) * LOG2E
        for v in range(SYM):
            lac[(d * SYM + v) * 16 + s * 8 : (d * SYM + v) * 16 + s * 8 + 8, :] = jnp.broadcast_to(
                la[:, v : v + 1], (8, CH)
            )
        code = iota((CH, CH), 0).astype(F32)
        lane = iota((CH, CH), 1) & 63
        slot = lane >> 3
        sym = (lane & 7).astype(F32)
        d0 = jnp.floor((code + 0.5) * (1.0 / 25.0))
        d01 = jnp.floor((code + 0.5) * (1.0 / 5.0))
        digits = (d0, d01 - 5.0 * d0, code - 5.0 * d01)
        hot = jnp.zeros((CH, CH), F32)
        for j in range(KW - 1):
            hot = jnp.where(
                slot == tap_row(d, j), jnp.where(sym == digits[j], 1.0, 0.0), hot
            )
        partial = nn(hot.astype(BF16), tw[q])
        last = blocks[tap_row(d, KW - 1)]
        for v in range(SYM):
            high, low = split(silu_half(partial + last[v : v + 1, :]))
            xch[(q * SYM + v) * CH : (q * SYM + v + 1) * CH, :] = high
            xcl[(q * SYM + v) * CH : (q * SYM + v + 1) * CH, :] = low
        done(q)


def table_kernel(
    emb_h, w_in_h, cw_h, bias_h, rate_h, skip_h, gain_h,
    tab, cst, lac, tw, emb16, xch_h, xcl_h,
    emb, w_in, cw, bias, rate, skip, gain, atab, gtab, zg, xch, xcl, sems, out_sems,
):
    for copy in begin((emb_h, w_in_h, cw_h, bias_h, rate_h, skip_h, gain_h),
                      (emb, w_in, cw, bias, rate, skip, gain), sems):
        copy.wait()
    part = SYM * CH
    leaving = []

    def done(q):
        rows = slice(q * part, (q + 1) * part)
        for i, (source, target) in enumerate(((xch, xch_h), (xcl, xcl_h))):
            copy = pltpu.make_async_copy(source.at[rows, :], target.at[rows, :], out_sems.at[i, q])
            copy.start()
            leaving.append(copy)

    symbol_tables(
        (0, 1), (zg, lac, xch, xcl, done),
        emb, w_in, cw, bias, rate, skip, gain, emb16, atab, gtab, cst, tw,
    )
    for d in range(2):
        for u in range(SYM):
            at = (d * SYM + u) * 64
            tab[at : at + 8, :] = atab[d * 64 + u * 8 : d * 64 + u * 8 + 8, :]
            for w in range(SYM):
                row = (d * SYM + w) * 64 + u * 8
                tab[at + 8 + w * 8 : at + 16 + w * 8, :] = gtab[row : row + 8, :]
            tab[at + 48 : at + 56, :] = zg[u * 8 : u * 8 + 8, :]
    for copy in leaving:
        copy.wait()


def layer_kernel(count, mine, tok_s, *others):
    finish_layer(others[:count], mine, tok_s, *others[count:])


def finish_layer(
    blocks, mine, tok_s, tab_h, cst_h, lac_h, tw_h, emb16_h, w_out_h, xch_h, xcl_h,
    out,
    tab, cst, lac, tw, emb16, w_out, xch, xcl,
    tok_x, tok_f, code, tri, hist, svec, xad, xbc, yad, ybc, mix,
    ring0, ring1, ring2, ring3, sems,
):
    rows = tok_x.shape[0]
    own = rows // 8
    total = tok_s.shape[0]
    nchunk = total // CH
    j = mine[0]
    size = rows // len(blocks)
    arriving = begin(
        (*blocks, lac_h, tw_h, tab_h, cst_h, emb16_h, w_out_h, xch_h, xcl_h),
        (*[tok_x.at[size * m : size * m + size, :] for m in range(len(blocks))],
         lac, tw, tab, cst, emb16, w_out, xch, xcl), sems)
    for copy in arriving[: len(blocks)]:
        copy.wait()
    for b in range(own):
        slot = (j ^ b) * 8
        tok_f[3, 8 * b : 8 * b + 8, :] = tok_x[pl.ds(pl.multiple_of(slot, 8), 8), :].astype(F32)
    tok = tok_f[3]
    for o in (-3, -2, -1, 1, 2, 3):
        tok_f[3 + o] = shifted(tok, o, rows)
    lane = iota((rows, CH), 1)
    row = iota((rows, CH), 0)
    lane_f = lane.astype(F32)
    before = 25.0 * tok_f[0] + 5.0 * tok_f[1] + tok_f[2]
    after = 25.0 * tok_f[6] + 5.0 * tok_f[5] + tok_f[4]
    code[0] = jnp.where((row == 0) & (lane < 3), 125.0 + lane_f, before)
    code[1] = jnp.where((row == rows - 1) & (lane >= CH - 3), lane_f, after)
    si = iota((CH, CH), 0)
    ri = iota((CH, CH), 1)
    ones = jnp.ones((CH, CH), F32)
    tri[0] = jnp.concatenate([jnp.where(si > ri, 1.0, 0.0), ones], axis=1).astype(BF16)
    tri[1] = jnp.concatenate([jnp.where(si < ri, 1.0, 0.0), ones], axis=1).astype(BF16)
    hist[...] = jnp.zeros_like(hist)
    sub8 = iota((8, CH), 0).astype(F32)
    subc = iota((CH, CH), 0).astype(F32)

    for copy in arriving[len(blocks) : len(blocks) + 6]:
        copy.wait()

    def block(b, off):
        side = jnp.where(b >= j, 1, 0)
        index = jnp.where(b >= j, b + 1, j - 1 - b)
        off = off * jnp.where(b == j, 0.0, 1.0)
        use_prefix = side.astype(F32)
        at = pl.ds(pl.multiple_of(index * 8, 8), 8)
        tk = tok_f[3, at, :]
        cd = code[side, at, :]
        hots = [jnp.where(tk[m : m + 1, :] == sub8, 1.0, 0.0) for m in range(8)]
        counts = nn(jnp.concatenate(hots, axis=0).astype(BF16), tri[side])
        totals = [counts[8 * m : 8 * m + 8, CH:] for m in range(8)]
        prefix = [jnp.zeros((8, CH), F32)]
        for m in range(8):
            prefix.append(prefix[-1] + totals[m])
        las = [lac[pl.ds(pl.multiple_of((side * SYM + v) * 16, 16), 16), :] for v in range(SYM)]
        acc = jnp.zeros((160, CH), F32)
        for pair in range(4):
            lefts, rights = [], []
            for m in (2 * pair, 2 * pair + 1):
                suffix = prefix[8] - prefix[m + 1]
                inside = suffix + use_prefix * (prefix[m] - suffix)
                count = counts[8 * m : 8 * m + 8, :CH] + off + inside
                exponent = las[0] * count[0:1, :]
                for v in range(1, SYM):
                    exponent = exponent + las[v] * count[v : v + 1, :]
                weight = jnp.exp2(exponent)
                masked = jnp.concatenate(
                    [jnp.where(tk[m : m + 1, :] == float(v), weight, 0.0) for v in range(SYM)],
                    axis=0,
                )
                high, low = split(masked)
                lefts.append(jnp.concatenate([high, low], axis=0))
                rights.append(jnp.where(cd[m : m + 1, :] == subc, 1.0, 0.0).astype(BF16))
            acc = acc + nt(
                jnp.concatenate(lefts, axis=1), jnp.concatenate(rights, axis=1)
            )
        hist[side] = hist[side] + acc
        return off + prefix[8]

    mine8 = pl.ds(pl.multiple_of(j * 8, 8), 8)
    shifts = [tok_f[o, mine8, :] for o in range(7)]

    def convolve(c):
        hot = window_onehot([sh[c : c + 1, :] for sh in shifts])
        for q, (d, s, k) in enumerate(CHAINS):
            x = silu_half(nn(hot, tw[q]))
            ref = (xad, xbc)[d]
            for i in range(4):
                ref[pl.ds(c * 8 * CH + s * 4 + i, CH, stride=8), :] = x[:, 128 * i : 128 * i + 128]

    if own <= 8:
        seen = jnp.zeros((8, CH), F32)
        for b in range(own - 1):
            seen = block(jnp.int32(b), seen)
            if b < nchunk:
                convolve(b)
        for c in range(own - 1, nchunk):
            convolve(c)
    else:
        lax.fori_loop(0, own - 1, block, jnp.zeros((8, CH), F32))
        for c in range(nchunk):
            convolve(c)

    for copy in arriving[len(blocks) + 6 :]:
        copy.wait()
    last8 = rows - 8
    xs = {}
    for d in range(2):
        edge = 0 if d == 0 else 7
        seq_at = pl.ds(0 if d == 0 else last8, 8)
        hot = window_onehot([tok_f[o, seq_at, :][edge : edge + 1, :] for o in range(7)])
        for s in range(2):
            if d == 0:
                xs[s] = pltpu.roll(silu_half(nn(hot[0:16, :], tw[s]))[0:8, :], 5, 0)
            else:
                xs[2 + s] = silu_half(nn(hot[CH - 16 :, :], tw[2 + s]))[8:16, :]
    diag = iota((H, E), 0) == (iota((H, E), 1) >> 6)
    sub16 = iota((16, E), 0)
    for q in range(4):
        d, s = q // 2, q % 2
        rim = jnp.concatenate([jnp.zeros((8, E), F32), xs[q]], axis=0)
        rim_h, rim_l = split(rim)
        for v in range(SYM):
            start = (q * SYM + v) * CH
            body = slice(start, start + CH - 16)
            tail = slice(start + CH - 16, start + CH)
            tail_h = jnp.where(sub16 >= 13, rim_h.astype(F32), xch[tail, :].astype(F32))
            tail_l = jnp.where(sub16 >= 13, rim_l.astype(F32), xcl[tail, :].astype(F32))
            table_h = jnp.concatenate([xch[body, :], tail_h.astype(BF16)], axis=0)
            table_l = jnp.concatenate([xcl[body, :], tail_l.astype(BF16)], axis=0)
            at = v * 16 + s * 8
            w = hist[d, at : at + 8, :] + hist[d, 80 + at : 88 + at, :]
            high, low = split(w)
            both = jnp.concatenate([high.astype(F32), low.astype(F32)], axis=0).astype(BF16)
            one = nn(both, table_h)
            two = nn(both, table_l)
            full = one[0:8, :] + one[8:16, :] + two[0:8, :]
            vec = jnp.sum(jnp.where(diag, full, 0.0), axis=0, keepdims=True)
            for i in range(4):
                at = (d * SYM + v) * 8 + s * 4 + i
                svec[at : at + 1, :] = vec[:, 128 * i : 128 * i + 128]
    starts = []
    for d in range(2):
        for w in range(SYM):
            value = jnp.zeros((8, CH), F32)
            for v in range(SYM):
                at = (d * SYM + v) * 64 + 8 + w * 8
                sat = (d * SYM + v) * 8
                value = value + tab[at : at + 8, :] * svec[sat : sat + 8, :]
            starts.append(value)

    skips = (cst[0:8, :], cst[8:16, :])

    def rows8(ref, k):
        return ref[k * 8 : k * 8 + 8, :]

    unroll = 128
    held = 8
    rings = ((ring0, ring1), (ring2, ring3))

    def group(g, carry):
        states = [list(carry[:SYM]), list(carry[SYM:])]
        firsts = (g * unroll, total - (g + 1) * unroll)
        spans = [pl.ds(pl.multiple_of(f * 8, unroll * 8), unroll * 8) for f in firsts]
        sources = (xad.at[spans[0], :], xbc.at[spans[1], :])
        targets = (yad.at[spans[0], :], ybc.at[spans[1], :])
        for begin in range(0, unroll, held):
            pair = rings[(begin // held) % 2]
            done = []
            for i in range(held):
                for d in range(2):
                    n = begin + i
                    local = n if d == 0 else unroll - 1 - n
                    u = tok_s[firsts[d] + local]
                    part = tab.at[pl.ds(pl.multiple_of((d * SYM + u) * 64, 64), 64), :]
                    x = rows8(sources[d], local)
                    a = rows8(part, 0)
                    states[d] = [a * states[d][w] + rows8(part, 1 + w) * x for w in range(SYM)]
                    for w in range(SYM):
                        pair[d][(i * SYM + w) * 8 : (i * SYM + w) * 8 + 8, :] = states[d][w]
                    done.append((d, i, local, x, u, part))
            for d, i, local, x, u, part in done:
                y = tile_at(pair[d], i * SYM * 8 + u * 8) + skips[d] * x
                targets[d][local * 8 : local * 8 + 8, :] = y * rows8(part, 6)
        return tuple(states[0] + states[1])

    lax.fori_loop(0, total // unroll, group, tuple(starts))

    flip = jnp.where(iota((D, D), 0) + iota((D, D), 1) == D - 1, 1.0, 0.0).astype(BF16)
    wout = w_out[...]
    wflip = nn(wout, flip).astype(BF16)
    mean = jnp.where(
        ((iota((4 * CH, 2 * CH), 0) & 255) >> 6) == (iota((4 * CH, 2 * CH), 1) >> 6), 1.0 / 64.0, 0.0
    ).astype(BF16)
    emb_rows = jnp.concatenate(
        [emb16[0:8, :], jnp.zeros((CH - 8, D), F32)], axis=0
    ).astype(BF16)
    gains = (cst[16:24, :], cst[24:32, :])
    sub = iota((8, CH), 0).astype(F32)
    mix[...] = jnp.zeros_like(mix)
    tiles = CH // SUB

    def project(c):
        base = (c & 1) * (CH * 8)
        row = tok_f[3, pl.ds(j * 8 + c, 1), :]
        hot = jnp.concatenate(
            [jnp.where(row == sub, 1.0, 0.0), jnp.zeros((CH - 8, CH), F32)], axis=0
        ).T.astype(BF16)
        parts = [mix[pl.ds(base + i, CH, stride=8), :].astype(BF16) for i in range(8)]
        one = nn(jnp.concatenate(parts[0:4], axis=1), wout).astype(BF16).astype(F32)
        two = nn(jnp.concatenate(parts[4:8], axis=1), wflip).astype(BF16).astype(F32)
        out[pl.ds(pl.multiple_of(c * CH, CH), CH), :] = (nn(hot, emb_rows) + one + two).astype(BF16)

    def tile(c, k):
        at = pl.ds(pl.multiple_of((c * CH + k * SUB) * 8, SUB * 8), SUB * 8)
        found = (yad[at, :], ybc[at, :])
        high, low = split(jnp.concatenate([g * g for g in found], axis=1))
        scale = lax.rsqrt(nn(jnp.concatenate([high, low], axis=1), mean) + EPSILON)
        normed = None
        for d in range(2):
            scaled = (found[d] * scale[:, CH * d : CH * d + CH]).reshape(SUB, 8, CH) * gains[d][None]
            normed = scaled if normed is None else normed + scaled
        at = (c & 1) * (CH * 8) + k * SUB * 8
        mix[pl.ds(pl.multiple_of(at, 8), SUB * 8), :] = normed.reshape(SUB * 8, CH)

    def chunk(c, _):
        project(jnp.maximum(c - 1, 0))
        for k in range(tiles):
            tile(c, k)
        return 0

    lax.fori_loop(0, nchunk, chunk, 0)
    project(nchunk - 1)


def per_device(
    token_ids,
    embed_table,
    input_weight_matrix,
    output_weight_matrix,
    conv_weight,
    dt_bias,
    decay_rate,
    skip_gain,
    norm_gain,
):
    length = token_ids.shape[0]
    nchunk = length // CH
    own = lax.axis_size("seq")
    tok2 = token_ids.reshape(nchunk, CH)
    rounds = own.bit_length() - 1
    rows = own * nchunk
    vm = pl.BlockSpec(memory_space=pltpu.VMEM)
    sm = pl.BlockSpec(memory_space=pltpu.SMEM)
    hbm = pl.BlockSpec(memory_space=pl.ANY)
    sds = jax.ShapeDtypeStruct
    weights = (
        embed_table, input_weight_matrix.T, conv_weight, dt_bias, decay_rate, skip_gain, norm_gain,
    )

    def sent(blocks, mask):
        return lax.ppermute(blocks, "seq", [(i, i ^ mask) for i in range(own)])

    gathered = tok2
    low = max(rounds - 3, 0)
    for bit in range(low):
        gathered = jnp.concatenate([gathered, sent(gathered, 1 << bit)], axis=0)
    blocks = [gathered] + [sent(gathered, m << low) for m in range(1, own >> low)]
    if len(blocks) > 5:
        tied = lax.optimization_barrier((dt_bias, *blocks[-2:]))
        weights = weights[:3] + (tied[0],) + weights[4:]
        blocks[-2:] = tied[1:]
    limit = pltpu.CompilerParams(vmem_limit_bytes=56 * 1024 * 1024)
    dma = pltpu.SemaphoreType.DMA
    window = sds((4 * SYM * CH, E), BF16)
    shapes = (
        sds((2 * SYM * 64, CH), F32),
        sds((32, CH), F32),
        sds((2 * SYM * 16, CH), F32),
        sds((4, CH, E), BF16),
        sds((16, D), F32),
        window,
        window,
    )
    tab, cst, lac, tw, emb16, xch, xcl = pl.pallas_call(
        table_kernel,
        out_shape=shapes,
        in_specs=[hbm] * 7,
        out_specs=[vm] * 5 + [hbm] * 2,
        scratch_shapes=[pltpu.VMEM(w.shape, w.dtype) for w in weights]
        + [
            pltpu.VMEM((2 * 64, CH), F32),
            pltpu.VMEM((2 * SYM * 64, CH), F32),
            pltpu.VMEM((64, CH), F32),
            pltpu.VMEM(window.shape, BF16),
            pltpu.VMEM(window.shape, BF16),
            dma((7,)),
            dma((2, 4)),
        ],
        compiler_params=limit,
        cost_estimate=pl.CostEstimate(
            flops=1_000_000_000, bytes_accessed=6_000_000, transcendentals=0
        ),
        name="symbol_tables",
    )(*weights)
    fetched = (tab, cst, lac, tw, emb16, output_weight_matrix, xch, xcl)
    mine = lax.axis_index("seq").reshape(1).astype(jnp.int32)
    steps = pltpu.VMEM((length * 8, CH), F32)
    ring = pltpu.VMEM((8 * SYM * 8, CH), F32)
    return pl.pallas_call(
        functools.partial(layer_kernel, len(blocks)),
        out_shape=sds((length, D), BF16),
        in_specs=[sm, sm] + [hbm] * (len(blocks) + 8),
        out_specs=vm,
        scratch_shapes=[pltpu.VMEM(w.shape, w.dtype) for w in fetched]
        + [
            pltpu.VMEM((rows, CH), jnp.int32),
            pltpu.VMEM((7, rows, CH), F32),
            pltpu.VMEM((2, rows, CH), F32),
            pltpu.VMEM((2, CH, 2 * CH), BF16),
            pltpu.VMEM((2, 160, CH), F32),
            pltpu.VMEM((2 * SYM * 8, CH), F32),
            steps,
            steps,
            steps,
            steps,
            pltpu.VMEM((2 * CH * 8, CH), F32),
            ring,
            ring,
            ring,
            ring,
            dma((8 + len(blocks),)),
        ],
        compiler_params=limit,
        cost_estimate=pl.CostEstimate(
            flops=9_000_000_000, bytes_accessed=4_000_000, transcendentals=0
        ),
        name="bidirectional_layer",
    )(mine, token_ids, *blocks, *fetched)


def solution(mesh):
    placed = (P(("batch", "seq")), P(), P(), P(), P(), P(), P(), P(), P())
    return jax.shard_map(
        per_device, mesh=mesh, in_specs=placed, out_specs=P(("batch", "seq"), None), check_vma=False
    )
```

```python
import functools

import jax
import jax.numpy as jnp
from jax import lax
from jax.experimental import pallas as pl
from jax.experimental.pallas import tpu as pltpu
from jax.sharding import PartitionSpec as P

D = 256
E = 512
NS = 16
H = 8
KW = 4
SYM = 5
LOG2E = 1.4426950408889634
EPSILON = 1e-05
CH = 128
SUB = 32

F32 = jnp.float32
BF16 = jnp.bfloat16

CHAINS = ((0, 0, 0), (0, 1, 1), (1, 0, 1), (1, 1, 0))


def iota(shape, dim):
    return lax.broadcasted_iota(jnp.int32, shape, dim)


def nn(a, b, **kw):
    return lax.dot_general(a, b, (((1,), (0,)), ((), ())), preferred_element_type=F32, **kw)


def nt(a, b, **kw):
    return lax.dot_general(a, b, (((1,), (1,)), ((), ())), preferred_element_type=F32, **kw)


def split(value):
    high = value.astype(BF16)
    low = (value - high.astype(F32)).astype(BF16)
    return high, low


def softplus(x):
    return jnp.maximum(x, 0.0) + jnp.log1p(jnp.exp(-jnp.abs(x)))


def silu_half(half):
    return half + half * jnp.tanh(half)


def tap_row(direction, j):
    return j if direction == 0 else 2 * (KW - 1) - j


def window_onehot(rows):
    sub = iota((8, CH), 0).astype(F32)
    blocks = [jnp.where(row == sub, 1.0, 0.0) for row in rows]
    blocks.append(jnp.zeros((8, CH), F32))
    stacked = jnp.concatenate(blocks + blocks, axis=0)
    return stacked.T.astype(BF16)


def shifted(tok, offset, rows):
    if offset == 0:
        return tok
    lane = iota((rows, CH), 1)
    row = iota((rows, CH), 0)
    moved = pltpu.roll(tok, (-offset) % CH, 1)
    if offset < 0:
        other = pltpu.roll(moved, 1, 0)
        crossing = lane < -offset
        outside = crossing & (row == 0)
    else:
        other = pltpu.roll(moved, rows - 1, 0)
        crossing = lane >= CH - offset
        outside = crossing & (row == rows - 1)
    return jnp.where(outside, 5.0, jnp.where(crossing, other, moved))


def pick(values, u):
    low = (u & 1) == 1
    first = jnp.where(low, values[1], values[0])
    second = jnp.where(low, values[3], values[2])
    return jnp.where(u > 3, values[4], jnp.where((u & 2) == 2, second, first))


def tile_at(ref, row):
    return ref[pl.ds(pl.multiple_of(row, 8), 8), :]


def begin(sources, targets, sems):
    copies = [
        pltpu.make_async_copy(a, b, sems.at[i]) for i, (a, b) in enumerate(zip(sources, targets))
    ]
    for copy in copies:
        copy.start()
    return copies


def symbol_tables(
    directions, full, emb, w_in, cw, bias, rate, skip, gain, emb16, atab, gtab, cst, tw
):
    highest = lax.Precision.HIGHEST
    emb16[...] = jnp.zeros_like(emb16)
    e32 = emb[...].astype(F32)
    emb16[0:SYM, :] = e32
    for v in range(4):
        emb16[8 + v : 9 + v, :] = e32[3 - v : 4 - v, :]
    emb16[12:13, :] = e32[4:5, :]
    embs = emb16[...].astype(BF16)
    x16 = nt(embs, w_in[E : 2 * E, :]).astype(BF16).astype(F32)
    rest = nt(embs, w_in[2 * E :, :]).astype(BF16)
    nrest = 2 * NS + H
    expand = jnp.where(
        iota((nrest, E), 0) == (iota((nrest, E), 1) >> 6) + 2 * NS, 1.0, 0.0
    ).astype(BF16)
    heads = jnp.where(iota((H, E), 0) == (iota((H, E), 1) >> 6), 1.0, 0.0)
    r_exp = nn(rest, expand)
    bias_e = nn(bias[...], heads, precision=highest)
    rate_e = nn(rate[...], heads, precision=highest)
    skip_e = nn(skip[...], heads, precision=highest)
    shift = jnp.where(
        iota((nrest, nrest), 0) + NS == iota((nrest, nrest), 1),
        jnp.where(iota((nrest, nrest), 0) < NS, 1.0, 0.0),
        0.0,
    ).astype(BF16)
    rest_b = nn(rest, shift).astype(BF16)
    cb = nt(rest_b, rest)
    if full is not None:
        zg, lac, xch, xcl = full
        z16 = nt(embs, w_in[0:E, :]).astype(BF16).astype(F32)
        sz = z16 * (0.5 + 0.5 * jnp.tanh(0.5 * z16))
        for s in range(2):
            for i in range(4):
                zg[pl.ds(s * 4 + i, 8, stride=8), :] = sz[8 * s : 8 * s + 8, 128 * i : 128 * i + 128]
        pick_r = jnp.where(
            iota((H, nrest), 0) + 2 * NS == iota((H, nrest), 1), 1.0, 0.0
        ).astype(BF16)
        r_t = nt(pick_r, rest)
        eye = jnp.where(iota((H, H), 0) == iota((H, H), 1), 1.0, 0.0)
        bias_t = nt(eye, bias[...], precision=highest)
        rate_t = nt(eye, rate[...], precision=highest)
    for q, (d, s, k) in enumerate(CHAINS):
        if d not in directions:
            continue
        dt = softplus(r_exp[8 * s : 8 * s + 8, :] + bias_e[k : k + 1, :])
        a = jnp.exp(-rate_e[k : k + 1, :] * dt)
        for i in range(4):
            lanes = slice(128 * i, 128 * i + 128)
            atab[pl.ds(d * 64 + s * 4 + i, 8, stride=8), :] = a[:, lanes]
            cst[d * 8 + s * 4 + i : d * 8 + s * 4 + i + 1, :] = skip_e[k : k + 1, lanes]
            cst[16 + d * 8 + s * 4 + i : 17 + d * 8 + s * 4 + i, :] = gain[k : k + 1, lanes]
        for u in range(SYM):
            g = cb[8 * s : 8 * s + 8, 8 * s + u : 8 * s + u + 1] * dt
            for i in range(4):
                gtab[pl.ds((d * SYM + u) * 64 + s * 4 + i, 8, stride=8), :] = g[
                    :, 128 * i : 128 * i + 128
                ]
        xs = x16[8 * s : 8 * s + 8, :]
        blocks = [jnp.zeros((8, E), F32)] * 8
        for j in range(KW):
            blocks[tap_row(d, j)] = (0.5 * cw[k, j : j + 1, :]) * xs
        high, low = split(jnp.concatenate(blocks, axis=0))
        tw[q, 0:64, :] = high
        tw[q, 64:128, :] = low
        if full is None:
            continue
        la = (
            -rate_t[:, k : k + 1] * softplus(r_t[:, 8 * s : 8 * s + 8] + bias_t[:, k : k + 1])
        ) * LOG2E
        for v in range(SYM):
            lac[(d * SYM + v) * 16 + s * 8 : (d * SYM + v) * 16 + s * 8 + 8, :] = jnp.broadcast_to(
                la[:, v : v + 1], (8, CH)
            )
        code = iota((CH, CH), 0).astype(F32)
        lane = iota((CH, CH), 1) & 63
        slot = lane >> 3
        sym = (lane & 7).astype(F32)
        d0 = jnp.floor((code + 0.5) * (1.0 / 25.0))
        d01 = jnp.floor((code + 0.5) * (1.0 / 5.0))
        digits = (d0, d01 - 5.0 * d0, code - 5.0 * d01)
        hot = jnp.zeros((CH, CH), F32)
        for j in range(KW - 1):
            hot = jnp.where(
                slot == tap_row(d, j), jnp.where(sym == digits[j], 1.0, 0.0), hot
            )
        partial = nn(hot.astype(BF16), tw[q])
        last = blocks[tap_row(d, KW - 1)]
        for v in range(SYM):
            high, low = split(silu_half(partial + last[v : v + 1, :]))
            xch[(q * SYM + v) * CH : (q * SYM + v + 1) * CH, :] = high
            xcl[(q * SYM + v) * CH : (q * SYM + v + 1) * CH, :] = low


def layer_kernel(
    count, mine, tok_s, emb_h, w_in_h, cw_h, bias_h, rate_h, skip_h, gain_h, w_out_h, *others
):
    finish_layer(
        others[:count], mine, tok_s, emb_h, w_in_h, cw_h, bias_h, rate_h, skip_h, gain_h, w_out_h,
        *others[count:]
    )


def finish_layer(
    blocks, mine, tok_s, emb_h, w_in_h, cw_h, bias_h, rate_h, skip_h, gain_h, w_out_h,
    out,
    emb, w_in, cw, bias, rate, skip, gain, w_out, emb16, atab, gtab, cst, tw, zg, lac, xch, xcl,
    tok_x, tok_f, code, tri, hist, svec, xad, xbc, yad, ybc, mix,
    tab, ring0, ring1, ring2, ring3, sems,
):
    rows = tok_x.shape[0]
    own = rows // 8
    total = tok_s.shape[0]
    nchunk = total // CH
    j = mine[0]
    size = rows // len(blocks)
    arriving = begin(
        (*blocks, emb_h, w_in_h, cw_h, bias_h, rate_h, skip_h, gain_h, w_out_h),
        (*[tok_x.at[size * m : size * m + size, :] for m in range(len(blocks))],
         emb, w_in, cw, bias, rate, skip, gain, w_out), sems)
    for copy in arriving[: len(blocks)]:
        copy.wait()
    for b in range(own):
        slot = (j ^ b) * 8
        tok_f[3, 8 * b : 8 * b + 8, :] = tok_x[pl.ds(pl.multiple_of(slot, 8), 8), :].astype(F32)
    tok = tok_f[3]
    for o in (-3, -2, -1, 1, 2, 3):
        tok_f[3 + o] = shifted(tok, o, rows)
    lane = iota((rows, CH), 1)
    row = iota((rows, CH), 0)
    lane_f = lane.astype(F32)
    before = 25.0 * tok_f[0] + 5.0 * tok_f[1] + tok_f[2]
    after = 25.0 * tok_f[6] + 5.0 * tok_f[5] + tok_f[4]
    code[0] = jnp.where((row == 0) & (lane < 3), 125.0 + lane_f, before)
    code[1] = jnp.where((row == rows - 1) & (lane >= CH - 3), lane_f, after)
    si = iota((CH, CH), 0)
    ri = iota((CH, CH), 1)
    ones = jnp.ones((CH, CH), F32)
    tri[0] = jnp.concatenate([jnp.where(si > ri, 1.0, 0.0), ones], axis=1).astype(BF16)
    tri[1] = jnp.concatenate([jnp.where(si < ri, 1.0, 0.0), ones], axis=1).astype(BF16)
    hist[...] = jnp.zeros_like(hist)
    sub8 = iota((8, CH), 0).astype(F32)
    subc = iota((CH, CH), 0).astype(F32)

    for copy in arriving[len(blocks) :]:
        copy.wait()
    symbol_tables(
        (0, 1), (zg, lac, xch, xcl),
        emb, w_in, cw, bias, rate, skip, gain, emb16, atab, gtab, cst, tw,
    )

    def block(b, off):
        side = jnp.where(b >= j, 1, 0)
        index = jnp.where(b >= j, b + 1, j - 1 - b)
        off = off * jnp.where(b == j, 0.0, 1.0)
        use_prefix = side.astype(F32)
        at = pl.ds(pl.multiple_of(index * 8, 8), 8)
        tk = tok_f[3, at, :]
        cd = code[side, at, :]
        hots = [jnp.where(tk[m : m + 1, :] == sub8, 1.0, 0.0) for m in range(8)]
        counts = nn(jnp.concatenate(hots, axis=0).astype(BF16), tri[side])
        totals = [counts[8 * m : 8 * m + 8, CH:] for m in range(8)]
        prefix = [jnp.zeros((8, CH), F32)]
        for m in range(8):
            prefix.append(prefix[-1] + totals[m])
        las = [lac[pl.ds(pl.multiple_of((side * SYM + v) * 16, 16), 16), :] for v in range(SYM)]
        acc = jnp.zeros((160, CH), F32)
        for pair in range(4):
            lefts, rights = [], []
            for m in (2 * pair, 2 * pair + 1):
                suffix = prefix[8] - prefix[m + 1]
                inside = suffix + use_prefix * (prefix[m] - suffix)
                count = counts[8 * m : 8 * m + 8, :CH] + off + inside
                exponent = las[0] * count[0:1, :]
                for v in range(1, SYM):
                    exponent = exponent + las[v] * count[v : v + 1, :]
                weight = jnp.exp2(exponent)
                masked = jnp.concatenate(
                    [jnp.where(tk[m : m + 1, :] == float(v), weight, 0.0) for v in range(SYM)],
                    axis=0,
                )
                high, low = split(masked)
                lefts.append(jnp.concatenate([high, low], axis=0))
                rights.append(jnp.where(cd[m : m + 1, :] == subc, 1.0, 0.0).astype(BF16))
            acc = acc + nt(
                jnp.concatenate(lefts, axis=1), jnp.concatenate(rights, axis=1)
            )
        hist[side] = hist[side] + acc
        return off + prefix[8]

    mine8 = pl.ds(pl.multiple_of(j * 8, 8), 8)
    shifts = [tok_f[o, mine8, :] for o in range(7)]

    def convolve(c):
        hot = window_onehot([sh[c : c + 1, :] for sh in shifts])
        for q, (d, s, k) in enumerate(CHAINS):
            x = silu_half(nn(hot, tw[q]))
            ref = (xad, xbc)[d]
            for i in range(4):
                ref[pl.ds(c * 8 * CH + s * 4 + i, CH, stride=8), :] = x[:, 128 * i : 128 * i + 128]

    if own <= 8:
        seen = jnp.zeros((8, CH), F32)
        for b in range(own - 1):
            seen = block(jnp.int32(b), seen)
            if b < nchunk:
                convolve(b)
        for c in range(own - 1, nchunk):
            convolve(c)
    else:
        lax.fori_loop(0, own - 1, block, jnp.zeros((8, CH), F32))
        for c in range(nchunk):
            convolve(c)

    last8 = rows - 8
    xs = {}
    for d in range(2):
        edge = 0 if d == 0 else 7
        seq_at = pl.ds(0 if d == 0 else last8, 8)
        hot = window_onehot([tok_f[o, seq_at, :][edge : edge + 1, :] for o in range(7)])
        for s in range(2):
            if d == 0:
                xs[s] = pltpu.roll(silu_half(nn(hot[0:16, :], tw[s]))[0:8, :], 5, 0)
            else:
                xs[2 + s] = silu_half(nn(hot[CH - 16 :, :], tw[2 + s]))[8:16, :]
    diag = iota((H, E), 0) == (iota((H, E), 1) >> 6)
    sub16 = iota((16, E), 0)
    for q in range(4):
        d, s = q // 2, q % 2
        rim = jnp.concatenate([jnp.zeros((8, E), F32), xs[q]], axis=0)
        rim_h, rim_l = split(rim)
        for v in range(SYM):
            start = (q * SYM + v) * CH
            body = slice(start, start + CH - 16)
            tail = slice(start + CH - 16, start + CH)
            tail_h = jnp.where(sub16 >= 13, rim_h.astype(F32), xch[tail, :].astype(F32))
            tail_l = jnp.where(sub16 >= 13, rim_l.astype(F32), xcl[tail, :].astype(F32))
            table_h = jnp.concatenate([xch[body, :], tail_h.astype(BF16)], axis=0)
            table_l = jnp.concatenate([xcl[body, :], tail_l.astype(BF16)], axis=0)
            at = v * 16 + s * 8
            w = hist[d, at : at + 8, :] + hist[d, 80 + at : 88 + at, :]
            high, low = split(w)
            both = jnp.concatenate([high.astype(F32), low.astype(F32)], axis=0).astype(BF16)
            one = nn(both, table_h)
            two = nn(both, table_l)
            full = one[0:8, :] + one[8:16, :] + two[0:8, :]
            vec = jnp.sum(jnp.where(diag, full, 0.0), axis=0, keepdims=True)
            for i in range(4):
                at = (d * SYM + v) * 8 + s * 4 + i
                svec[at : at + 1, :] = vec[:, 128 * i : 128 * i + 128]
    starts = []
    for d in range(2):
        for w in range(SYM):
            value = jnp.zeros((8, CH), F32)
            for v in range(SYM):
                at = (d * SYM + w) * 64 + v * 8
                sat = (d * SYM + v) * 8
                value = value + gtab[at : at + 8, :] * svec[sat : sat + 8, :]
            starts.append(value)

    skips = (cst[0:8, :], cst[8:16, :])

    for d in range(2):
        for u in range(SYM):
            at = (d * SYM + u) * 64
            tab[at : at + 8, :] = atab[d * 64 + u * 8 : d * 64 + u * 8 + 8, :]
            for w in range(SYM):
                row = (d * SYM + w) * 64 + u * 8
                tab[at + 8 + w * 8 : at + 16 + w * 8, :] = gtab[row : row + 8, :]
            tab[at + 48 : at + 56, :] = zg[u * 8 : u * 8 + 8, :]

    def rows8(ref, k):
        return ref[k * 8 : k * 8 + 8, :]

    unroll = 128
    held = 8
    rings = ((ring0, ring1), (ring2, ring3))

    def group(g, carry):
        states = [list(carry[:SYM]), list(carry[SYM:])]
        firsts = (g * unroll, total - (g + 1) * unroll)
        spans = [pl.ds(pl.multiple_of(f * 8, unroll * 8), unroll * 8) for f in firsts]
        sources = (xad.at[spans[0], :], xbc.at[spans[1], :])
        targets = (yad.at[spans[0], :], ybc.at[spans[1], :])
        for begin in range(0, unroll, held):
            pair = rings[(begin // held) % 2]
            done = []
            for i in range(held):
                for d in range(2):
                    n = begin + i
                    local = n if d == 0 else unroll - 1 - n
                    u = tok_s[firsts[d] + local]
                    part = tab.at[pl.ds(pl.multiple_of((d * SYM + u) * 64, 64), 64), :]
                    x = rows8(sources[d], local)
                    a = rows8(part, 0)
                    states[d] = [a * states[d][w] + rows8(part, 1 + w) * x for w in range(SYM)]
                    for w in range(SYM):
                        pair[d][(i * SYM + w) * 8 : (i * SYM + w) * 8 + 8, :] = states[d][w]
                    done.append((d, i, local, x, u, part))
            for d, i, local, x, u, part in done:
                y = tile_at(pair[d], i * SYM * 8 + u * 8) + skips[d] * x
                targets[d][local * 8 : local * 8 + 8, :] = y * rows8(part, 6)
        return tuple(states[0] + states[1])

    lax.fori_loop(0, total // unroll, group, tuple(starts))

    flip = jnp.where(iota((D, D), 0) + iota((D, D), 1) == D - 1, 1.0, 0.0).astype(BF16)
    wout = w_out[...]
    wflip = nn(wout, flip).astype(BF16)
    mean = jnp.where(
        ((iota((4 * CH, 2 * CH), 0) & 255) >> 6) == (iota((4 * CH, 2 * CH), 1) >> 6), 1.0 / 64.0, 0.0
    ).astype(BF16)
    emb_rows = jnp.concatenate(
        [emb16[0:8, :], jnp.zeros((CH - 8, D), F32)], axis=0
    ).astype(BF16)
    gains = (cst[16:24, :], cst[24:32, :])
    sub = iota((8, CH), 0).astype(F32)
    mix[...] = jnp.zeros_like(mix)
    tiles = CH // SUB

    def project(c):
        base = (c & 1) * (CH * 8)
        row = tok_f[3, pl.ds(j * 8 + c, 1), :]
        hot = jnp.concatenate(
            [jnp.where(row == sub, 1.0, 0.0), jnp.zeros((CH - 8, CH), F32)], axis=0
        ).T.astype(BF16)
        held_rows = mix.at[pl.ds(pl.multiple_of(base, CH * 8), CH * 8), :]
        parts = [held_rows[pl.ds(i, CH, stride=8), :].astype(BF16) for i in range(8)]
        one = nn(jnp.concatenate(parts[0:4], axis=1), wout).astype(BF16).astype(F32)
        two = nn(jnp.concatenate(parts[4:8], axis=1), wflip).astype(BF16).astype(F32)
        out[pl.ds(pl.multiple_of(c * CH, CH), CH), :] = (nn(hot, emb_rows) + one + two).astype(BF16)

    def tile(c, k):
        at = pl.ds(pl.multiple_of((c * CH + k * SUB) * 8, SUB * 8), SUB * 8)
        found = (yad[at, :], ybc[at, :])
        high, low = split(jnp.concatenate([g * g for g in found], axis=1))
        scale = lax.rsqrt(nn(jnp.concatenate([high, low], axis=1), mean) + EPSILON)
        normed = None
        for d in range(2):
            scaled = (found[d] * scale[:, CH * d : CH * d + CH]).reshape(SUB, 8, CH) * gains[d][None]
            normed = scaled if normed is None else normed + scaled
        at = (c & 1) * (CH * 8) + k * SUB * 8
        mix[pl.ds(pl.multiple_of(at, 8), SUB * 8), :] = normed.reshape(SUB * 8, CH)

    def chunk(c, _):
        project(jnp.maximum(c - 1, 0))
        for k in range(tiles):
            tile(c, k)
        return 0

    lax.fori_loop(0, nchunk, chunk, 0)
    project(nchunk - 1)


def per_device(
    token_ids,
    embed_table,
    input_weight_matrix,
    output_weight_matrix,
    conv_weight,
    dt_bias,
    decay_rate,
    skip_gain,
    norm_gain,
):
    length = token_ids.shape[0]
    nchunk = length // CH
    own = lax.axis_size("seq")
    tok2 = token_ids.reshape(nchunk, CH)
    rounds = own.bit_length() - 1
    rows = own * nchunk
    vm = pl.BlockSpec(memory_space=pltpu.VMEM)
    sm = pl.BlockSpec(memory_space=pltpu.SMEM)
    hbm = pl.BlockSpec(memory_space=pl.ANY)
    sds = jax.ShapeDtypeStruct
    weights = (
        embed_table, input_weight_matrix.T, conv_weight, dt_bias, decay_rate, skip_gain, norm_gain,
        output_weight_matrix,
    )

    def sent(blocks, mask):
        return lax.ppermute(blocks, "seq", [(i, i ^ mask) for i in range(own)])

    gathered = tok2
    low = max(rounds - 3, 0)
    for bit in range(low):
        gathered = jnp.concatenate([gathered, sent(gathered, 1 << bit)], axis=0)
    blocks = [gathered] + [None] * ((own >> low) - 1)
    for m in sorted(range(1, own >> low), key=lambda m: (bin(m).count("1"), m)):
        top = 1 << (m.bit_length() - 1)
        blocks[m] = sent(blocks[m ^ top], top << low)
    mine = lax.axis_index("seq").reshape(1).astype(jnp.int32)
    table = pltpu.VMEM((4 * SYM * CH, E), BF16)
    steps = pltpu.VMEM((length * 8, CH), F32)
    ring = pltpu.VMEM((8 * SYM * 8, CH), F32)
    return pl.pallas_call(
        functools.partial(layer_kernel, len(blocks)),
        out_shape=sds((length, D), BF16),
        in_specs=[sm, sm] + [hbm] * 8 + [hbm] * len(blocks),
        out_specs=vm,
        scratch_shapes=[pltpu.VMEM(w.shape, w.dtype) for w in weights]
        + [
            pltpu.VMEM((16, D), F32),
            pltpu.VMEM((2 * 64, CH), F32),
            pltpu.VMEM((2 * SYM * 64, CH), F32),
            pltpu.VMEM((32, CH), F32),
            pltpu.VMEM((4, CH, E), BF16),
            pltpu.VMEM((64, CH), F32),
            pltpu.VMEM((2 * SYM * 16, CH), F32),
            table,
            table,
            pltpu.VMEM((rows, CH), jnp.int32),
            pltpu.VMEM((7, rows, CH), F32),
            pltpu.VMEM((2, rows, CH), F32),
            pltpu.VMEM((2, CH, 2 * CH), BF16),
            pltpu.VMEM((2, 160, CH), F32),
            pltpu.VMEM((2 * SYM * 8, CH), F32),
            steps,
            steps,
            steps,
            steps,
            pltpu.VMEM((2 * CH * 8, CH), F32),
            pltpu.VMEM((2 * SYM * 64, CH), F32),
            ring,
            ring,
            ring,
            ring,
            pltpu.SemaphoreType.DMA((8 + len(blocks),)),
        ],
        compiler_params=pltpu.CompilerParams(vmem_limit_bytes=56 * 1024 * 1024),
        cost_estimate=pl.CostEstimate(
            flops=9_000_000_000, bytes_accessed=4_000_000, transcendentals=0
        ),
        name="bidirectional_layer",
    )(mine, token_ids, *weights, *blocks)


def solution(mesh):
    placed = (P(("batch", "seq")), P(), P(), P(), P(), P(), P(), P(), P())
    return jax.shard_map(
        per_device, mesh=mesh, in_specs=placed, out_specs=P(("batch", "seq"), None), check_vma=False
    )
```

```python
import functools

import jax
import jax.numpy as jnp
from jax import lax
from jax.experimental import pallas as pl
from jax.experimental.pallas import tpu as pltpu
from jax.sharding import PartitionSpec as P

D = 256
E = 512
NS = 16
H = 8
KW = 4
SYM = 5
LOG2E = 1.4426950408889634
EPSILON = 1e-05
CH = 128
SUB = 32

F32 = jnp.float32
BF16 = jnp.bfloat16

CHAINS = ((0, 0, 0), (0, 1, 1), (1, 0, 1), (1, 1, 0))


def iota(shape, dim):
    return lax.broadcasted_iota(jnp.int32, shape, dim)


def nn(a, b, **kw):
    return lax.dot_general(a, b, (((1,), (0,)), ((), ())), preferred_element_type=F32, **kw)


def nt(a, b, **kw):
    return lax.dot_general(a, b, (((1,), (1,)), ((), ())), preferred_element_type=F32, **kw)


def split(value):
    high = value.astype(BF16)
    low = (value - high.astype(F32)).astype(BF16)
    return high, low


def softplus(x):
    return jnp.maximum(x, 0.0) + jnp.log1p(jnp.exp(-jnp.abs(x)))


def silu_half(half):
    return half + half * jnp.tanh(half)


def tap_row(direction, j):
    return j if direction == 0 else 2 * (KW - 1) - j


def window_onehot(rows):
    sub = iota((8, CH), 0).astype(F32)
    blocks = [jnp.where(row == sub, 1.0, 0.0) for row in rows]
    blocks.append(jnp.zeros((8, CH), F32))
    stacked = jnp.concatenate(blocks + blocks, axis=0)
    return stacked.T.astype(BF16)


def shifted(tok, offset, rows):
    if offset == 0:
        return tok
    lane = iota((rows, CH), 1)
    row = iota((rows, CH), 0)
    moved = pltpu.roll(tok, (-offset) % CH, 1)
    if offset < 0:
        other = pltpu.roll(moved, 1, 0)
        crossing = lane < -offset
        outside = crossing & (row == 0)
    else:
        other = pltpu.roll(moved, rows - 1, 0)
        crossing = lane >= CH - offset
        outside = crossing & (row == rows - 1)
    return jnp.where(outside, 5.0, jnp.where(crossing, other, moved))


def pick(values, u):
    low = (u & 1) == 1
    first = jnp.where(low, values[1], values[0])
    second = jnp.where(low, values[3], values[2])
    return jnp.where(u > 3, values[4], jnp.where((u & 2) == 2, second, first))


def tile_at(ref, row):
    return ref[pl.ds(pl.multiple_of(row, 8), 8), :]


def begin(sources, targets, sems):
    copies = [
        pltpu.make_async_copy(a, b, sems.at[i]) for i, (a, b) in enumerate(zip(sources, targets))
    ]
    for copy in copies:
        copy.start()
    return copies


def symbol_tables(
    directions, full, emb, w_in, cw, bias, rate, skip, gain, emb16, atab, gtab, cst, tw
):
    highest = lax.Precision.HIGHEST
    emb16[...] = jnp.zeros_like(emb16)
    e32 = emb[...].astype(F32)
    emb16[0:SYM, :] = e32
    for v in range(4):
        emb16[8 + v : 9 + v, :] = e32[3 - v : 4 - v, :]
    emb16[12:13, :] = e32[4:5, :]
    embs = emb16[...].astype(BF16)
    x16 = nt(embs, w_in[E : 2 * E, :]).astype(BF16).astype(F32)
    rest = nt(embs, w_in[2 * E :, :]).astype(BF16)
    nrest = 2 * NS + H
    expand = jnp.where(
        iota((nrest, E), 0) == (iota((nrest, E), 1) >> 6) + 2 * NS, 1.0, 0.0
    ).astype(BF16)
    heads = jnp.where(iota((H, E), 0) == (iota((H, E), 1) >> 6), 1.0, 0.0)
    r_exp = nn(rest, expand)
    bias_e = nn(bias[...], heads, precision=highest)
    rate_e = nn(rate[...], heads, precision=highest)
    skip_e = nn(skip[...], heads, precision=highest)
    shift = jnp.where(
        iota((nrest, nrest), 0) + NS == iota((nrest, nrest), 1),
        jnp.where(iota((nrest, nrest), 0) < NS, 1.0, 0.0),
        0.0,
    ).astype(BF16)
    rest_b = nn(rest, shift).astype(BF16)
    cb = nt(rest_b, rest)
    if full is not None:
        zg, lac, xch, xcl = full
        z16 = nt(embs, w_in[0:E, :]).astype(BF16).astype(F32)
        sz = z16 * (0.5 + 0.5 * jnp.tanh(0.5 * z16))
        for s in range(2):
            for i in range(4):
                zg[pl.ds(s * 4 + i, 8, stride=8), :] = sz[8 * s : 8 * s + 8, 128 * i : 128 * i + 128]
        pick_r = jnp.where(
            iota((H, nrest), 0) + 2 * NS == iota((H, nrest), 1), 1.0, 0.0
        ).astype(BF16)
        r_t = nt(pick_r, rest)
        eye = jnp.where(iota((H, H), 0) == iota((H, H), 1), 1.0, 0.0)
        bias_t = nt(eye, bias[...], precision=highest)
        rate_t = nt(eye, rate[...], precision=highest)
    for q, (d, s, k) in enumerate(CHAINS):
        if d not in directions:
            continue
        dt = softplus(r_exp[8 * s : 8 * s + 8, :] + bias_e[k : k + 1, :])
        a = jnp.exp(-rate_e[k : k + 1, :] * dt)
        for i in range(4):
            lanes = slice(128 * i, 128 * i + 128)
            atab[pl.ds(d * 64 + s * 4 + i, 8, stride=8), :] = a[:, lanes]
            cst[d * 8 + s * 4 + i : d * 8 + s * 4 + i + 1, :] = skip_e[k : k + 1, lanes]
            cst[16 + d * 8 + s * 4 + i : 17 + d * 8 + s * 4 + i, :] = gain[k : k + 1, lanes]
        for u in range(SYM):
            g = cb[8 * s : 8 * s + 8, 8 * s + u : 8 * s + u + 1] * dt
            for i in range(4):
                gtab[pl.ds((d * SYM + u) * 64 + s * 4 + i, 8, stride=8), :] = g[
                    :, 128 * i : 128 * i + 128
                ]
        xs = x16[8 * s : 8 * s + 8, :]
        blocks = [jnp.zeros((8, E), F32)] * 8
        for j in range(KW):
            blocks[tap_row(d, j)] = (0.5 * cw[k, j : j + 1, :]) * xs
        high, low = split(jnp.concatenate(blocks, axis=0))
        tw[q, 0:64, :] = high
        tw[q, 64:128, :] = low
        if full is None:
            continue
        la = (
            -rate_t[:, k : k + 1] * softplus(r_t[:, 8 * s : 8 * s + 8] + bias_t[:, k : k + 1])
        ) * LOG2E
        for v in range(SYM):
            lac[(d * SYM + v) * 16 + s * 8 : (d * SYM + v) * 16 + s * 8 + 8, :] = jnp.broadcast_to(
                la[:, v : v + 1], (8, CH)
            )
        code = iota((CH, CH), 0).astype(F32)
        lane = iota((CH, CH), 1) & 63
        slot = lane >> 3
        sym = (lane & 7).astype(F32)
        d0 = jnp.floor((code + 0.5) * (1.0 / 25.0))
        d01 = jnp.floor((code + 0.5) * (1.0 / 5.0))
        digits = (d0, d01 - 5.0 * d0, code - 5.0 * d01)
        hot = jnp.zeros((CH, CH), F32)
        for j in range(KW - 1):
            hot = jnp.where(
                slot == tap_row(d, j), jnp.where(sym == digits[j], 1.0, 0.0), hot
            )
        partial = nn(hot.astype(BF16), tw[q])
        last = blocks[tap_row(d, KW - 1)]
        for v in range(SYM):
            high, low = split(silu_half(partial + last[v : v + 1, :]))
            xch[(q * SYM + v) * CH : (q * SYM + v + 1) * CH, :] = high
            xcl[(q * SYM + v) * CH : (q * SYM + v + 1) * CH, :] = low


def layer_kernel(
    count, mine, tok_s, emb_h, w_in_h, cw_h, bias_h, rate_h, skip_h, gain_h, w_out_h, *others
):
    finish_layer(
        others[:count], mine, tok_s, emb_h, w_in_h, cw_h, bias_h, rate_h, skip_h, gain_h, w_out_h,
        *others[count:]
    )


def finish_layer(
    blocks, mine, tok_s, emb_h, w_in_h, cw_h, bias_h, rate_h, skip_h, gain_h, w_out_h,
    out,
    emb, w_in, cw, bias, rate, skip, gain, w_out, emb16, atab, gtab, cst, tw, zg, lac, xch, xcl,
    tok_x, tok_f, code, tri, hist, svec, xad, xbc, yad, ybc, mix,
    tab, ring0, ring1, ring2, ring3, sems,
):
    rows = tok_x.shape[0]
    own = rows // 8
    total = tok_s.shape[0]
    nchunk = total // CH
    j = mine[0]
    size = rows // len(blocks)
    arriving = begin(
        (*blocks, emb_h, w_in_h, cw_h, bias_h, rate_h, skip_h, gain_h, w_out_h),
        (*[tok_x.at[size * m : size * m + size, :] for m in range(len(blocks))],
         emb, w_in, cw, bias, rate, skip, gain, w_out), sems)
    for copy in arriving[: len(blocks)]:
        copy.wait()
    for b in range(own):
        slot = (j ^ b) * 8
        tok_f[3, 8 * b : 8 * b + 8, :] = tok_x[pl.ds(pl.multiple_of(slot, 8), 8), :].astype(F32)
    tok = tok_f[3]
    for o in (-3, -2, -1, 1, 2, 3):
        tok_f[3 + o] = shifted(tok, o, rows)
    lane = iota((rows, CH), 1)
    row = iota((rows, CH), 0)
    lane_f = lane.astype(F32)
    before = 25.0 * tok_f[0] + 5.0 * tok_f[1] + tok_f[2]
    after = 25.0 * tok_f[6] + 5.0 * tok_f[5] + tok_f[4]
    code[0] = jnp.where((row == 0) & (lane < 3), 125.0 + lane_f, before)
    code[1] = jnp.where((row == rows - 1) & (lane >= CH - 3), lane_f, after)
    si = iota((CH, CH), 0)
    ri = iota((CH, CH), 1)
    ones = jnp.ones((CH, CH), F32)
    tri[0] = jnp.concatenate([jnp.where(si > ri, 1.0, 0.0), ones], axis=1).astype(BF16)
    tri[1] = jnp.concatenate([jnp.where(si < ri, 1.0, 0.0), ones], axis=1).astype(BF16)
    hist[...] = jnp.zeros_like(hist)
    sub8 = iota((8, CH), 0).astype(F32)
    subc = iota((CH, CH), 0).astype(F32)

    for copy in arriving[len(blocks) :]:
        copy.wait()
    symbol_tables(
        (0, 1), (zg, lac, xch, xcl),
        emb, w_in, cw, bias, rate, skip, gain, emb16, atab, gtab, cst, tw,
    )

    def block(b, off):
        side = jnp.where(b >= j, 1, 0)
        index = jnp.where(b >= j, b + 1, j - 1 - b)
        off = off * jnp.where(b == j, 0.0, 1.0)
        use_prefix = side.astype(F32)
        at = pl.ds(pl.multiple_of(index * 8, 8), 8)
        tk = tok_f[3, at, :]
        cd = code[side, at, :]
        hots = [jnp.where(tk[m : m + 1, :] == sub8, 1.0, 0.0) for m in range(8)]
        counts = nn(jnp.concatenate(hots, axis=0).astype(BF16), tri[side])
        totals = [counts[8 * m : 8 * m + 8, CH:] for m in range(8)]
        prefix = [jnp.zeros((8, CH), F32)]
        for m in range(8):
            prefix.append(prefix[-1] + totals[m])
        las = [lac[pl.ds(pl.multiple_of((side * SYM + v) * 16, 16), 16), :] for v in range(SYM)]
        acc = jnp.zeros((160, CH), F32)
        for pair in range(4):
            lefts, rights = [], []
            for m in (2 * pair, 2 * pair + 1):
                suffix = prefix[8] - prefix[m + 1]
                inside = suffix + use_prefix * (prefix[m] - suffix)
                count = counts[8 * m : 8 * m + 8, :CH] + off + inside
                exponent = las[0] * count[0:1, :]
                for v in range(1, SYM):
                    exponent = exponent + las[v] * count[v : v + 1, :]
                weight = jnp.exp2(exponent)
                masked = jnp.concatenate(
                    [jnp.where(tk[m : m + 1, :] == float(v), weight, 0.0) for v in range(SYM)],
                    axis=0,
                )
                high, low = split(masked)
                lefts.append(jnp.concatenate([high, low], axis=0))
                rights.append(jnp.where(cd[m : m + 1, :] == subc, 1.0, 0.0).astype(BF16))
            acc = acc + nt(
                jnp.concatenate(lefts, axis=1), jnp.concatenate(rights, axis=1)
            )
        hist[side] = hist[side] + acc
        return off + prefix[8]

    mine8 = pl.ds(pl.multiple_of(j * 8, 8), 8)
    shifts = [tok_f[o, mine8, :] for o in range(7)]

    def convolve(c):
        hot = window_onehot([sh[c : c + 1, :] for sh in shifts])
        for q, (d, s, k) in enumerate(CHAINS):
            x = silu_half(nn(hot, tw[q]))
            ref = (xad, xbc)[d]
            for i in range(4):
                ref[pl.ds(c * 8 * CH + s * 4 + i, CH, stride=8), :] = x[:, 128 * i : 128 * i + 128]

    if own <= 8:
        seen = jnp.zeros((8, CH), F32)
        for b in range(own - 1):
            seen = block(jnp.int32(b), seen)
            if b < nchunk:
                convolve(b)
        for c in range(own - 1, nchunk):
            convolve(c)
    else:
        lax.fori_loop(0, own - 1, block, jnp.zeros((8, CH), F32))
        for c in range(nchunk):
            convolve(c)

    last8 = rows - 8
    xs = {}
    for d in range(2):
        edge = 0 if d == 0 else 7
        seq_at = pl.ds(0 if d == 0 else last8, 8)
        hot = window_onehot([tok_f[o, seq_at, :][edge : edge + 1, :] for o in range(7)])
        for s in range(2):
            if d == 0:
                xs[s] = pltpu.roll(silu_half(nn(hot[0:16, :], tw[s]))[0:8, :], 5, 0)
            else:
                xs[2 + s] = silu_half(nn(hot[CH - 16 :, :], tw[2 + s]))[8:16, :]
    diag = iota((H, E), 0) == (iota((H, E), 1) >> 6)
    sub16 = iota((16, E), 0)
    for q in range(4):
        d, s = q // 2, q % 2
        rim = jnp.concatenate([jnp.zeros((8, E), F32), xs[q]], axis=0)
        rim_h, rim_l = split(rim)
        for v in range(SYM):
            start = (q * SYM + v) * CH
            body = slice(start, start + CH - 16)
            tail = slice(start + CH - 16, start + CH)
            tail_h = jnp.where(sub16 >= 13, rim_h.astype(F32), xch[tail, :].astype(F32))
            tail_l = jnp.where(sub16 >= 13, rim_l.astype(F32), xcl[tail, :].astype(F32))
            table_h = jnp.concatenate([xch[body, :], tail_h.astype(BF16)], axis=0)
            table_l = jnp.concatenate([xcl[body, :], tail_l.astype(BF16)], axis=0)
            at = v * 16 + s * 8
            w = hist[d, at : at + 8, :] + hist[d, 80 + at : 88 + at, :]
            high, low = split(w)
            both = jnp.concatenate([high.astype(F32), low.astype(F32)], axis=0).astype(BF16)
            one = nn(both, table_h)
            two = nn(both, table_l)
            full = one[0:8, :] + one[8:16, :] + two[0:8, :]
            vec = jnp.sum(jnp.where(diag, full, 0.0), axis=0, keepdims=True)
            for i in range(4):
                at = (d * SYM + v) * 8 + s * 4 + i
                svec[at : at + 1, :] = vec[:, 128 * i : 128 * i + 128]
    starts = []
    for d in range(2):
        for w in range(SYM):
            value = jnp.zeros((8, CH), F32)
            for v in range(SYM):
                at = (d * SYM + w) * 64 + v * 8
                sat = (d * SYM + v) * 8
                value = value + gtab[at : at + 8, :] * svec[sat : sat + 8, :]
            starts.append(value)

    skips = (cst[0:8, :], cst[8:16, :])

    for d in range(2):
        for u in range(SYM):
            at = (d * SYM + u) * 64
            tab[at : at + 8, :] = atab[d * 64 + u * 8 : d * 64 + u * 8 + 8, :]
            for w in range(SYM):
                row = (d * SYM + w) * 64 + u * 8
                tab[at + 8 + w * 8 : at + 16 + w * 8, :] = gtab[row : row + 8, :]
            tab[at + 48 : at + 56, :] = zg[u * 8 : u * 8 + 8, :]

    def rows8(ref, k):
        return ref[k * 8 : k * 8 + 8, :]

    unroll = CH
    held = 8
    rings = ((ring0, ring1), (ring2, ring3))

    def group(g, carry):
        states = [list(carry[:SYM]), list(carry[SYM:])]
        firsts = (g * unroll, total - (g + 1) * unroll)
        spans = [pl.ds(pl.multiple_of(f * 8, unroll * 8), unroll * 8) for f in firsts]
        sources = (xad.at[spans[0], :], xbc.at[spans[1], :])
        targets = (yad.at[spans[0], :], ybc.at[spans[1], :])
        for begin in range(0, unroll, held):
            pair = rings[(begin // held) % 2]
            done = []
            for i in range(held):
                for d in range(2):
                    n = begin + i
                    local = n if d == 0 else unroll - 1 - n
                    u = tok_s[firsts[d] + local]
                    part = tab.at[pl.ds(pl.multiple_of((d * SYM + u) * 64, 64), 64), :]
                    x = rows8(sources[d], local)
                    a = rows8(part, 0)
                    states[d] = [a * states[d][w] + rows8(part, 1 + w) * x for w in range(SYM)]
                    for w in range(SYM):
                        pair[d][(i * SYM + w) * 8 : (i * SYM + w) * 8 + 8, :] = states[d][w]
                    done.append((d, i, local, x, u, part))
            for d, i, local, x, u, part in done:
                y = tile_at(pair[d], i * SYM * 8 + u * 8) + skips[d] * x
                targets[d][local * 8 : local * 8 + 8, :] = y * rows8(part, 6)
        return tuple(states[0] + states[1])


    flip = jnp.where(iota((D, D), 0) + iota((D, D), 1) == D - 1, 1.0, 0.0).astype(BF16)
    wout = w_out[...]
    wflip = nn(wout, flip).astype(BF16)
    mean = jnp.where(
        ((iota((4 * CH, 2 * CH), 0) & 255) >> 6) == (iota((4 * CH, 2 * CH), 1) >> 6), 1.0 / 64.0, 0.0
    ).astype(BF16)
    emb_rows = jnp.concatenate(
        [emb16[0:8, :], jnp.zeros((CH - 8, D), F32)], axis=0
    ).astype(BF16)
    gains = (cst[16:24, :], cst[24:32, :])
    sub = iota((8, CH), 0).astype(F32)
    tiles = CH // SUB

    def project(c):
        base = (c & 1) * (CH * 8)
        row = tok_f[3, pl.ds(j * 8 + c, 1), :]
        hot = jnp.concatenate(
            [jnp.where(row == sub, 1.0, 0.0), jnp.zeros((CH - 8, CH), F32)], axis=0
        ).T.astype(BF16)
        parts = [mix[pl.ds(base + i, CH, stride=8), :].astype(BF16) for i in range(8)]
        one = nn(jnp.concatenate(parts[0:4], axis=1), wout).astype(BF16).astype(F32)
        two = nn(jnp.concatenate(parts[4:8], axis=1), wflip).astype(BF16).astype(F32)
        out[pl.ds(pl.multiple_of(c * CH, CH), CH), :] = (nn(hot, emb_rows) + one + two).astype(BF16)

    def tile(c, k):
        at = pl.ds(pl.multiple_of((c * CH + k * SUB) * 8, SUB * 8), SUB * 8)
        found = (yad[at, :], ybc[at, :])
        high, low = split(jnp.concatenate([g * g for g in found], axis=1))
        scale = lax.rsqrt(nn(jnp.concatenate([high, low], axis=1), mean) + EPSILON)
        normed = None
        for d in range(2):
            scaled = (found[d] * scale[:, CH * d : CH * d + CH]).reshape(SUB, 8, CH) * gains[d][None]
            normed = scaled if normed is None else normed + scaled
        at = (c & 1) * (CH * 8) + k * SUB * 8
        mix[pl.ds(pl.multiple_of(at, 8), SUB * 8), :] = normed.reshape(SUB * 8, CH)

    def chunks(pair):
        for c in pair:
            for k in range(tiles):
                tile(c, k)

    def late_group(g, carry):
        pair = (nchunk - g, g - 1)
        chunks(pair)
        carry = group(g, carry)
        for c in pair:
            project(c)
        return carry

    half = nchunk // 2 + 1
    carry = lax.fori_loop(0, half, group, tuple(starts))
    lax.fori_loop(half, nchunk, late_group, carry)
    pair = (0, nchunk - 1)
    chunks(pair)
    for c in pair:
        project(c)


def per_device(
    token_ids,
    embed_table,
    input_weight_matrix,
    output_weight_matrix,
    conv_weight,
    dt_bias,
    decay_rate,
    skip_gain,
    norm_gain,
):
    length = token_ids.shape[0]
    nchunk = length // CH
    own = lax.axis_size("seq")
    tok2 = token_ids.reshape(nchunk, CH)
    rounds = own.bit_length() - 1
    rows = own * nchunk
    vm = pl.BlockSpec(memory_space=pltpu.VMEM)
    sm = pl.BlockSpec(memory_space=pltpu.SMEM)
    hbm = pl.BlockSpec(memory_space=pl.ANY)
    sds = jax.ShapeDtypeStruct
    weights = (
        embed_table, input_weight_matrix.T, conv_weight, dt_bias, decay_rate, skip_gain, norm_gain,
        output_weight_matrix,
    )

    def sent(blocks, mask):
        return lax.ppermute(blocks, "seq", [(i, i ^ mask) for i in range(own)])

    gathered = tok2
    low = max(rounds - 3, 0)
    for bit in range(low):
        gathered = jnp.concatenate([gathered, sent(gathered, 1 << bit)], axis=0)
    blocks = [gathered] + [sent(gathered, m << low) for m in range(1, own >> low)]
    mine = lax.axis_index("seq").reshape(1).astype(jnp.int32)
    table = pltpu.VMEM((4 * SYM * CH, E), BF16)
    steps = pltpu.VMEM((length * 8, CH), F32)
    ring = pltpu.VMEM((8 * SYM * 8, CH), F32)
    return pl.pallas_call(
        functools.partial(layer_kernel, len(blocks)),
        out_shape=sds((length, D), BF16),
        in_specs=[sm, sm] + [hbm] * 8 + [hbm] * len(blocks),
        out_specs=vm,
        scratch_shapes=[pltpu.VMEM(w.shape, w.dtype) for w in weights]
        + [
            pltpu.VMEM((16, D), F32),
            pltpu.VMEM((2 * 64, CH), F32),
            pltpu.VMEM((2 * SYM * 64, CH), F32),
            pltpu.VMEM((32, CH), F32),
            pltpu.VMEM((4, CH, E), BF16),
            pltpu.VMEM((64, CH), F32),
            pltpu.VMEM((2 * SYM * 16, CH), F32),
            table,
            table,
            pltpu.VMEM((rows, CH), jnp.int32),
            pltpu.VMEM((7, rows, CH), F32),
            pltpu.VMEM((2, rows, CH), F32),
            pltpu.VMEM((2, CH, 2 * CH), BF16),
            pltpu.VMEM((2, 160, CH), F32),
            pltpu.VMEM((2 * SYM * 8, CH), F32),
            steps,
            steps,
            steps,
            steps,
            pltpu.VMEM((2 * CH * 8, CH), F32),
            pltpu.VMEM((2 * SYM * 64, CH), F32),
            ring,
            ring,
            ring,
            ring,
            pltpu.SemaphoreType.DMA((8 + len(blocks),)),
        ],
        compiler_params=pltpu.CompilerParams(vmem_limit_bytes=56 * 1024 * 1024),
        cost_estimate=pl.CostEstimate(
            flops=9_000_000_000, bytes_accessed=4_000_000, transcendentals=0
        ),
        name="bidirectional_layer",
    )(mine, token_ids, *weights, *blocks)


def solution(mesh):
    placed = (P(("batch", "seq")), P(), P(), P(), P(), P(), P(), P(), P())
    return jax.shard_map(
        per_device, mesh=mesh, in_specs=placed, out_specs=P(("batch", "seq"), None), check_vma=False
    )
```

```python
import functools

import jax
import jax.numpy as jnp
from jax import lax
from jax.experimental import pallas as pl
from jax.experimental.pallas import tpu as pltpu
from jax.sharding import PartitionSpec as P

D = 256
E = 512
NS = 16
H = 8
KW = 4
SYM = 5
LOG2E = 1.4426950408889634
EPSILON = 1e-05
CH = 128
SUB = 32

F32 = jnp.float32
BF16 = jnp.bfloat16

CHAINS = ((0, 0, 0), (0, 1, 1), (1, 0, 1), (1, 1, 0))


def iota(shape, dim):
    return lax.broadcasted_iota(jnp.int32, shape, dim)


def nn(a, b, **kw):
    return lax.dot_general(a, b, (((1,), (0,)), ((), ())), preferred_element_type=F32, **kw)


def nt(a, b, **kw):
    return lax.dot_general(a, b, (((1,), (1,)), ((), ())), preferred_element_type=F32, **kw)


def split(value):
    high = value.astype(BF16)
    low = (value - high.astype(F32)).astype(BF16)
    return high, low


def softplus(x):
    return jnp.maximum(x, 0.0) + jnp.log1p(jnp.exp(-jnp.abs(x)))


def silu_half(half):
    return half + half * jnp.tanh(half)


def tap_row(direction, j):
    return j if direction == 0 else 2 * (KW - 1) - j


def window_onehot(rows):
    sub = iota((8, CH), 0).astype(F32)
    blocks = [jnp.where(row == sub, 1.0, 0.0) for row in rows]
    blocks.append(jnp.zeros((8, CH), F32))
    stacked = jnp.concatenate(blocks + blocks, axis=0)
    return stacked.T.astype(BF16)


def shifted(tok, offset, rows):
    if offset == 0:
        return tok
    lane = iota((rows, CH), 1)
    row = iota((rows, CH), 0)
    moved = pltpu.roll(tok, (-offset) % CH, 1)
    if offset < 0:
        other = pltpu.roll(moved, 1, 0)
        crossing = lane < -offset
        outside = crossing & (row == 0)
    else:
        other = pltpu.roll(moved, rows - 1, 0)
        crossing = lane >= CH - offset
        outside = crossing & (row == rows - 1)
    return jnp.where(outside, 5.0, jnp.where(crossing, other, moved))


def pick(values, u):
    low = (u & 1) == 1
    first = jnp.where(low, values[1], values[0])
    second = jnp.where(low, values[3], values[2])
    return jnp.where(u > 3, values[4], jnp.where((u & 2) == 2, second, first))


def tile_at(ref, row):
    return ref[pl.ds(pl.multiple_of(row, 8), 8), :]


def begin(sources, targets, sems):
    copies = [
        pltpu.make_async_copy(a, b, sems.at[i]) for i, (a, b) in enumerate(zip(sources, targets))
    ]
    for copy in copies:
        copy.start()
    return copies


def symbol_tables(
    directions, full, emb, w_in, cw, bias, rate, skip, gain, emb16, atab, gtab, cst, tw
):
    highest = lax.Precision.HIGHEST
    emb16[...] = jnp.zeros_like(emb16)
    e32 = emb[...].astype(F32)
    emb16[0:SYM, :] = e32
    for v in range(4):
        emb16[8 + v : 9 + v, :] = e32[3 - v : 4 - v, :]
    emb16[12:13, :] = e32[4:5, :]
    embs = emb16[...].astype(BF16)
    x16 = nt(embs, w_in[E : 2 * E, :]).astype(BF16).astype(F32)
    rest = nt(embs, w_in[2 * E :, :]).astype(BF16)
    nrest = 2 * NS + H
    expand = jnp.where(
        iota((nrest, E), 0) == (iota((nrest, E), 1) >> 6) + 2 * NS, 1.0, 0.0
    ).astype(BF16)
    heads = jnp.where(iota((H, E), 0) == (iota((H, E), 1) >> 6), 1.0, 0.0)
    r_exp = nn(rest, expand)
    bias_e = nn(bias[...], heads, precision=highest)
    rate_e = nn(rate[...], heads, precision=highest)
    skip_e = nn(skip[...], heads, precision=highest)
    shift = jnp.where(
        iota((nrest, nrest), 0) + NS == iota((nrest, nrest), 1),
        jnp.where(iota((nrest, nrest), 0) < NS, 1.0, 0.0),
        0.0,
    ).astype(BF16)
    rest_b = nn(rest, shift).astype(BF16)
    cb = nt(rest_b, rest)
    if full is not None:
        zg, lac, xch, xcl = full
        z16 = nt(embs, w_in[0:E, :]).astype(BF16).astype(F32)
        sz = z16 * (0.5 + 0.5 * jnp.tanh(0.5 * z16))
        for s in range(2):
            for i in range(4):
                zg[pl.ds(s * 4 + i, 8, stride=8), :] = sz[8 * s : 8 * s + 8, 128 * i : 128 * i + 128]
        pick_r = jnp.where(
            iota((H, nrest), 0) + 2 * NS == iota((H, nrest), 1), 1.0, 0.0
        ).astype(BF16)
        r_t = nt(pick_r, rest)
        eye = jnp.where(iota((H, H), 0) == iota((H, H), 1), 1.0, 0.0)
        bias_t = nt(eye, bias[...], precision=highest)
        rate_t = nt(eye, rate[...], precision=highest)
    for q, (d, s, k) in enumerate(CHAINS):
        if d not in directions:
            continue
        dt = softplus(r_exp[8 * s : 8 * s + 8, :] + bias_e[k : k + 1, :])
        a = jnp.exp(-rate_e[k : k + 1, :] * dt)
        for i in range(4):
            lanes = slice(128 * i, 128 * i + 128)
            atab[pl.ds(d * 64 + s * 4 + i, 8, stride=8), :] = a[:, lanes]
            cst[d * 8 + s * 4 + i : d * 8 + s * 4 + i + 1, :] = skip_e[k : k + 1, lanes]
            cst[16 + d * 8 + s * 4 + i : 17 + d * 8 + s * 4 + i, :] = gain[k : k + 1, lanes]
        for u in range(SYM):
            g = cb[8 * s : 8 * s + 8, 8 * s + u : 8 * s + u + 1] * dt
            for i in range(4):
                gtab[pl.ds((d * SYM + u) * 64 + s * 4 + i, 8, stride=8), :] = g[
                    :, 128 * i : 128 * i + 128
                ]
        xs = x16[8 * s : 8 * s + 8, :]
        blocks = [jnp.zeros((8, E), F32)] * 8
        for j in range(KW):
            blocks[tap_row(d, j)] = (0.5 * cw[k, j : j + 1, :]) * xs
        high, low = split(jnp.concatenate(blocks, axis=0))
        tw[q, 0:64, :] = high
        tw[q, 64:128, :] = low
        if full is None:
            continue
        la = (
            -rate_t[:, k : k + 1] * softplus(r_t[:, 8 * s : 8 * s + 8] + bias_t[:, k : k + 1])
        ) * LOG2E
        for v in range(SYM):
            lac[(d * SYM + v) * 16 + s * 8 : (d * SYM + v) * 16 + s * 8 + 8, :] = jnp.broadcast_to(
                la[:, v : v + 1], (8, CH)
            )
        code = iota((CH, CH), 0).astype(F32)
        lane = iota((CH, CH), 1) & 63
        slot = lane >> 3
        sym = (lane & 7).astype(F32)
        d0 = jnp.floor((code + 0.5) * (1.0 / 25.0))
        d01 = jnp.floor((code + 0.5) * (1.0 / 5.0))
        digits = (d0, d01 - 5.0 * d0, code - 5.0 * d01)
        hot = jnp.zeros((CH, CH), F32)
        for j in range(KW - 1):
            hot = jnp.where(
                slot == tap_row(d, j), jnp.where(sym == digits[j], 1.0, 0.0), hot
            )
        partial = nn(hot.astype(BF16), tw[q])
        last = blocks[tap_row(d, KW - 1)]
        for v in range(SYM):
            high, low = split(silu_half(partial + last[v : v + 1, :]))
            xch[(q * SYM + v) * CH : (q * SYM + v + 1) * CH, :] = high
            xcl[(q * SYM + v) * CH : (q * SYM + v + 1) * CH, :] = low


def layer_kernel(
    count, mine, tok_s, emb_h, w_in_h, cw_h, bias_h, rate_h, skip_h, gain_h, w_out_h, *others
):
    finish_layer(
        others[:count], mine, tok_s, emb_h, w_in_h, cw_h, bias_h, rate_h, skip_h, gain_h, w_out_h,
        *others[count:]
    )


def finish_layer(
    blocks, mine, tok_s, emb_h, w_in_h, cw_h, bias_h, rate_h, skip_h, gain_h, w_out_h,
    out,
    emb, w_in, cw, bias, rate, skip, gain, w_out, emb16, atab, gtab, cst, tw, zg, lac, xch, xcl,
    tok_x, tok_f, code, tri, hist, svec, xad, xbc, yad, ybc, mix,
    tab, ring0, ring1, ring2, ring3, sems,
):
    rows = tok_x.shape[0]
    own = rows // 8
    total = tok_s.shape[0]
    nchunk = total // CH
    j = mine[0]
    size = rows // len(blocks)
    arriving = begin(
        (*blocks, emb_h, w_in_h, cw_h, bias_h, rate_h, skip_h, gain_h, w_out_h),
        (*[tok_x.at[size * m : size * m + size, :] for m in range(len(blocks))],
         emb, w_in, cw, bias, rate, skip, gain, w_out), sems)
    for copy in arriving[: len(blocks)]:
        copy.wait()
    for b in range(own):
        slot = (j ^ b) * 8
        tok_f[3, 8 * b : 8 * b + 8, :] = tok_x[pl.ds(pl.multiple_of(slot, 8), 8), :].astype(F32)
    tok = tok_f[3]
    for o in (-3, -2, -1, 1, 2, 3):
        tok_f[3 + o] = shifted(tok, o, rows)
    lane = iota((rows, CH), 1)
    row = iota((rows, CH), 0)
    lane_f = lane.astype(F32)
    before = 25.0 * tok_f[0] + 5.0 * tok_f[1] + tok_f[2]
    after = 25.0 * tok_f[6] + 5.0 * tok_f[5] + tok_f[4]
    code[0] = jnp.where((row == 0) & (lane < 3), 125.0 + lane_f, before)
    code[1] = jnp.where((row == rows - 1) & (lane >= CH - 3), lane_f, after)
    si = iota((CH, CH), 0)
    ri = iota((CH, CH), 1)
    ones = jnp.ones((CH, CH), F32)
    tri[0] = jnp.concatenate([jnp.where(si > ri, 1.0, 0.0), ones], axis=1).astype(BF16)
    tri[1] = jnp.concatenate([jnp.where(si < ri, 1.0, 0.0), ones], axis=1).astype(BF16)
    hist[...] = jnp.zeros_like(hist)
    sub8 = iota((8, CH), 0).astype(F32)
    subc = iota((CH, CH), 0).astype(F32)

    for copy in arriving[len(blocks) :]:
        copy.wait()
    symbol_tables(
        (0, 1), (zg, lac, xch, xcl),
        emb, w_in, cw, bias, rate, skip, gain, emb16, atab, gtab, cst, tw,
    )

    def block(b, off):
        side = jnp.where(b >= j, 1, 0)
        index = jnp.where(b >= j, b + 1, j - 1 - b)
        off = off * jnp.where(b == j, 0.0, 1.0)
        use_prefix = side.astype(F32)
        at = pl.ds(pl.multiple_of(index * 8, 8), 8)
        tk = tok_f[3, at, :]
        cd = code[side, at, :]
        hots = [jnp.where(tk[m : m + 1, :] == sub8, 1.0, 0.0) for m in range(8)]
        counts = nn(jnp.concatenate(hots, axis=0).astype(BF16), tri[side])
        totals = [counts[8 * m : 8 * m + 8, CH:] for m in range(8)]
        prefix = [jnp.zeros((8, CH), F32)]
        for m in range(8):
            prefix.append(prefix[-1] + totals[m])
        las = [lac[pl.ds(pl.multiple_of((side * SYM + v) * 16, 16), 16), :] for v in range(SYM)]
        acc = jnp.zeros((160, CH), F32)
        for pair in range(4):
            lefts, rights = [], []
            for m in (2 * pair, 2 * pair + 1):
                suffix = prefix[8] - prefix[m + 1]
                inside = suffix + use_prefix * (prefix[m] - suffix)
                count = counts[8 * m : 8 * m + 8, :CH] + off + inside
                exponent = las[0] * count[0:1, :]
                for v in range(1, SYM):
                    exponent = exponent + las[v] * count[v : v + 1, :]
                weight = jnp.exp2(exponent)
                masked = jnp.concatenate(
                    [jnp.where(tk[m : m + 1, :] == float(v), weight, 0.0) for v in range(SYM)],
                    axis=0,
                )
                high, low = split(masked)
                lefts.append(jnp.concatenate([high, low], axis=0))
                rights.append(jnp.where(cd[m : m + 1, :] == subc, 1.0, 0.0).astype(BF16))
            acc = acc + nt(
                jnp.concatenate(lefts, axis=1), jnp.concatenate(rights, axis=1)
            )
        hist[side] = hist[side] + acc
        return off + prefix[8]

    mine8 = pl.ds(pl.multiple_of(j * 8, 8), 8)
    shifts = [tok_f[o, mine8, :] for o in range(7)]

    def convolve(c):
        hot = window_onehot([sh[c : c + 1, :] for sh in shifts])
        for q, (d, s, k) in enumerate(CHAINS):
            x = silu_half(nn(hot, tw[q]))
            ref = (xad, xbc)[d]
            for i in range(4):
                ref[pl.ds(c * 8 * CH + s * 4 + i, CH, stride=8), :] = x[:, 128 * i : 128 * i + 128]

    if own <= 8:
        seen = jnp.zeros((8, CH), F32)
        for b in range(own - 1):
            seen = block(jnp.int32(b), seen)
            if b < nchunk:
                convolve(b)
        for c in range(own - 1, nchunk):
            convolve(c)
    else:
        lax.fori_loop(0, own - 1, block, jnp.zeros((8, CH), F32))
        for c in range(nchunk):
            convolve(c)

    last8 = rows - 8
    xs = {}
    for d in range(2):
        edge = 0 if d == 0 else 7
        seq_at = pl.ds(0 if d == 0 else last8, 8)
        hot = window_onehot([tok_f[o, seq_at, :][edge : edge + 1, :] for o in range(7)])
        for s in range(2):
            if d == 0:
                xs[s] = pltpu.roll(silu_half(nn(hot[0:16, :], tw[s]))[0:8, :], 5, 0)
            else:
                xs[2 + s] = silu_half(nn(hot[CH - 16 :, :], tw[2 + s]))[8:16, :]
    diag = iota((H, E), 0) == (iota((H, E), 1) >> 6)
    sub16 = iota((16, E), 0)
    for q in range(4):
        d, s = q // 2, q % 2
        rim = jnp.concatenate([jnp.zeros((8, E), F32), xs[q]], axis=0)
        rim_h, rim_l = split(rim)
        for v in range(SYM):
            start = (q * SYM + v) * CH
            body = slice(start, start + CH - 16)
            tail = slice(start + CH - 16, start + CH)
            tail_h = jnp.where(sub16 >= 13, rim_h.astype(F32), xch[tail, :].astype(F32))
            tail_l = jnp.where(sub16 >= 13, rim_l.astype(F32), xcl[tail, :].astype(F32))
            table_h = jnp.concatenate([xch[body, :], tail_h.astype(BF16)], axis=0)
            table_l = jnp.concatenate([xcl[body, :], tail_l.astype(BF16)], axis=0)
            at = v * 16 + s * 8
            w = hist[d, at : at + 8, :] + hist[d, 80 + at : 88 + at, :]
            high, low = split(w)
            both = jnp.concatenate([high.astype(F32), low.astype(F32)], axis=0).astype(BF16)
            one = nn(both, table_h)
            two = nn(both, table_l)
            full = one[0:8, :] + one[8:16, :] + two[0:8, :]
            vec = jnp.sum(jnp.where(diag, full, 0.0), axis=0, keepdims=True)
            for i in range(4):
                at = (d * SYM + v) * 8 + s * 4 + i
                svec[at : at + 1, :] = vec[:, 128 * i : 128 * i + 128]
    starts = []
    for d in range(2):
        for w in range(SYM):
            value = jnp.zeros((8, CH), F32)
            for v in range(SYM):
                at = (d * SYM + w) * 64 + v * 8
                sat = (d * SYM + v) * 8
                value = value + gtab[at : at + 8, :] * svec[sat : sat + 8, :]
            starts.append(value)

    skips = (cst[0:8, :], cst[8:16, :])

    for d in range(2):
        for u in range(SYM):
            at = (d * SYM + u) * 64
            tab[at : at + 8, :] = atab[d * 64 + u * 8 : d * 64 + u * 8 + 8, :]
            for w in range(SYM):
                row = (d * SYM + w) * 64 + u * 8
                tab[at + 8 + w * 8 : at + 16 + w * 8, :] = gtab[row : row + 8, :]
            tab[at + 48 : at + 56, :] = zg[u * 8 : u * 8 + 8, :]

    def rows8(ref, k):
        return ref[k * 8 : k * 8 + 8, :]

    unroll = CH
    held = 8
    rings = ((ring0, ring1), (ring2, ring3))

    def group(g, carry):
        states = [list(carry[:SYM]), list(carry[SYM:])]
        firsts = (g * unroll, total - (g + 1) * unroll)
        spans = [pl.ds(pl.multiple_of(f * 8, unroll * 8), unroll * 8) for f in firsts]
        sources = (xad.at[spans[0], :], xbc.at[spans[1], :])
        targets = (yad.at[spans[0], :], ybc.at[spans[1], :])
        for begin in range(0, unroll, held):
            pair = rings[(begin // held) % 2]
            done = []
            for i in range(held):
                for d in range(2):
                    n = begin + i
                    local = n if d == 0 else unroll - 1 - n
                    u = tok_s[firsts[d] + local]
                    part = tab.at[pl.ds(pl.multiple_of((d * SYM + u) * 64, 64), 64), :]
                    x = rows8(sources[d], local)
                    a = rows8(part, 0)
                    states[d] = [a * states[d][w] + rows8(part, 1 + w) * x for w in range(SYM)]
                    odd = (u & 1) == 1
                    kept = (
                        jnp.where(odd, states[d][1], states[d][0]),
                        jnp.where(odd, states[d][3], states[d][2]),
                        states[d][4],
                    )
                    for w in range(3):
                        pair[d][(i * 3 + w) * 8 : (i * 3 + w) * 8 + 8, :] = kept[w]
                    done.append((d, i, local, x, u, part))
            for d, i, local, x, u, part in done:
                y = tile_at(pair[d], i * 24 + (u >> 1) * 8) + skips[d] * x
                targets[d][local * 8 : local * 8 + 8, :] = y * rows8(part, 6)
        return tuple(states[0] + states[1])


    flip = jnp.where(iota((D, D), 0) + iota((D, D), 1) == D - 1, 1.0, 0.0).astype(BF16)
    wout = w_out[...]
    wflip = nn(wout, flip).astype(BF16)
    mean = jnp.where(
        ((iota((4 * CH, 2 * CH), 0) & 255) >> 6) == (iota((4 * CH, 2 * CH), 1) >> 6), 1.0 / 64.0, 0.0
    ).astype(BF16)
    emb_rows = jnp.concatenate(
        [emb16[0:8, :], jnp.zeros((CH - 8, D), F32)], axis=0
    ).astype(BF16)
    gains = (cst[16:24, :], cst[24:32, :])
    sub = iota((8, CH), 0).astype(F32)
    tiles = CH // SUB

    def project(c):
        base = (c & 1) * (CH * 8)
        row = tok_f[3, pl.ds(j * 8 + c, 1), :]
        hot = jnp.concatenate(
            [jnp.where(row == sub, 1.0, 0.0), jnp.zeros((CH - 8, CH), F32)], axis=0
        ).T.astype(BF16)
        parts = [mix[pl.ds(base + i, CH, stride=8), :].astype(BF16) for i in range(8)]
        one = nn(jnp.concatenate(parts[0:4], axis=1), wout).astype(BF16).astype(F32)
        two = nn(jnp.concatenate(parts[4:8], axis=1), wflip).astype(BF16).astype(F32)
        out[pl.ds(pl.multiple_of(c * CH, CH), CH), :] = (nn(hot, emb_rows) + one + two).astype(BF16)

    def tile(c, k):
        at = pl.ds(pl.multiple_of((c * CH + k * SUB) * 8, SUB * 8), SUB * 8)
        found = (yad[at, :], ybc[at, :])
        high, low = split(jnp.concatenate([g * g for g in found], axis=1))
        scale = lax.rsqrt(nn(jnp.concatenate([high, low], axis=1), mean) + EPSILON)
        normed = None
        for d in range(2):
            scaled = (found[d] * scale[:, CH * d : CH * d + CH]).reshape(SUB, 8, CH) * gains[d][None]
            normed = scaled if normed is None else normed + scaled
        at = (c & 1) * (CH * 8) + k * SUB * 8
        mix[pl.ds(pl.multiple_of(at, 8), SUB * 8), :] = normed.reshape(SUB * 8, CH)

    def chunks(pair):
        for c in pair:
            for k in range(tiles):
                tile(c, k)

    def late_group(g, carry):
        pair = (nchunk - g, g - 1)
        chunks(pair)
        carry = group(g, carry)
        for c in pair:
            project(c)
        return carry

    half = nchunk // 2 + 1
    carry = lax.fori_loop(0, half, group, tuple(starts))
    lax.fori_loop(half, nchunk, late_group, carry)
    pair = (0, nchunk - 1)
    chunks(pair)
    for c in pair:
        project(c)


def per_device(
    token_ids,
    embed_table,
    input_weight_matrix,
    output_weight_matrix,
    conv_weight,
    dt_bias,
    decay_rate,
    skip_gain,
    norm_gain,
):
    length = token_ids.shape[0]
    nchunk = length // CH
    own = lax.axis_size("seq")
    tok2 = token_ids.reshape(nchunk, CH)
    rounds = own.bit_length() - 1
    rows = own * nchunk
    vm = pl.BlockSpec(memory_space=pltpu.VMEM)
    sm = pl.BlockSpec(memory_space=pltpu.SMEM)
    hbm = pl.BlockSpec(memory_space=pl.ANY)
    sds = jax.ShapeDtypeStruct
    weights = (
        embed_table, input_weight_matrix.T, conv_weight, dt_bias, decay_rate, skip_gain, norm_gain,
        output_weight_matrix,
    )

    def sent(blocks, mask):
        return lax.ppermute(blocks, "seq", [(i, i ^ mask) for i in range(own)])

    gathered = tok2
    low = max(rounds - 3, 0)
    for bit in range(low):
        gathered = jnp.concatenate([gathered, sent(gathered, 1 << bit)], axis=0)
    blocks = [gathered] + [sent(gathered, m << low) for m in range(1, own >> low)]
    mine = lax.axis_index("seq").reshape(1).astype(jnp.int32)
    table = pltpu.VMEM((4 * SYM * CH, E), BF16)
    steps = pltpu.VMEM((length * 8, CH), F32)
    ring = pltpu.VMEM((8 * SYM * 8, CH), F32)
    return pl.pallas_call(
        functools.partial(layer_kernel, len(blocks)),
        out_shape=sds((length, D), BF16),
        in_specs=[sm, sm] + [hbm] * 8 + [hbm] * len(blocks),
        out_specs=vm,
        scratch_shapes=[pltpu.VMEM(w.shape, w.dtype) for w in weights]
        + [
            pltpu.VMEM((16, D), F32),
            pltpu.VMEM((2 * 64, CH), F32),
            pltpu.VMEM((2 * SYM * 64, CH), F32),
            pltpu.VMEM((32, CH), F32),
            pltpu.VMEM((4, CH, E), BF16),
            pltpu.VMEM((64, CH), F32),
            pltpu.VMEM((2 * SYM * 16, CH), F32),
            table,
            table,
            pltpu.VMEM((rows, CH), jnp.int32),
            pltpu.VMEM((7, rows, CH), F32),
            pltpu.VMEM((2, rows, CH), F32),
            pltpu.VMEM((2, CH, 2 * CH), BF16),
            pltpu.VMEM((2, 160, CH), F32),
            pltpu.VMEM((2 * SYM * 8, CH), F32),
            steps,
            steps,
            steps,
            steps,
            pltpu.VMEM((2 * CH * 8, CH), F32),
            pltpu.VMEM((2 * SYM * 64, CH), F32),
            ring,
            ring,
            ring,
            ring,
            pltpu.SemaphoreType.DMA((8 + len(blocks),)),
        ],
        compiler_params=pltpu.CompilerParams(vmem_limit_bytes=56 * 1024 * 1024),
        cost_estimate=pl.CostEstimate(
            flops=9_000_000_000, bytes_accessed=4_000_000, transcendentals=0
        ),
        name="bidirectional_layer",
    )(mine, token_ids, *weights, *blocks)


def solution(mesh):
    placed = (P(("batch", "seq")), P(), P(), P(), P(), P(), P(), P(), P())
    return jax.shard_map(
        per_device, mesh=mesh, in_specs=placed, out_specs=P(("batch", "seq"), None), check_vma=False
    )
```
